128 devices in a mesh: inner: 2 (over core), outer: 32 (over x, y_lo, z), dp: 2 (over y_hi).
Axes of the slice: x: 4, y: 4 (y_hi: 2, y_lo: 2; y = y_hi * 2 + y_lo), z: 4, core: 2. Of those that a mesh axis runs over, the one named last changes fastest.
Arguments:
- queries: bfloat16 [32768, 3072], P(('dp', 'inner', 'outer')), parts along dimension 0, may hold values from -170 to 170
- keys: bfloat16 [32768, 1024], P(('dp', 'inner', 'outer')), parts along dimension 0, may hold values from -6 to 6
- values: bfloat16 [32768, 1024], P(('dp', 'inner', 'outer')), parts along dimension 0, may hold values from -3 to 3
- grad_out: bfloat16 [32768, 3072], P(('dp', 'inner', 'outer')), parts along dimension 0, may hold values from -6 to 6
- weights: float32 [32768], P(('dp', 'inner', 'outer')), parts along dimension 0, may hold values from 0.25 to 4
- doc_ids: int32 [32768], P(('dp', 'inner', 'outer')), parts along dimension 0, may hold values from 0 to 72, as said below
Outputs:
- grad_queries: bfloat16 [32768, 3072], P(('dp', 'inner', 'outer')), parts along dimension 0
- key_gradient: bfloat16 [32768, 1024], P(('dp', 'inner', 'outer')), parts along dimension 0
- value_gradient: bfloat16 [32768, 1024], P(('dp', 'inner', 'outer')), parts along dimension 0
The draws below stay inside these ranges and needn't reach their ends.
There are 2 independent parts, one for each index of `dp`. The reference program is written for one: setup_inputs(seed, part) draws one part's arguments, and reference() takes and returns one part's arrays. A program takes and returns all parts, laid end to end along the dimension named above; each array names one. Nothing has to cross between parts.
Inputs may be any that keep to these rules, and one draw needn't show every extreme that they name: `doc_ids`: document numbers start at 0, never fall along the sequence and rise by at most one from a position to the next; every document covers 1 to 1024 consecutive positions, and at least one covers exactly 1024.
All inputs are finite; a program needn't handle non-finite values.
Results may differ from the reference program's by a relative error of at most 0.012.
The reference program's roundings to bfloat16 on the way count: a program that leaves them out, or rounds other values in their place, can miss the bound.
Values may be sent and summed in bfloat16 or wider, within the bound.
No kernel may reach another device: no remote copies, remote signals or barrier semaphores. Data moves between devices by JAX's collectives and lax.ppermute only.
A program may use at most 192 MiB of HBM per device.

```python
import math
import jax
import jax.numpy as jnp
from jax import lax

HQ = 24
KEY_HEADS = 8
HEAD_WIDTH = 128
TOK_DEV = 256
REACH = 4
QUERY_PER_KEY = 3
SPAN = 1024
PACKED_TOKENS = 16384


def shared_normals(key):
    random_query_seed = jax.random.fold_in(key, 101)
    random_key_seed = jax.random.fold_in(key, 202)
    query_offset = jnp.clip(jax.random.normal(random_query_seed, (PACKED_TOKENS, KEY_HEADS, QUERY_PER_KEY, HEAD_WIDTH), jnp.float32), -6.0, 6.0)
    key_offset = jnp.clip(jax.random.normal(random_key_seed, (PACKED_TOKENS, KEY_HEADS, HEAD_WIDTH), jnp.float32), -6.0, 6.0)
    return (query_offset, key_offset)


def draw_queries(key, part):
    query_offset, key_offset = shared_normals(key)
    return query_offset.reshape(PACKED_TOKENS, HQ * HEAD_WIDTH).astype(jnp.bfloat16)


def draw_keys(key, part):
    query_offset, key_offset = shared_normals(key)
    return key_offset.reshape(PACKED_TOKENS, KEY_HEADS * HEAD_WIDTH).astype(jnp.bfloat16)


def draw_doc_ids(key, part):
    key = jax.random.fold_in(key, 7)
    segment_count = PACKED_TOKENS // SPAN + 1
    cut_count = 7
    segment_keys = jax.random.split(key, segment_count)
    cut_points = jax.vmap(lambda one_key: jax.random.permutation(one_key, SPAN - 1)[:cut_count] + 1)(segment_keys).astype(jnp.int32)
    positions = jnp.arange(PACKED_TOKENS, dtype=jnp.int32)
    shifted = positions - TOK_DEV // 2 + SPAN
    segment = shifted // SPAN
    within = shifted % SPAN
    seg_cuts = cut_points[segment]
    inner_doc = jnp.sum((within[:, None] >= seg_cuts).astype(jnp.int32), axis=1)
    odd_segment = segment % 2
    inner_doc = inner_doc * odd_segment
    half_seg = segment // 2
    base = half_seg * 9 + odd_segment
    return (base + inner_doc).astype(jnp.int32)


def steps_of(stream_key, shape, pieces, smallest, top_value):
    def one(dim, parts):
        draws = jax.random.uniform(jax.random.fold_in(jax.random.fold_in(stream_key, 6), dim), (parts,), jnp.float32, smallest / len(pieces), top_value / len(pieces))
        return jnp.repeat(jnp.exp(draws), shape[dim] // parts).reshape((-1,) + (1,) * (len(shape) - dim - 1))

    loudness = one(*pieces[0])
    for cut in pieces[1:]:
        loudness = loudness * one(*cut)
    return loudness


def scatter_about(rng, shape, width, most, cuts=(), kind=jnp.bfloat16):
    gain = steps_of(rng, shape, cuts, -0.22, 0.18) if cuts else 1.0
    entries = jax.random.normal(rng, shape, jnp.float32) * width * gain
    return jnp.minimum(jnp.maximum(entries, -most), most).astype(kind)


def setup_inputs(seed: int = 0, part: int = 0) -> dict:
    arg_keys = jax.random.split(jax.random.key(seed), 7)
    part_keys = jax.random.split(jax.random.fold_in(arg_keys[6], part), 7)
    queries = draw_queries(jax.random.fold_in(jax.random.fold_in(arg_keys[6], part), 71), part)
    keys = draw_keys(jax.random.fold_in(jax.random.fold_in(arg_keys[6], part), 71), part)
    values = scatter_about(part_keys[2], (PACKED_TOKENS, KEY_HEADS * HEAD_WIDTH), 0.5, 3.0, ((0, 64),))
    grad_out = scatter_about(part_keys[3], (PACKED_TOKENS, HQ * HEAD_WIDTH), 1.0, 6.0, ((0, 64),))
    weights = jnp.clip(jnp.exp(math.log(4.0) - 2.7725887 * jax.random.uniform(part_keys[4], (PACKED_TOKENS,), jnp.float32) ** steps_of(part_keys[4], (PACKED_TOKENS,), ((0, 64),), -0.2, 0.2)), 0.25, 4.0)
    doc_ids = draw_doc_ids(jax.random.fold_in(jax.random.fold_in(arg_keys[6], part), 71), part)
    return dict(queries=queries, keys=keys, values=values, grad_out=grad_out, weights=weights, doc_ids=doc_ids)


masked_score = -1e+30

def reference(queries, keys, values, grad_out, weights, doc_ids):
    border_rows = REACH * TOK_DEV
    band_width = border_rows + TOK_DEV
    count_blocks = PACKED_TOKENS // TOK_DEV
    score_scale = 1.0 / math.sqrt(HEAD_WIDTH)
    heads_of_query = queries.reshape(PACKED_TOKENS, KEY_HEADS, QUERY_PER_KEY, HEAD_WIDTH)
    gradient_rescaled = (weights[:, None] * grad_out.astype(jnp.float32)).astype(jnp.bfloat16)
    head_gradient = gradient_rescaled.reshape(PACKED_TOKENS, KEY_HEADS, QUERY_PER_KEY, HEAD_WIDTH)
    keys_with_padding = jnp.concatenate([jnp.zeros((border_rows, KEY_HEADS * HEAD_WIDTH), keys.dtype), keys], axis=0).reshape(PACKED_TOKENS + border_rows, KEY_HEADS, HEAD_WIDTH)
    values_with_padding = jnp.concatenate([jnp.zeros((border_rows, KEY_HEADS * HEAD_WIDTH), values.dtype), values], axis=0).reshape(PACKED_TOKENS + border_rows, KEY_HEADS, HEAD_WIDTH)
    padded_ids = jnp.concatenate([jnp.full((border_rows,), -1, jnp.int32), doc_ids.astype(jnp.int32)], axis=0)
    row_ids = jnp.arange(TOK_DEV, dtype=jnp.int32)
    col_ids = jnp.arange(band_width, dtype=jnp.int32)
    remote_rows = (col_ids < border_rows)[:, None, None]

    def one_block(sums_carry, block_index):
        grad_k_all, grad_v_all = sums_carry
        first_row = (block_index * TOK_DEV).astype(jnp.int32)
        q_rows = lax.dynamic_slice_in_dim(heads_of_query, first_row, TOK_DEV, 0).astype(jnp.float32)
        g_rows = lax.dynamic_slice_in_dim(head_gradient, first_row, TOK_DEV, 0).astype(jnp.float32)
        q_ids = lax.dynamic_slice_in_dim(doc_ids.astype(jnp.int32), first_row, TOK_DEV, 0)
        band_keys = lax.dynamic_slice_in_dim(keys_with_padding, first_row, band_width, 0).astype(jnp.float32)
        band_values = lax.dynamic_slice_in_dim(values_with_padding, first_row, band_width, 0).astype(jnp.float32)
        band_ids = lax.dynamic_slice_in_dim(padded_ids, first_row, band_width, 0)
        visible = (q_ids[:, None] == band_ids[None, :]) & (col_ids[None, :] <= row_ids[:, None] + border_rows)
        scores = jnp.einsum('ihgd,jhd->hgij', q_rows, band_keys) * score_scale
        scores = jnp.where(visible, scores, masked_score)
        row_max = lax.optimization_barrier(jnp.max(scores, axis=-1, keepdims=True))
        row_total = lax.optimization_barrier(jnp.sum(jnp.exp(scores - row_max), axis=-1, keepdims=True))
        log_total = row_max + jnp.log(row_total)
        attn_probs = jnp.where(visible, jnp.exp(scores - log_total), 0.0)
        probs16 = lax.optimization_barrier(attn_probs.astype(jnp.bfloat16)).astype(jnp.float32)
        attn_out = jnp.einsum('hgij,jhd->ihgd', probs16, band_values).astype(jnp.bfloat16)
        attn_out = lax.optimization_barrier(attn_out).astype(jnp.float32)
        row_delta = jnp.einsum('ihgd,ihgd->hgi', g_rows, attn_out)
        dprobs = jnp.einsum('ihgd,jhd->hgij', g_rows, band_values)
        dscores = (attn_probs * (dprobs - row_delta[..., None]) * score_scale).astype(jnp.bfloat16)
        dscores = lax.optimization_barrier(dscores).astype(jnp.float32)
        grad_q = jnp.einsum('hgij,jhd->ihgd', dscores, band_keys)
        grad_k = jnp.einsum('hgij,ihgd->jhd', dscores, q_rows)
        grad_v = jnp.einsum('hgij,ihgd->jhd', probs16, g_rows)
        rounded_k = lax.optimization_barrier(grad_k.astype(jnp.bfloat16)).astype(jnp.float32)
        rounded_v = lax.optimization_barrier(grad_v.astype(jnp.bfloat16)).astype(jnp.float32)
        grad_k = jnp.where(remote_rows, rounded_k, grad_k)
        grad_v = jnp.where(remote_rows, rounded_v, grad_v)
        old_k = lax.dynamic_slice_in_dim(grad_k_all, first_row, band_width, 0)
        old_v = lax.dynamic_slice_in_dim(grad_v_all, first_row, band_width, 0)
        grad_k_all = lax.dynamic_update_slice_in_dim(grad_k_all, old_k + grad_k, first_row, 0)
        grad_v_all = lax.dynamic_update_slice_in_dim(grad_v_all, old_v + grad_v, first_row, 0)
        return ((grad_k_all, grad_v_all), grad_q.astype(jnp.bfloat16))
    opening_totals = (jnp.zeros((PACKED_TOKENS + border_rows, KEY_HEADS, HEAD_WIDTH), jnp.float32), jnp.zeros((PACKED_TOKENS + border_rows, KEY_HEADS, HEAD_WIDTH), jnp.float32))
    closing_totals, grad_blocks = lax.scan(one_block, opening_totals, jnp.arange(count_blocks, dtype=jnp.int32))
    grad_queries = grad_blocks.reshape(PACKED_TOKENS, HQ * HEAD_WIDTH)
    key_gradient = closing_totals[0][border_rows:].reshape(PACKED_TOKENS, KEY_HEADS * HEAD_WIDTH).astype(jnp.bfloat16)
    value_gradient = closing_totals[1][border_rows:].reshape(PACKED_TOKENS, KEY_HEADS * HEAD_WIDTH).astype(jnp.bfloat16)
    return (grad_queries, key_gradient, value_gradient)
```

```python
import functools
import math

import jax
import jax.numpy as jnp
from jax import lax
from jax.experimental import pallas as pl
from jax.experimental.pallas import tpu as pltpu
from jax.sharding import PartitionSpec as P

WIDTH = 128
GROUP = 3
RING = 4
TOK = 256
ROW = RING * TOK
CHUNKS = 2
QT = 128
KT = 256
PAD = 128
QW = GROUP * WIDTH
TILES = ROW // QT
KEYS = PAD + 2 * ROW
WINDOWS = 5
AXES = ("inner", "outer")
NEG = -1e30

anywhere = pl.BlockSpec(memory_space=pl.ANY)
in_smem = pl.BlockSpec(memory_space=pltpu.SMEM)
in_vmem = pl.BlockSpec(memory_space=pltpu.VMEM)


def shift_ring(x, by, count):
    return lax.ppermute(x, AXES, [(i, i // RING * RING + (i + by) % RING) for i in range(count)])


def shift_row(x, by, count):
    pairs = [(i, i + by * RING) for i in range(count) if 0 <= i + by * RING < count]
    return lax.ppermute(x, AXES, pairs)


def run_copies(copies, sems):
    started = [pltpu.make_async_copy(a, b, sems.at[i]) for i, (a, b) in enumerate(copies)]
    for c in started:
        c.start()
    for c in started:
        c.wait()


def columns(ref, first, width):
    return ref.at[:, pl.ds(pl.multiple_of(first, WIDTH), width)]


def split_keys_kernel(z_ref, k_ref, v_ref, *rest):
    outs, sems = rest[:RING], rest[RING]
    z = z_ref[0]
    copies = []
    for s in range(RING):
        target = lax.rem(z + s, RING)
        for c in range(CHUNKS):
            first = (target * CHUNKS + c) * WIDTH
            for i, ref in enumerate((k_ref, v_ref)):
                at = (2 * c + i) * WIDTH
                copies.append((columns(ref, first, WIDTH), outs[s].at[:, at : at + WIDTH]))
    run_copies(copies, sems)


def split_keys(z, keys, values):
    piece = jax.ShapeDtypeStruct((TOK, 2 * CHUNKS * WIDTH), keys.dtype)
    return pl.pallas_call(
        split_keys_kernel,
        out_shape=[piece] * RING,
        in_specs=[in_smem, anywhere, anywhere],
        out_specs=[anywhere] * RING,
        scratch_shapes=[pltpu.SemaphoreType.DMA((RING * CHUNKS * 2,))],
        name="split_keys",
    )(z, keys, values)


def split_queries_kernel(chunk, z_ref, q_ref, g_ref, *rest):
    outs, sems = rest[:RING], rest[RING]
    z = z_ref[0]
    copies = []
    for s in range(RING):
        target = lax.rem(z + s, RING)
        first = (target * CHUNKS + chunk) * QW
        copies.append((columns(q_ref, first, QW), outs[s].at[:, :QW]))
        copies.append((columns(g_ref, first, QW), outs[s].at[:, QW:]))
    run_copies(copies, sems)


def split_queries(chunk, z, queries, head_gradient):
    piece = jax.ShapeDtypeStruct((TOK, 2 * QW), queries.dtype)
    return pl.pallas_call(
        functools.partial(split_queries_kernel, chunk),
        out_shape=[piece] * RING,
        in_specs=[in_smem, anywhere, anywhere],
        out_specs=[anywhere] * RING,
        scratch_shapes=[pltpu.SemaphoreType.DMA((RING * 2,))],
        name="split_queries",
    )(z, queries, head_gradient)


def attention_kernel(chunk, z_ref, low_ref, start_ref, *rest):
    kv_refs, halo_ref, qg_refs = rest[:RING], rest[RING], rest[RING + 1 : 2 * RING + 1]
    rest = rest[2 * RING + 1 :]
    dq_refs, own_ref, back_ref = rest[:RING], rest[RING], rest[RING + 1]
    k, v, kt, vt, q, g, dk, dv, dq, probs, sems = rest[RING + 2 :]
    z = z_ref[0]
    scale = 1.0 / math.sqrt(WIDTH)

    copies = []
    for s in range(RING):
        source = lax.rem(z + RING - s, RING)
        rows = pl.ds(pl.multiple_of(source * TOK, TOK), TOK)
        halo_rows = pl.ds(pl.multiple_of(PAD + source * TOK, WIDTH), TOK)
        own_rows = pl.ds(pl.multiple_of(PAD + ROW + source * TOK, WIDTH), TOK)
        for i, ref in enumerate((k, v)):
            at = (2 * chunk + i) * WIDTH
            copies.append((kv_refs[s].at[:, at : at + WIDTH], ref.at[own_rows, :]))
            copies.append(
                (halo_ref.at[s * TOK : (s + 1) * TOK, i * WIDTH : (i + 1) * WIDTH], ref.at[halo_rows, :])
            )
        for i, ref in enumerate((q, g)):
            for h in range(GROUP):
                at = (i * GROUP + h) * WIDTH
                copies.append((qg_refs[s].at[:, at : at + WIDTH], ref.at[h, rows, :]))
    started = [pltpu.make_async_copy(a, b, sems.at[i]) for i, (a, b) in enumerate(copies)]
    for c in started:
        c.start()
    k[0:PAD, :] = jnp.zeros((PAD, WIDTH), k.dtype)
    v[0:PAD, :] = jnp.zeros((PAD, WIDTH), v.dtype)
    dk[...] = jnp.zeros(dk.shape, dk.dtype)
    dv[...] = jnp.zeros(dv.shape, dv.dtype)
    for c in started:
        c.wait()
    kt[...] = k[...].T
    vt[...] = v[...].T

    def tile(t, carry):
        first = pl.multiple_of(t * QT, QT)
        qs = q[:, pl.ds(first, QT), :].reshape(QW, WIDTH)
        gs = g[:, pl.ds(first, QT), :].reshape(QW, WIDTH)
        q_t, g_t = qs.T, gs.T
        starts = start_ref[:, pl.ds(first, QT)]
        end = PAD + ROW + first + QT
        count = (end - PAD - low_ref[t] + KT - 1) // KT
        query_at = ROW + first + lax.broadcasted_iota(jnp.int32, (KT, QT), 1)
        key_at = lax.broadcasted_iota(jnp.int32, (KT, QT), 0)

        def base_of(w):
            return pl.multiple_of(end - KT * (w + 1), WIDTH)

        def slot(w):
            return pl.ds(pl.multiple_of(w * KT, KT), KT)

        def scores(w, top):
            base = base_of(w)
            s = jnp.dot(k[pl.ds(base, KT), :], q_t, preferred_element_type=jnp.float32) * scale
            at = key_at + (base - PAD)
            seen = (at >= starts) & (at <= query_at)
            s = jnp.where(jnp.concatenate([seen] * GROUP, axis=1), s, NEG)
            probs[slot(w), :] = s
            return jnp.maximum(top, jnp.max(s.reshape(KT // 8, 8, QW), axis=0))

        top = lax.fori_loop(0, count, scores, jnp.full((8, QW), NEG, jnp.float32))
        top = jnp.max(top, axis=0, keepdims=True)

        def exponents(w, total):
            e = jnp.exp(probs[slot(w), :] - top)
            probs[slot(w), :] = e
            return total + jnp.sum(e.reshape(KT // 8, 8, QW), axis=0)

        total = lax.fori_loop(0, count, exponents, jnp.zeros((8, QW), jnp.float32))
        inverse = 1.0 / jnp.sum(total, axis=0, keepdims=True)

        def outputs(w, out):
            p16 = (probs[slot(w), :] * inverse).astype(jnp.bfloat16)
            return out + jnp.dot(
                vt[:, pl.ds(base_of(w), KT)], p16, preferred_element_type=jnp.float32
            )

        zeros = jnp.zeros((WIDTH, QW), jnp.float32)
        out = lax.fori_loop(0, count, outputs, zeros)
        out = out.astype(jnp.bfloat16).astype(jnp.float32)
        delta = jnp.sum(g_t.astype(jnp.float32) * out, axis=0, keepdims=True)

        def gradients(w, dq_t):
            base = base_of(w)
            keys = pl.ds(base, KT)
            p = probs[slot(w), :] * inverse
            p16 = p.astype(jnp.bfloat16)
            dp = jnp.dot(v[keys, :], g_t, preferred_element_type=jnp.float32)
            ds = (p * (dp - delta) * scale).astype(jnp.bfloat16)
            dk[keys, :] += jnp.dot(ds, qs, preferred_element_type=jnp.float32)
            dv[keys, :] += jnp.dot(p16, gs, preferred_element_type=jnp.float32)
            return dq_t + jnp.dot(kt[:, keys], ds, preferred_element_type=jnp.float32)

        dq_t = lax.fori_loop(0, count, gradients, zeros)
        for h in range(GROUP):
            dq[pl.ds(first, QT), h * WIDTH : (h + 1) * WIDTH] = (
                dq_t[:, h * WIDTH : (h + 1) * WIDTH].T.astype(jnp.bfloat16)
            )
        return carry

    lax.fori_loop(0, TILES, tile, 0)
    copies = []
    for s in range(RING):
        owner = lax.rem(z + s, RING)
        copies.append((dq.at[pl.ds(pl.multiple_of(owner * TOK, TOK), TOK), :], dq_refs[s]))
    started = [pltpu.make_async_copy(a, b, sems.at[i]) for i, (a, b) in enumerate(copies)]
    for c in started:
        c.start()
    for i, ref in enumerate((dk, dv)):
        cols = slice(i * WIDTH, (i + 1) * WIDTH)
        back_ref[:, cols] = ref[PAD : PAD + ROW, :].astype(jnp.bfloat16)
        own_ref[:, cols] = ref[PAD + ROW :, :]
    for c in started:
        c.wait()


def attention(chunk, z, low, starts, kv, halo, qg):
    bf16, f32 = jnp.bfloat16, jnp.float32
    products = 7 * GROUP * ROW * ROW * WIDTH
    return pl.pallas_call(
        functools.partial(attention_kernel, chunk),
        out_shape=[jax.ShapeDtypeStruct((TOK, QW), bf16)] * RING
        + [
            jax.ShapeDtypeStruct((ROW, 2 * WIDTH), f32),
            jax.ShapeDtypeStruct((ROW, 2 * WIDTH), bf16),
        ],
        in_specs=[in_smem, in_smem, in_vmem] + [anywhere] * (2 * RING + 1),
        out_specs=[anywhere] * RING + [in_vmem, in_vmem],
        scratch_shapes=[
            pltpu.VMEM((KEYS, WIDTH), bf16),
            pltpu.VMEM((KEYS, WIDTH), bf16),
            pltpu.VMEM((WIDTH, KEYS), bf16),
            pltpu.VMEM((WIDTH, KEYS), bf16),
            pltpu.VMEM((GROUP, ROW, WIDTH), bf16),
            pltpu.VMEM((GROUP, ROW, WIDTH), bf16),
            pltpu.VMEM((KEYS, WIDTH), f32),
            pltpu.VMEM((KEYS, WIDTH), f32),
            pltpu.VMEM((ROW, QW), bf16),
            pltpu.VMEM((WINDOWS * KT, QW), f32),
            pltpu.SemaphoreType.DMA((RING * (4 + 2 * GROUP),)),
        ],
        compiler_params=pltpu.CompilerParams(vmem_limit_bytes=40 * 1024 * 1024),
        cost_estimate=pl.CostEstimate(
            flops=2 * products, bytes_accessed=8 * 1024 * 1024, transcendentals=GROUP * ROW * ROW
        ),
        name="attention",
    )(z, low, starts, *kv, halo, *qg)


def join_kernel(z_ref, *rest):
    n = RING * CHUNKS
    dq_refs, dkv_refs = rest[:n], rest[n : 2 * n]
    dq_out, dk_out, dv_out, sems = rest[2 * n :]
    z = z_ref[0]
    copies = []
    for s in range(RING):
        group = lax.rem(z + RING - s, RING)
        for c in range(CHUNKS):
            head = group * CHUNKS + c
            copies.append((dq_refs[s * CHUNKS + c], columns(dq_out, head * QW, QW)))
            for i, ref in enumerate((dk_out, dv_out)):
                piece = dkv_refs[s * CHUNKS + c].at[:, i * WIDTH : (i + 1) * WIDTH]
                copies.append((piece, columns(ref, head * WIDTH, WIDTH)))
    run_copies(copies, sems)


def join(z, dq, dkv):
    heads = RING * CHUNKS
    return pl.pallas_call(
        join_kernel,
        out_shape=[
            jax.ShapeDtypeStruct((TOK, heads * QW), jnp.bfloat16),
            jax.ShapeDtypeStruct((TOK, heads * WIDTH), jnp.bfloat16),
            jax.ShapeDtypeStruct((TOK, heads * WIDTH), jnp.bfloat16),
        ],
        in_specs=[in_smem] + [anywhere] * (2 * heads),
        out_specs=[anywhere] * 3,
        scratch_shapes=[pltpu.SemaphoreType.DMA((3 * heads,))],
        name="join",
    )(z, *dq, *dkv)


def body(queries, keys, values, grad_out, weights, doc_ids):
    count = lax.axis_size(AXES)
    place = lax.axis_index(AXES)
    row = place // RING
    ring_place = lax.rem(place, RING)
    z = ring_place.reshape(1).astype(jnp.int32)
    shifts = range(RING)

    kv = split_keys(z, keys, values)
    kv = [kv[0]] + [shift_ring(kv[s], s, count) for s in shifts[1:]]

    all_ids = lax.all_gather(doc_ids, AXES, tiled=True)
    own_ids = lax.dynamic_slice(all_ids, (row * ROW,), (ROW,))
    past_ids = lax.dynamic_slice(all_ids, (jnp.maximum(row - 1, 0) * ROW,), (ROW,))
    past_ids = jnp.where(row > 0, past_ids, -1)
    both = jnp.concatenate([past_ids, own_ids])
    starts = jnp.sum((both[:, None] < own_ids[None, :]).astype(jnp.int32), axis=0)
    low = starts[::QT]
    starts = starts[None, :]

    head_gradient = (weights[:, None] * grad_out.astype(jnp.float32)).astype(jnp.bfloat16)
    qg = []
    for c in range(CHUNKS):
        pieces = split_queries(c, z, queries, head_gradient)
        qg.append([pieces[0]] + [shift_ring(pieces[s], s, count) for s in shifts[1:]])
    halo = []
    for c in range(CHUNKS):
        cols = slice(2 * c * WIDTH, 2 * (c + 1) * WIDTH)
        halo.append(shift_row(jnp.concatenate([kv[s][:, cols] for s in shifts]), 1, count))

    dq_parts, dkv_parts = {}, {}
    for c in range(CHUNKS):
        results = attention(c, z, low, starts, kv, halo[c], qg[c])
        dq, own, back = results[:RING], results[RING], results[RING + 1]
        from_next = shift_row(back, -1, count)
        for s in shifts:
            first = lax.rem(ring_place + s, RING) * TOK
            part = lax.dynamic_slice(own, (first, 0), (TOK, 2 * WIDTH)) + lax.dynamic_slice(
                from_next, (first, 0), (TOK, 2 * WIDTH)
            ).astype(jnp.float32)
            part = part.astype(jnp.bfloat16)
            dq_parts[s, c] = shift_ring(dq[s], s, count) if s else dq[s]
            dkv_parts[s, c] = shift_ring(part, s, count) if s else part
    order = [(s, c) for s in shifts for c in range(CHUNKS)]
    return tuple(join(z, [dq_parts[o] for o in order], [dkv_parts[o] for o in order]))


def solution(mesh):
    rows = P(("dp", "inner", "outer"), None)
    flat = P(("dp", "inner", "outer"))
    return jax.shard_map(
        body,
        mesh=mesh,
        in_specs=(rows, rows, rows, rows, flat, flat),
        out_specs=(rows, rows, rows),
        check_vma=False,
    )
```

```python
import functools
import math

import jax
import jax.numpy as jnp
from jax import lax
from jax.experimental import pallas as pl
from jax.experimental.pallas import tpu as pltpu
from jax.sharding import PartitionSpec as P

WIDTH = 128
GROUP = 3
RING = 4
TOK = 256
ROW = RING * TOK
CHUNKS = 2
QT = 128
KT = 256
PAD = 128
QW = GROUP * WIDTH
TILES = ROW // QT
KEYS = PAD + 2 * ROW
WINDOWS = 5
IDS = 16
AXES = ("inner", "outer")
NEG = -1e30

anywhere = pl.BlockSpec(memory_space=pl.ANY)
in_smem = pl.BlockSpec(memory_space=pltpu.SMEM)
in_vmem = pl.BlockSpec(memory_space=pltpu.VMEM)


def shift_ring(x, by, count):
    return lax.ppermute(x, AXES, [(i, i // RING * RING + (i + by) % RING) for i in range(count)])


def shift_row(x, by, count):
    pairs = [(i, i + by * RING) for i in range(count) if 0 <= i + by * RING < count]
    return lax.ppermute(x, AXES, pairs)


def run_copies(copies, sems):
    started = [pltpu.make_async_copy(a, b, sems.at[i]) for i, (a, b) in enumerate(copies)]
    for c in started:
        c.start()
    for c in started:
        c.wait()


def columns(ref, first, width):
    return ref.at[:, pl.ds(pl.multiple_of(first, WIDTH), width)]


def split_keys_kernel(z_ref, k_ref, v_ref, ids_ref, *rest):
    outs, sems = rest[:RING], rest[RING]
    z = z_ref[0]
    copies = []
    for s in range(RING):
        target = lax.rem(z + s, RING)
        for c in range(CHUNKS):
            first = (target * CHUNKS + c) * WIDTH
            for i, ref in enumerate((k_ref, v_ref)):
                at = (2 * c + i) * WIDTH
                copies.append((columns(ref, first, WIDTH), outs[s].at[0:TOK, at : at + WIDTH]))
        copies.append((ids_ref, outs[s].at[TOK:, :]))
    run_copies(copies, sems)


def split_keys(z, keys, values, ids):
    piece = jax.ShapeDtypeStruct((TOK + IDS, 2 * CHUNKS * WIDTH), keys.dtype)
    return pl.pallas_call(
        split_keys_kernel,
        out_shape=[piece] * RING,
        in_specs=[in_smem, in_vmem, in_vmem, in_vmem],
        out_specs=[anywhere] * RING,
        scratch_shapes=[pltpu.SemaphoreType.DMA((RING * (CHUNKS * 2 + 1),))],
        name="split_keys",
    )(z, keys, values, ids)


def split_queries_kernel(z_ref, q_ref, g_ref, w_ref, *rest):
    n = RING * CHUNKS
    outs, scaled, sems = rest[:n], rest[n], rest[n + 1]
    z = z_ref[0]
    started = []

    def start(source, target):
        copy = pltpu.make_async_copy(source, target, sems.at[len(started)])
        copy.start()
        started.append(copy)

    places = [(c, s) for c in range(CHUNKS) for s in (1, 2, 3, 0)]
    for c, s in places:
        first = (lax.rem(z + s, RING) * CHUNKS + c) * QW
        start(columns(q_ref, first, QW), outs[c * RING + s].at[:, :QW])
    w = w_ref[...]
    for c, s in places:
        first = pl.multiple_of((lax.rem(z + s, RING) * CHUNKS + c) * QW, WIDTH)
        cols = pl.ds(first, QW)
        scaled[:, cols] = (w * g_ref[:, cols].astype(jnp.float32)).astype(jnp.bfloat16)
        start(scaled.at[:, cols], outs[c * RING + s].at[:, QW:])
    for copy in started:
        copy.wait()


def split_queries(z, queries, grad_out, weights):
    piece = jax.ShapeDtypeStruct((TOK, 2 * QW), queries.dtype)
    pieces = pl.pallas_call(
        split_queries_kernel,
        out_shape=[piece] * (RING * CHUNKS),
        in_specs=[in_smem, in_vmem, in_vmem, in_vmem],
        out_specs=[anywhere] * (RING * CHUNKS),
        scratch_shapes=[
            pltpu.VMEM(grad_out.shape, jnp.bfloat16),
            pltpu.SemaphoreType.DMA((RING * CHUNKS * 2,)),
        ],
        compiler_params=pltpu.CompilerParams(vmem_limit_bytes=32 * 1024 * 1024),
        name="split_queries",
    )(z, queries, grad_out, weights)
    return [pieces[c * RING : (c + 1) * RING] for c in range(CHUNKS)]


def attention_kernel(chunk, z_ref, low_ref, start_ref, *rest):
    kv_refs, halo_ref, qg_refs = rest[:RING], rest[RING], rest[RING + 1 : 2 * RING + 1]
    rest = rest[2 * RING + 1 :]
    dq_refs, own_ref, back_ref = rest[:RING], rest[RING], rest[RING + 1]
    k, v, kt, vt, q, g, dk, dv, dq, probs, sems = rest[RING + 2 :]
    z = z_ref[0]
    scale = 1.0 / math.sqrt(WIDTH)

    copies = []
    for s in range(RING):
        source = lax.rem(z + RING - s, RING)
        rows = pl.ds(pl.multiple_of(source * TOK, TOK), TOK)
        halo_rows = pl.ds(pl.multiple_of(PAD + source * TOK, WIDTH), TOK)
        own_rows = pl.ds(pl.multiple_of(PAD + ROW + source * TOK, WIDTH), TOK)
        for i, ref in enumerate((k, v)):
            at = (2 * chunk + i) * WIDTH
            copies.append((kv_refs[s].at[0:TOK, at : at + WIDTH], ref.at[own_rows, :]))
            copies.append(
                (halo_ref.at[s * TOK : (s + 1) * TOK, i * WIDTH : (i + 1) * WIDTH], ref.at[halo_rows, :])
            )
        for i, ref in enumerate((q, g)):
            for h in range(GROUP):
                at = (i * GROUP + h) * WIDTH
                copies.append((qg_refs[s].at[:, at : at + WIDTH], ref.at[h, rows, :]))
    started = [pltpu.make_async_copy(a, b, sems.at[i]) for i, (a, b) in enumerate(copies)]
    for c in started:
        c.start()
    k[0:PAD, :] = jnp.zeros((PAD, WIDTH), k.dtype)
    v[0:PAD, :] = jnp.zeros((PAD, WIDTH), v.dtype)
    dk[...] = jnp.zeros(dk.shape, dk.dtype)
    dv[...] = jnp.zeros(dv.shape, dv.dtype)
    for c in started:
        c.wait()
    kt[...] = k[...].T
    vt[...] = v[...].T

    def tile(t, carry):
        first = pl.multiple_of(t * QT, QT)
        qs = q[:, pl.ds(first, QT), :].reshape(QW, WIDTH)
        gs = g[:, pl.ds(first, QT), :].reshape(QW, WIDTH)
        q_t, g_t = qs.T, gs.T
        starts = start_ref[:, pl.ds(first, QT)]
        end = PAD + ROW + first + QT
        count = (end - PAD - low_ref[t] + KT - 1) // KT
        query_at = ROW + first + lax.broadcasted_iota(jnp.int32, (KT, QT), 1)
        key_at = lax.broadcasted_iota(jnp.int32, (KT, QT), 0)

        def base_of(w):
            return pl.multiple_of(end - KT * (w + 1), WIDTH)

        def slot(w):
            return pl.ds(pl.multiple_of(w * KT, KT), KT)

        def scores(w, top):
            base = base_of(w)
            s = jnp.dot(k[pl.ds(base, KT), :], q_t, preferred_element_type=jnp.float32) * scale
            at = key_at + (base - PAD)
            seen = (at >= starts) & (at <= query_at)
            s = jnp.where(jnp.concatenate([seen] * GROUP, axis=1), s, NEG)
            probs[slot(w), :] = s
            return jnp.maximum(top, jnp.max(s.reshape(KT // 8, 8, QW), axis=0))

        top = lax.fori_loop(0, count, scores, jnp.full((8, QW), NEG, jnp.float32))
        top = jnp.max(top, axis=0, keepdims=True)

        def exponents(w, total):
            e = jnp.exp(probs[slot(w), :] - top)
            probs[slot(w), :] = e
            return total + jnp.sum(e.reshape(KT // 8, 8, QW), axis=0)

        total = lax.fori_loop(0, count, exponents, jnp.zeros((8, QW), jnp.float32))
        inverse = 1.0 / jnp.sum(total, axis=0, keepdims=True)

        def outputs(w, out):
            p16 = (probs[slot(w), :] * inverse).astype(jnp.bfloat16)
            return out + jnp.dot(
                vt[:, pl.ds(base_of(w), KT)], p16, preferred_element_type=jnp.float32
            )

        zeros = jnp.zeros((WIDTH, QW), jnp.float32)
        out = lax.fori_loop(0, count, outputs, zeros)
        out = out.astype(jnp.bfloat16).astype(jnp.float32)
        delta = jnp.sum(g_t.astype(jnp.float32) * out, axis=0, keepdims=True)

        def gradients(w, dq_t):
            base = base_of(w)
            keys = pl.ds(base, KT)
            p = probs[slot(w), :] * inverse
            p16 = p.astype(jnp.bfloat16)
            dp = jnp.dot(v[keys, :], g_t, preferred_element_type=jnp.float32)
            ds = (p * (dp - delta) * scale).astype(jnp.bfloat16)
            dk[keys, :] += jnp.dot(ds, qs, preferred_element_type=jnp.float32)
            dv[keys, :] += jnp.dot(p16, gs, preferred_element_type=jnp.float32)
            return dq_t + jnp.dot(kt[:, keys], ds, preferred_element_type=jnp.float32)

        dq_t = lax.fori_loop(0, count, gradients, zeros)
        for h in range(GROUP):
            dq[pl.ds(first, QT), h * WIDTH : (h + 1) * WIDTH] = (
                dq_t[:, h * WIDTH : (h + 1) * WIDTH].T.astype(jnp.bfloat16)
            )
        return carry

    lax.fori_loop(0, TILES, tile, 0)
    copies = []
    for s in range(RING):
        owner = lax.rem(z + s, RING)
        copies.append((dq.at[pl.ds(pl.multiple_of(owner * TOK, TOK), TOK), :], dq_refs[s]))
    started = [pltpu.make_async_copy(a, b, sems.at[i]) for i, (a, b) in enumerate(copies)]
    for c in started:
        c.start()
    for i, ref in enumerate((dk, dv)):
        cols = slice(i * WIDTH, (i + 1) * WIDTH)
        back_ref[:, cols] = ref[PAD : PAD + ROW, :].astype(jnp.bfloat16)
        own_ref[:, cols] = ref[PAD + ROW :, :]
    for c in started:
        c.wait()


def attention(chunk, z, low, starts, kv, halo, qg):
    bf16, f32 = jnp.bfloat16, jnp.float32
    products = 7 * GROUP * ROW * ROW * WIDTH
    return pl.pallas_call(
        functools.partial(attention_kernel, chunk),
        out_shape=[jax.ShapeDtypeStruct((TOK, QW), bf16)] * RING
        + [
            jax.ShapeDtypeStruct((ROW, 2 * WIDTH), f32),
            jax.ShapeDtypeStruct((ROW, 2 * WIDTH), bf16),
        ],
        in_specs=[in_smem, in_smem, in_vmem] + [anywhere] * (2 * RING + 1),
        out_specs=[anywhere] * RING + [in_vmem, in_vmem],
        scratch_shapes=[
            pltpu.VMEM((KEYS, WIDTH), bf16),
            pltpu.VMEM((KEYS, WIDTH), bf16),
            pltpu.VMEM((WIDTH, KEYS), bf16),
            pltpu.VMEM((WIDTH, KEYS), bf16),
            pltpu.VMEM((GROUP, ROW, WIDTH), bf16),
            pltpu.VMEM((GROUP, ROW, WIDTH), bf16),
            pltpu.VMEM((KEYS, WIDTH), f32),
            pltpu.VMEM((KEYS, WIDTH), f32),
            pltpu.VMEM((ROW, QW), bf16),
            pltpu.VMEM((WINDOWS * KT, QW), f32),
            pltpu.SemaphoreType.DMA((RING * (4 + 2 * GROUP),)),
        ],
        compiler_params=pltpu.CompilerParams(vmem_limit_bytes=40 * 1024 * 1024),
        cost_estimate=pl.CostEstimate(
            flops=2 * products, bytes_accessed=8 * 1024 * 1024, transcendentals=GROUP * ROW * ROW
        ),
        name="attention",
    )(z, low, starts, *kv, halo, *qg)


def join_kernel(z_ref, *rest):
    n = RING * CHUNKS
    dq_refs, dkv_refs = rest[:n], rest[n : 2 * n]
    dq_out, dk_out, dv_out, sems = rest[2 * n :]
    z = z_ref[0]
    copies = []
    for s in range(RING):
        group = lax.rem(z + RING - s, RING)
        for c in range(CHUNKS):
            head = group * CHUNKS + c
            copies.append((dq_refs[s * CHUNKS + c], columns(dq_out, head * QW, QW)))
            for i, ref in enumerate((dk_out, dv_out)):
                piece = dkv_refs[s * CHUNKS + c].at[:, i * WIDTH : (i + 1) * WIDTH]
                copies.append((piece, columns(ref, head * WIDTH, WIDTH)))
    run_copies(copies, sems)


def join(z, dq, dkv):
    heads = RING * CHUNKS
    return pl.pallas_call(
        join_kernel,
        out_shape=[
            jax.ShapeDtypeStruct((TOK, heads * QW), jnp.bfloat16),
            jax.ShapeDtypeStruct((TOK, heads * WIDTH), jnp.bfloat16),
            jax.ShapeDtypeStruct((TOK, heads * WIDTH), jnp.bfloat16),
        ],
        in_specs=[in_smem] + [anywhere] * (2 * heads),
        out_specs=[in_vmem] * 3,
        scratch_shapes=[pltpu.SemaphoreType.DMA((3 * heads,))],
        compiler_params=pltpu.CompilerParams(vmem_limit_bytes=32 * 1024 * 1024),
        name="join",
    )(z, *dq, *dkv)


def body(queries, keys, values, grad_out, weights, doc_ids):
    count = lax.axis_size(AXES)
    place = lax.axis_index(AXES)
    row = place // RING
    ring_place = lax.rem(place, RING)
    z = ring_place.reshape(1).astype(jnp.int32)
    shifts = range(RING)

    bf16 = jnp.bfloat16
    ids = jnp.pad(doc_ids.astype(bf16)[None, :], ((0, IDS - 1), (0, 2 * CHUNKS * WIDTH - TOK)))
    kv = split_keys(z, keys, values, ids)
    kv = [kv[0]] + [shift_ring(kv[s], s, count) for s in shifts[1:]]
    qg = split_queries(z, queries, grad_out, weights[:, None])
    qg = [[q[0]] + [shift_ring(q[s], s, count) for s in shifts[1:]] for q in qg]

    row_ids = jnp.concatenate([kv[s][TOK : TOK + 1, :TOK] for s in shifts])
    halo = []
    for c in range(CHUNKS):
        cols = slice(2 * c * WIDTH, 2 * (c + 1) * WIDTH)
        parts = [kv[s][:TOK, cols] for s in shifts]
        if c == 0:
            parts.append(jnp.pad(row_ids, ((0, IDS - RING), (0, 0))))
        halo.append(shift_row(jnp.concatenate(parts), 1, count))
    past_ids = jnp.where(row > 0, halo[0][ROW : ROW + RING], -1.0)
    before = jnp.concatenate([past_ids, row_ids]).reshape(-1)
    own_ids = jnp.roll(row_ids[::-1], ring_place + 1, axis=0).reshape(-1)
    starts = jnp.sum((before[:, None] < own_ids[None, :]).astype(jnp.int32), axis=0)
    low = starts[::QT]
    starts = starts[None, :]

    dq_parts, dkv_parts = {}, {}
    for c in range(CHUNKS):
        results = attention(c, z, low, starts, kv, halo[c], qg[c])
        dq, own, back = results[:RING], results[RING], results[RING + 1]
        from_next = shift_row(back, -1, count)
        for s in shifts:
            first = lax.rem(ring_place + s, RING) * TOK
            part = lax.dynamic_slice(own, (first, 0), (TOK, 2 * WIDTH)) + lax.dynamic_slice(
                from_next, (first, 0), (TOK, 2 * WIDTH)
            ).astype(jnp.float32)
            part = part.astype(jnp.bfloat16)
            dq_parts[s, c] = shift_ring(dq[s], s, count) if s else dq[s]
            dkv_parts[s, c] = shift_ring(part, s, count) if s else part
    order = [(s, c) for s in shifts for c in range(CHUNKS)]
    return tuple(join(z, [dq_parts[o] for o in order], [dkv_parts[o] for o in order]))


def solution(mesh):
    rows = P(("dp", "inner", "outer"), None)
    flat = P(("dp", "inner", "outer"))
    return jax.shard_map(
        body,
        mesh=mesh,
        in_specs=(rows, rows, rows, rows, flat, flat),
        out_specs=(rows, rows, rows),
        check_vma=False,
    )
```

```python
import functools
import math

import jax
import jax.numpy as jnp
from jax import lax
from jax.experimental import pallas as pl
from jax.experimental.pallas import tpu as pltpu
from jax.sharding import PartitionSpec as P

WIDTH = 128
GROUP = 3
RING = 4
TOK = 256
ROW = RING * TOK
CHUNKS = 2
QT = 128
KT = 256
PAD = 128
QW = GROUP * WIDTH
TILES = ROW // QT
KEYS = PAD + 2 * ROW
WINDOWS = 5
IDS = 16
EARLY, LATE = (0, 2), (1, 3)
AXES = ("inner", "outer")
NEG = -1e30
VMEM_LIMIT = 48 * 1024 * 1024
PACK_LIMIT = 60 * 1024 * 1024

in_hbm = pl.BlockSpec(memory_space=pltpu.HBM)
in_smem = pl.BlockSpec(memory_space=pltpu.SMEM)
in_vmem = pl.BlockSpec(memory_space=pltpu.VMEM)


def shift_ring(x, by, count):
    return lax.ppermute(x, AXES, [(i, i // RING * RING + (i + by) % RING) for i in range(count)])


def shift_row(x, by, ring_by, count):
    pairs = [(i, (i // RING + by) * RING + (i + ring_by) % RING) for i in range(count)]
    return lax.ppermute(x, AXES, [(i, j) for i, j in pairs if 0 <= j < count])


class Copies:
    def __init__(self, sems):
        self.sems, self.started = sems, []

    def start(self, source, target):
        copy = pltpu.make_async_copy(source, target, self.sems.at[len(self.started)])
        copy.start()
        self.started.append(copy)
        return copy

    def wait(self):
        for copy in self.started:
            copy.wait()


def columns(ref, first, width):
    return ref.at[:, pl.ds(pl.multiple_of(first, WIDTH), width)]


def pack_keys_kernel(place_ref, k_ref, v_ref, ids_ref, *rest):
    kv_refs, (kv, ids, sems_in, sems_out) = rest[:RING], rest[RING:]
    z = place_ref[0]
    order = (2, 1, 3, 0)
    inward, outward = Copies(sems_in), Copies(sems_out)
    for s in order:
        target = lax.rem(z + s, RING)
        for c in range(CHUNKS):
            for i, ref in enumerate((k_ref, v_ref)):
                at = (2 * c + i) * WIDTH
                source = columns(ref, (target * CHUNKS + c) * WIDTH, WIDTH)
                inward.start(source, kv.at[s, :, at : at + WIDTH])
    ids[...] = jnp.zeros(ids.shape, ids.dtype)
    ids[0:1, 0:TOK] = ids_ref[...].astype(jnp.float32).astype(jnp.bfloat16)
    for s in range(RING):
        outward.start(ids, kv_refs[s].at[TOK:, :])
    for i, s in enumerate(order):
        for copy in inward.started[2 * CHUNKS * i : 2 * CHUNKS * (i + 1)]:
            copy.wait()
        outward.start(kv.at[s], kv_refs[s].at[0:TOK, :])
    outward.wait()


def pack_keys(place, keys, values, ids):
    bf16 = jnp.bfloat16
    width = 2 * CHUNKS * WIDTH
    return pl.pallas_call(
        pack_keys_kernel,
        out_shape=[jax.ShapeDtypeStruct((TOK + IDS, width), bf16)] * RING,
        in_specs=[in_smem, in_hbm, in_hbm, in_vmem],
        out_specs=[in_hbm] * RING,
        scratch_shapes=[
            pltpu.VMEM((RING, TOK, width), bf16),
            pltpu.VMEM((IDS, width), bf16),
            pltpu.SemaphoreType.DMA((RING * 2 * CHUNKS,)),
            pltpu.SemaphoreType.DMA((RING * 2,)),
        ],
        compiler_params=pltpu.CompilerParams(vmem_limit_bytes=PACK_LIMIT),
        name="pack_keys",
    )(place, keys, values, ids)


def pack_queries_kernel(place_ref, w_ref, q_ref, g_ref, *rest):
    n = RING * CHUNKS
    qg_refs, (qg, sems_in, sems_out) = rest[:n], rest[n:]
    z = place_ref[0]
    order = [c * RING + s for c in range(CHUNKS) for s in (2, 1, 3, 0)]
    inward, outward = Copies(sems_in), Copies(sems_out)
    for n in order:
        first = (lax.rem(z + n % RING, RING) * CHUNKS + n // RING) * QW
        inward.start(columns(q_ref, first, QW), qg.at[n, :, :QW])
        inward.start(columns(g_ref, first, QW), qg.at[n, :, QW:])
    w = jnp.broadcast_to(w_ref[...], (8, TOK)).T[:, 0:1]
    for i, n in enumerate(order):
        inward.started[2 * i].wait()
        inward.started[2 * i + 1].wait()
        qg[n, :, QW:] = (w * qg[n, :, QW:].astype(jnp.float32)).astype(jnp.bfloat16)
        outward.start(qg.at[n], qg_refs[n])
    outward.wait()


def pack_queries(place, weights, queries, grad_out):
    bf16 = jnp.bfloat16
    n = RING * CHUNKS
    pieces = pl.pallas_call(
        pack_queries_kernel,
        out_shape=[jax.ShapeDtypeStruct((TOK, 2 * QW), bf16)] * n,
        in_specs=[in_smem, in_vmem, in_hbm, in_hbm],
        out_specs=[in_hbm] * n,
        scratch_shapes=[
            pltpu.VMEM((n, TOK, 2 * QW), bf16),
            pltpu.SemaphoreType.DMA((2 * n,)),
            pltpu.SemaphoreType.DMA((n,)),
        ],
        compiler_params=pltpu.CompilerParams(vmem_limit_bytes=PACK_LIMIT),
        name="pack_queries",
    )(place, weights, queries, grad_out)
    return [pieces[c * RING : (c + 1) * RING] for c in range(CHUNKS)]


def starts_kernel(place_ref, *rest):
    kv_refs, (near_ref, far_ref) = rest[:RING], rest[RING : RING + 2]
    starts_ref, ids, sems = rest[RING + 2 :]
    copies = Copies(sems)
    for i, ref in enumerate(kv_refs + (near_ref,)):
        copies.start(ref.at[TOK:, 0:TOK], ids.at[i * IDS : (i + 1) * IDS, :])
    for s in range(1, RING):
        last = s * (TOK + IDS)
        i = RING + s
        copies.start(far_ref.at[last - IDS : last, 0:TOK], ids.at[i * IDS : (i + 1) * IDS, :])
    copies.wait()
    z, row = place_ref[0], place_ref[1]
    rows = ids[...].astype(jnp.float32)
    by_key = rows.T
    past = jnp.where(row > 0, by_key[:, RING * IDS :], -1.0)
    before = [by_key[:, s * IDS : s * IDS + 1] for s in range(RING)]
    before += [past[:, s * IDS : s * IDS + 1] for s in range(RING)]
    for s in range(RING):
        own = rows[s * IDS : s * IDS + 1, :]
        found = jnp.zeros((TOK, TOK), jnp.int32)
        for column in before:
            found += jnp.where(column < own, 1, 0)
        source = lax.rem(z + RING - s, RING)
        at = pl.multiple_of(source * TOK, TOK)
        starts_ref[:, pl.ds(at, TOK)] = jnp.sum(found, axis=0, keepdims=True)


def document_starts(place, kv, halo):
    return pl.pallas_call(
        starts_kernel,
        out_shape=jax.ShapeDtypeStruct((1, ROW), jnp.int32),
        in_specs=[in_smem] + [in_hbm] * (RING + 2),
        out_specs=in_vmem,
        scratch_shapes=[
            pltpu.VMEM((2 * RING * IDS, TOK), jnp.bfloat16),
            pltpu.SemaphoreType.DMA((2 * RING,)),
        ],
        compiler_params=pltpu.CompilerParams(vmem_limit_bytes=VMEM_LIMIT),
        name="document_starts",
    )(place, *kv, *halo)


def attention_kernel(chunk, place_ref, start_ref, *rest):
    kv_refs, (near_ref, far_ref) = rest[:RING], rest[RING : RING + 2]
    qg_refs, rest = rest[RING + 2 : 2 * RING + 2], rest[2 * RING + 2 :]
    prior_refs, rest = rest[: len(LATE) * chunk], rest[len(LATE) * chunk :]
    own_refs, back_refs = rest[:RING], rest[RING : 2 * RING]
    kv, kvt, qg, dkv, dq, dkv16, prior, sems_kv, sems_qg, sems_prior, sems_out = rest[2 * RING :]
    z = place_ref[0]
    scale = 1.0 / math.sqrt(WIDTH)

    inward_kv, inward_qg, inward_prior = Copies(sems_kv), Copies(sems_qg), Copies(sems_prior)
    sources = [lax.rem(z + RING - s, RING) for s in range(RING)]
    cols = slice(2 * chunk * WIDTH, 2 * (chunk + 1) * WIDTH)
    for s in range(RING):
        halo_rows = pl.ds(pl.multiple_of(PAD + sources[s] * TOK, WIDTH), TOK)
        own_rows = pl.ds(pl.multiple_of(PAD + ROW + sources[s] * TOK, WIDTH), TOK)
        halo_ref, first = (far_ref, (s - 1) * (TOK + IDS)) if s else (near_ref, 0)
        inward_kv.start(kv_refs[s].at[0:TOK, cols], kv.at[own_rows, :])
        inward_kv.start(halo_ref.at[first : first + TOK, cols], kv.at[halo_rows, :])
    for s in range(RING):
        rows = pl.ds(pl.multiple_of(sources[s] * TOK, TOK), TOK)
        inward_qg.start(qg_refs[s], qg.at[rows, :])
    for i, ref in enumerate(prior_refs):
        inward_prior.start(ref, prior.at[i])
    kv[0:PAD, :] = jnp.zeros((PAD, 2 * WIDTH), kv.dtype)
    dkv[...] = jnp.zeros(dkv.shape, dkv.dtype)
    inward_kv.wait()
    kvt[...] = kv[...].T
    inward_qg.wait()

    def tile(t, carry):
        first = pl.multiple_of(t * QT, QT)
        starts = start_ref[:, pl.ds(first, QT)]
        end = PAD + ROW + first + QT
        count = (end - PAD - jnp.min(starts) + KT - 1) // KT

        def work(windows):
            span = windows * KT
            base = pl.multiple_of(end - span, WIDTH)
            keys = pl.ds(base, span)
            rows = qg[pl.ds(first, QT), :]
            heads = [rows[:, h * WIDTH : (h + 1) * WIDTH] for h in range(2 * GROUP)]
            qs = jnp.concatenate(heads[:GROUP], axis=0)
            gs = jnp.concatenate(heads[GROUP:], axis=0)
            q_t, g_t = qs.T, gs.T
            k, v = kv[keys, :WIDTH], kv[keys, WIDTH:]
            s = jnp.dot(k, q_t, preferred_element_type=jnp.float32) * scale
            key_at = lax.broadcasted_iota(jnp.int32, (span, QT), 0) + (base - PAD)
            query_at = ROW + first + lax.broadcasted_iota(jnp.int32, (span, QT), 1)
            seen = (key_at >= starts) & (key_at <= query_at)
            s = jnp.where(jnp.concatenate([seen] * GROUP, axis=1), s, NEG)
            e = jnp.exp(s - jnp.max(s, axis=0, keepdims=True))
            p = e * (1.0 / jnp.sum(e, axis=0, keepdims=True))
            p16 = p.astype(jnp.bfloat16)
            out = jnp.dot(kvt[WIDTH:, keys], p16, preferred_element_type=jnp.float32)
            out = out.astype(jnp.bfloat16).astype(jnp.float32)
            delta = jnp.sum(g_t.astype(jnp.float32) * out, axis=0, keepdims=True)
            dp = jnp.dot(v, g_t, preferred_element_type=jnp.float32)
            ds = (p * (dp - delta) * scale).astype(jnp.bfloat16)
            dkv[keys, :WIDTH] += jnp.dot(ds, qs, preferred_element_type=jnp.float32)
            dkv[keys, WIDTH:] += jnp.dot(p16, gs, preferred_element_type=jnp.float32)
            dq_t = jnp.dot(kvt[:WIDTH, keys], ds, preferred_element_type=jnp.float32)
            for h in range(GROUP):
                dq[pl.ds(first, QT), h * WIDTH : (h + 1) * WIDTH] = (
                    dq_t[:, h * WIDTH : (h + 1) * WIDTH].T.astype(jnp.bfloat16)
                )

        for windows in range(1, WINDOWS + 1):
            pl.when(count == windows)(functools.partial(work, windows))
        return carry

    lax.fori_loop(0, TILES, tile, 0)
    outward = Copies(sems_out)
    dkv16[...] = dkv[PAD:, :].astype(jnp.bfloat16)
    for s in (2, 1, 3, 0):
        owner = lax.rem(z + s, RING)
        rows = pl.ds(pl.multiple_of(owner * TOK, TOK), TOK)
        own_rows = pl.ds(pl.multiple_of(ROW + owner * TOK, TOK), TOK)
        outward.start(dq.at[rows, :], own_refs[s].at[:, :QW])
        outward.start(dkv16.at[own_rows, :], own_refs[s].at[:, QW:])
        if chunk and s in LATE:
            outward.start(dkv16.at[rows, :], back_refs[s].at[:, 2 * WIDTH :])
        else:
            outward.start(dkv16.at[rows, :], back_refs[s])
    inward_prior.wait()
    for i, s in enumerate(LATE[: len(prior_refs)]):
        outward.start(prior.at[i], back_refs[s].at[:, : 2 * WIDTH])
    outward.wait()


def attention(chunk, place, starts, kv, halo, qg, prior):
    bf16, f32 = jnp.bfloat16, jnp.float32
    wide = [2 if chunk and s in LATE else 1 for s in range(RING)]
    results = pl.pallas_call(
        functools.partial(attention_kernel, chunk),
        out_shape=[jax.ShapeDtypeStruct((TOK, QW + 2 * WIDTH), bf16)] * RING
        + [jax.ShapeDtypeStruct((TOK, 2 * WIDTH * n), bf16) for n in wide],
        in_specs=[in_smem, in_vmem] + [in_hbm] * (2 * RING + 2 + len(prior)),
        out_specs=[in_hbm] * (2 * RING),
        scratch_shapes=[
            pltpu.VMEM((KEYS, 2 * WIDTH), bf16),
            pltpu.VMEM((2 * WIDTH, KEYS), bf16),
            pltpu.VMEM((ROW, 2 * QW), bf16),
            pltpu.VMEM((KEYS, 2 * WIDTH), f32),
            pltpu.VMEM((ROW, QW), bf16),
            pltpu.VMEM((2 * ROW, 2 * WIDTH), bf16),
            pltpu.VMEM((len(LATE), TOK, 2 * WIDTH), bf16),
            pltpu.SemaphoreType.DMA((2 * RING,)),
            pltpu.SemaphoreType.DMA((RING,)),
            pltpu.SemaphoreType.DMA((len(LATE),)),
            pltpu.SemaphoreType.DMA((3 * RING + len(LATE),)),
        ],
        compiler_params=pltpu.CompilerParams(vmem_limit_bytes=VMEM_LIMIT),
        cost_estimate=pl.CostEstimate(flops=1, bytes_accessed=1, transcendentals=0),
        name="attention",
    )(place, starts, *kv, *halo, *qg, *prior)
    return results[:RING], results[RING:]


def join_kernel(place_ref, *rest):
    n = RING * CHUNKS
    own_refs, rest = rest[:n], rest[n:]
    early_refs, late_refs = rest[: 2 * len(EARLY)], rest[2 * len(EARLY) : 2 * len(EARLY) + len(LATE)]
    dq_out, dk_out, dv_out, own, back, total, sems, sems_back, sems_out = rest[
        2 * len(EARLY) + len(LATE) :
    ]
    z = place_ref[0]
    inward, terms, outward = Copies(sems), Copies(sems_back), Copies(sems_out)
    pieces = [(c, s) for c in range(CHUNKS) for s in range(RING)]
    for i, (c, s) in enumerate(pieces):
        inward.start(own_refs[i], own.at[i])
        if s in EARLY:
            term = early_refs[c * len(EARLY) + EARLY.index(s)]
        else:
            term = late_refs[LATE.index(s)].at[:, 2 * c * WIDTH : 2 * (c + 1) * WIDTH]
        terms.start(term, back.at[i])
    for i, (c, s) in enumerate(pieces):
        head = lax.rem(z + RING - s, RING) * CHUNKS + c
        inward.started[i].wait()
        outward.start(own.at[i, :, :QW], columns(dq_out, head * QW, QW))
    for i, (c, s) in enumerate(pieces):
        head = lax.rem(z + RING - s, RING) * CHUNKS + c
        terms.started[i].wait()
        sums = own[i, :, QW:].astype(jnp.float32) + back[i].astype(jnp.float32)
        total[i] = sums.astype(total.dtype)
        outward.start(total.at[i, :, :WIDTH], columns(dk_out, head * WIDTH, WIDTH))
        outward.start(total.at[i, :, WIDTH:], columns(dv_out, head * WIDTH, WIDTH))
    outward.wait()


def join(place, own, early, late):
    heads = RING * CHUNKS
    bf16 = jnp.bfloat16
    return pl.pallas_call(
        join_kernel,
        out_shape=[
            jax.ShapeDtypeStruct((TOK, heads * QW), bf16),
            jax.ShapeDtypeStruct((TOK, heads * WIDTH), bf16),
            jax.ShapeDtypeStruct((TOK, heads * WIDTH), bf16),
        ],
        in_specs=[in_smem] + [in_hbm] * (heads + 2 * len(EARLY) + len(LATE)),
        out_specs=[in_hbm] * 3,
        scratch_shapes=[
            pltpu.VMEM((heads, TOK, QW + 2 * WIDTH), bf16),
            pltpu.VMEM((heads, TOK, 2 * WIDTH), bf16),
            pltpu.VMEM((heads, TOK, 2 * WIDTH), bf16),
            pltpu.SemaphoreType.DMA((heads,)),
            pltpu.SemaphoreType.DMA((heads,)),
            pltpu.SemaphoreType.DMA((3 * heads,)),
        ],
        compiler_params=pltpu.CompilerParams(vmem_limit_bytes=VMEM_LIMIT),
        name="join",
    )(place, *own, *early, *late)


def body(queries, keys, values, grad_out, weights, doc_ids):
    count = lax.axis_size(AXES)
    index = lax.axis_index(AXES)
    place = jnp.stack([lax.rem(index, RING), index // RING]).astype(jnp.int32)
    shifts = range(1, RING)

    def send(pieces):
        return [pieces[0]] + [shift_ring(pieces[s], s, count) for s in shifts]

    kv = pack_keys(place, keys, values, doc_ids[None, :])
    near = shift_row(kv[0], 1, 0, count)
    kv = send(kv)
    qg = pack_queries(place, weights[None, :], queries, grad_out)
    beyond, near, _ = lax.optimization_barrier((jnp.concatenate(kv[1:]), near, qg))
    halo = (near, shift_row(beyond, 1, 0, count))
    qg = [send(pieces) for pieces in qg]
    starts = document_starts(place, kv, halo)

    first_own, first_back = attention(0, place, starts, kv, halo, qg[0], ())
    owns = send(first_own)
    early = [shift_row(first_back[s], -1, s, count) for s in EARLY]
    prior = [first_back[s] for s in LATE]
    own, back = attention(1, place, starts, kv, halo, qg[1], prior)
    own, back, owns, early = lax.optimization_barrier((own, back, owns, early))
    owns += send(own)
    late = [shift_row(back[s], -1, s, count) for s in LATE]
    early += [shift_row(back[s], -1, s, count) for s in EARLY]
    return tuple(join(place, owns, early, late))


def solution(mesh):
    rows = P(("dp", "inner", "outer"), None)
    flat = P(("dp", "inner", "outer"))
    return jax.shard_map(
        body,
        mesh=mesh,
        in_specs=(rows, rows, rows, rows, flat, flat),
        out_specs=(rows, rows, rows),
        check_vma=False,
    )
```

```python
import functools
import math

import jax
import jax.numpy as jnp
from jax import lax
from jax.experimental import pallas as pl
from jax.experimental.pallas import tpu as pltpu
from jax.sharding import PartitionSpec as P

WIDTH = 128
GROUP = 3
RING = 4
TOK = 256
ROW = RING * TOK
CHUNKS = 2
QT = 256
KT = 256
QW = GROUP * WIDTH
TILES = ROW // QT
KEYS = 2 * ROW
WINDOWS = 5
IDS = 16
EARLY, LATE = (0, 2), (1, 3)
FAR_FIRST = (2, 1, 3, 0)
AXES = ("inner", "outer")
NEG = -1e30
LOG2E = 1.4426950408889634
VMEM_LIMIT = 48 * 1024 * 1024
PACK_LIMIT = 60 * 1024 * 1024

in_hbm = pl.BlockSpec(memory_space=pltpu.HBM)
in_smem = pl.BlockSpec(memory_space=pltpu.SMEM)
in_vmem = pl.BlockSpec(memory_space=pltpu.VMEM)


def far_first(pieces):
    return [pieces[s] for s in FAR_FIRST]


def in_order(refs):
    return [refs[FAR_FIRST.index(s)] for s in range(RING)]


def shift_ring(x, by, count):
    return lax.ppermute(x, AXES, [(i, i // RING * RING + (i + by) % RING) for i in range(count)])


def shift_row(x, by, ring_by, count):
    pairs = [(i, (i // RING + by) * RING + (i + ring_by) % RING) for i in range(count)]
    return lax.ppermute(x, AXES, [(i, j) for i, j in pairs if 0 <= j < count])


class Copies:
    def __init__(self, sems):
        self.sems, self.started = sems, []

    def prepare(self, source, target):
        copy = pltpu.make_async_copy(source, target, self.sems.at[len(self.started)])
        self.started.append(copy)
        return copy

    def start(self, source, target):
        self.prepare(source, target).start()

    def wait(self):
        for copy in self.started:
            copy.wait()


def columns(ref, first, width):
    return ref.at[:, pl.ds(pl.multiple_of(first, WIDTH), width)]


def pack_keys_kernel(place_ref, k_ref, v_ref, ids_ref, *rest):
    kv_refs, (kv, sems_in, sems_out) = rest[:RING], rest[RING:]
    z = place_ref[0]
    order = (2, 1, 3, 0)
    inward, outward = Copies(sems_in), Copies(sems_out)
    for s in order:
        target = lax.rem(z + s, RING)
        for c in range(CHUNKS):
            for i, ref in enumerate((k_ref, v_ref)):
                source = columns(ref, (target * CHUNKS + c) * WIDTH, WIDTH)
                rows = pl.ds(IDS + c * TOK, TOK)
                inward.start(source, kv.at[s, rows, i * WIDTH : (i + 1) * WIDTH])
    ids = ids_ref[...].astype(jnp.float32).astype(jnp.bfloat16)
    ids = jnp.concatenate([ids, jnp.zeros((IDS - 1, TOK), jnp.bfloat16)], axis=0)
    for s in range(RING):
        kv[s, 0:IDS, :] = ids
    for i, s in enumerate(order):
        for copy in inward.started[2 * CHUNKS * i : 2 * CHUNKS * (i + 1)]:
            copy.wait()
        outward.start(kv.at[s], kv_refs[s])
    outward.wait()


def pack_keys(place, keys, values, ids):
    bf16 = jnp.bfloat16
    shape = (IDS + CHUNKS * TOK, 2 * WIDTH)
    return pl.pallas_call(
        pack_keys_kernel,
        out_shape=[jax.ShapeDtypeStruct(shape, bf16)] * RING,
        in_specs=[in_smem, in_hbm, in_hbm, in_vmem],
        out_specs=[in_hbm] * RING,
        scratch_shapes=[
            pltpu.VMEM((RING,) + shape, bf16),
            pltpu.SemaphoreType.DMA((RING * 2 * CHUNKS,)),
            pltpu.SemaphoreType.DMA((RING,)),
        ],
        compiler_params=pltpu.CompilerParams(vmem_limit_bytes=PACK_LIMIT),
        name="pack_keys",
    )(place, keys, values, ids)


def pack_queries_kernel(place_ref, w_ref, q_ref, g_ref, *rest):
    n = RING * CHUNKS
    qg_refs, (qg, sems_in, sems_out) = rest[:n], rest[n:]
    z = place_ref[0]
    order = [c * RING + s for c in range(CHUNKS) for s in (2, 1, 3, 0)]
    inward, outward = Copies(sems_in), Copies(sems_out)
    for n in order:
        first = (lax.rem(z + n % RING, RING) * CHUNKS + n // RING) * QW
        inward.start(columns(q_ref, first, QW), qg.at[n, :, :QW])
        inward.start(columns(g_ref, first, QW), qg.at[n, :, QW:])
    w = jnp.broadcast_to(w_ref[...], (8, TOK)).T[:, 0:1]
    for i, n in enumerate(order):
        inward.started[2 * i].wait()
        inward.started[2 * i + 1].wait()
        qg[n, :, QW:] = (w * qg[n, :, QW:].astype(jnp.float32)).astype(jnp.bfloat16)
        outward.start(qg.at[n], qg_refs[n])
    outward.wait()


def pack_queries(place, weights, queries, grad_out):
    bf16 = jnp.bfloat16
    n = RING * CHUNKS
    pieces = pl.pallas_call(
        pack_queries_kernel,
        out_shape=[jax.ShapeDtypeStruct((TOK, 2 * QW), bf16)] * n,
        in_specs=[in_smem, in_vmem, in_hbm, in_hbm],
        out_specs=[in_hbm] * n,
        scratch_shapes=[
            pltpu.VMEM((n, TOK, 2 * QW), bf16),
            pltpu.SemaphoreType.DMA((2 * n,)),
            pltpu.SemaphoreType.DMA((n,)),
        ],
        compiler_params=pltpu.CompilerParams(vmem_limit_bytes=PACK_LIMIT),
        name="pack_queries",
    )(place, weights, queries, grad_out)
    return [pieces[c * RING : (c + 1) * RING] for c in range(CHUNKS)]


def gather_halo_kernel(*refs):
    kv_refs = in_order(refs[:RING])
    first_ref, second_ref, kv, sems_in, sems_out = refs[RING:]
    inward, outward = Copies(sems_in), Copies(sems_out)
    for s in range(RING):
        inward.start(kv_refs[s], kv.at[s])
    top = IDS + TOK
    for s in range(RING):
        inward.started[s].wait()
        outward.start(kv.at[s, 0:top, :], first_ref.at[s * top : (s + 1) * top, :])
        outward.start(kv.at[s, top:, :], second_ref.at[s * TOK : (s + 1) * TOK, :])
    outward.wait()


def gather_halo(kv):
    bf16 = jnp.bfloat16
    return pl.pallas_call(
        gather_halo_kernel,
        out_shape=[
            jax.ShapeDtypeStruct((RING * (IDS + TOK), 2 * WIDTH), bf16),
            jax.ShapeDtypeStruct((ROW, 2 * WIDTH), bf16),
        ],
        in_specs=[in_hbm] * RING,
        out_specs=[in_hbm] * 2,
        scratch_shapes=[
            pltpu.VMEM((RING, IDS + CHUNKS * TOK, 2 * WIDTH), bf16),
            pltpu.SemaphoreType.DMA((RING,)),
            pltpu.SemaphoreType.DMA((2 * RING,)),
        ],
        compiler_params=pltpu.CompilerParams(vmem_limit_bytes=VMEM_LIMIT),
        name="gather_halo",
    )(*far_first(kv))


def starts_kernel(place_ref, *rest):
    kv_refs = in_order(rest[:RING])
    halo_ref, starts_ref, ids, sems = rest[RING:]
    copies = Copies(sems)
    for i, ref in enumerate(kv_refs):
        copies.start(ref.at[0:IDS, :], ids.at[i * IDS : (i + 1) * IDS, :])
    for s in range(RING):
        first, i = s * (IDS + TOK), RING + s
        copies.start(halo_ref.at[first : first + IDS, :], ids.at[i * IDS : (i + 1) * IDS, :])
    copies.wait()
    z, row = place_ref[0], place_ref[1]
    rows = ids[...].astype(jnp.float32)
    by_key = rows.T
    past = jnp.where(row > 0, by_key[:, RING * IDS :], -1.0)
    before = [by_key[:, s * IDS : s * IDS + 1] for s in range(RING)]
    before += [past[:, s * IDS : s * IDS + 1] for s in range(RING)]
    for s in range(RING):
        own = rows[s * IDS : s * IDS + 1, :]
        found = jnp.zeros((TOK, TOK), jnp.int32)
        for column in before:
            found += jnp.where(column < own, 1, 0)
        source = lax.rem(z + RING - s, RING)
        at = pl.multiple_of(source * TOK, TOK)
        starts_ref[:, pl.ds(at, TOK)] = jnp.sum(found, axis=0, keepdims=True)


def document_starts(place, kv, halo):
    return pl.pallas_call(
        starts_kernel,
        out_shape=jax.ShapeDtypeStruct((1, ROW), jnp.int32),
        in_specs=[in_smem] + [in_hbm] * (RING + 1),
        out_specs=in_vmem,
        scratch_shapes=[
            pltpu.VMEM((2 * RING * IDS, TOK), jnp.bfloat16),
            pltpu.SemaphoreType.DMA((2 * RING,)),
        ],
        compiler_params=pltpu.CompilerParams(vmem_limit_bytes=VMEM_LIMIT),
        name="document_starts",
    )(place, *far_first(kv), halo)


def attention_kernel(chunk, place_ref, start_ref, *rest):
    kv_refs, halo_ref = in_order(rest[:RING]), rest[RING]
    qg_refs, rest = in_order(rest[RING + 1 : 2 * RING + 1]), rest[2 * RING + 1 :]
    prior_refs, rest = rest[: len(LATE) * chunk], rest[len(LATE) * chunk :]
    own_refs, back_refs = rest[:RING], rest[RING : 2 * RING]
    kv, qg, dkv, dq, dkv16, prior, sems_kv, sems_qg, sems_prior, sems_out = rest[2 * RING :]
    z = place_ref[0]
    scale = 1.0 / math.sqrt(WIDTH)

    inward_kv, inward_qg, inward_prior = Copies(sems_kv), Copies(sems_qg), Copies(sems_prior)
    sources = [lax.rem(z + RING - s, RING) for s in range(RING)]
    skip = 0 if chunk else IDS
    for s in range(RING):
        halo_rows = pl.ds(pl.multiple_of(sources[s] * TOK, WIDTH), TOK)
        own_rows = pl.ds(pl.multiple_of(ROW + sources[s] * TOK, WIDTH), TOK)
        inward_kv.start(kv_refs[s].at[pl.ds(IDS + chunk * TOK, TOK), :], kv.at[own_rows, :])
        first = s * (skip + TOK) + skip
        inward_kv.start(halo_ref.at[first : first + TOK, :], kv.at[halo_rows, :])
    for s in range(RING):
        rows = pl.ds(pl.multiple_of(sources[s] * TOK, TOK), TOK)
        inward_qg.start(qg_refs[s], qg.at[rows, :])
    for i, ref in enumerate(prior_refs):
        inward_prior.start(ref, prior.at[i])
    dkv[...] = jnp.zeros(dkv.shape, dkv.dtype)
    inward_kv.wait()

    outward = Copies(sems_out)
    dq_copies = []
    for s in range(RING):
        rows = pl.ds(pl.multiple_of(lax.rem(z + s, RING) * TOK, TOK), TOK)
        dq_copies.append(outward.prepare(dq.at[rows, :], own_refs[s].at[:, :QW]))

    def tile(i, carry):
        first = pl.multiple_of(lax.rem(z + i, RING) * QT, QT)
        for s in range(RING):
            pl.when(i == s)(inward_qg.started[(RING - s) % RING].wait)
        starts = start_ref[:, pl.ds(first, QT)]
        end = ROW + first + QT
        count = (end - jnp.min(starts) + KT - 1) // KT

        def work(windows):
            span = windows * KT
            base = pl.multiple_of(end - span, WIDTH)
            keys = pl.ds(base, span)
            rows = qg[pl.ds(first, QT), :]
            heads = [rows[:, h * WIDTH : (h + 1) * WIDTH] for h in range(2 * GROUP)]
            qs = jnp.concatenate(heads[:GROUP], axis=0)
            gs = jnp.concatenate(heads[GROUP:], axis=0)
            q_t, g_t = qs.T, gs.T
            k, v = kv[keys, :WIDTH], kv[keys, WIDTH:]
            k_t, v_t = k.T, v.T
            s = jnp.dot(k, q_t, preferred_element_type=jnp.float32)
            key_at = lax.broadcasted_iota(jnp.int32, (span, QT), 0) + base
            query_at = ROW + first + lax.broadcasted_iota(jnp.int32, (span, QT), 1)
            seen = (key_at >= starts) & (key_at <= query_at)
            s = jnp.where(jnp.concatenate([seen] * GROUP, axis=1), s, NEG)
            e = jnp.exp2((s - jnp.max(s, axis=0, keepdims=True)) * (scale * LOG2E))
            p = e * (1.0 / jnp.sum(e, axis=0, keepdims=True))
            p16 = p.astype(jnp.bfloat16)
            out = jnp.dot(v_t, p16, preferred_element_type=jnp.float32)
            out = out.astype(jnp.bfloat16).astype(jnp.float32)
            delta = jnp.sum(g_t.astype(jnp.float32) * out, axis=0, keepdims=True)
            dp = jnp.dot(v, g_t, preferred_element_type=jnp.float32)
            ds = (p * (dp - delta) * scale).astype(jnp.bfloat16)
            dkv[keys, :WIDTH] += jnp.dot(ds, qs, preferred_element_type=jnp.float32)
            dkv[keys, WIDTH:] += jnp.dot(p16, gs, preferred_element_type=jnp.float32)
            dq_t = jnp.dot(k_t, ds, preferred_element_type=jnp.float32)
            for h in range(GROUP):
                dq[pl.ds(first, QT), h * WIDTH : (h + 1) * WIDTH] = (
                    dq_t[:, h * QT : (h + 1) * QT].T.astype(jnp.bfloat16)
                )

        for windows in range(1, WINDOWS + 1):
            pl.when(count == windows)(functools.partial(work, windows))
        for s in range(RING):
            pl.when(i == s)(dq_copies[s].start)
        return carry

    lax.fori_loop(0, TILES, tile, 0)
    for s in range(RING):
        owner = lax.rem(z + s, RING)
        for part in range(2):
            rows = pl.ds(pl.multiple_of(part * ROW + owner * TOK, TOK), TOK)
            dkv16[rows, :] = dkv[rows, :].astype(jnp.bfloat16)
            if part:
                target = own_refs[s].at[:, QW:]
            elif chunk and s in LATE:
                target = back_refs[s].at[:, 2 * WIDTH :]
            else:
                target = back_refs[s]
            outward.start(dkv16.at[rows, :], target)
    inward_prior.wait()
    for i, s in enumerate(LATE[: len(prior_refs)]):
        outward.start(prior.at[i], back_refs[s].at[:, : 2 * WIDTH])
    outward.wait()


def attention(chunk, place, starts, kv, halo, qg, prior):
    bf16, f32 = jnp.bfloat16, jnp.float32
    wide = [2 if chunk and s in LATE else 1 for s in range(RING)]
    results = pl.pallas_call(
        functools.partial(attention_kernel, chunk),
        out_shape=[jax.ShapeDtypeStruct((TOK, QW + 2 * WIDTH), bf16)] * RING
        + [jax.ShapeDtypeStruct((TOK, 2 * WIDTH * n), bf16) for n in wide],
        in_specs=[in_smem, in_vmem] + [in_hbm] * (2 * RING + 1 + len(prior)),
        out_specs=[in_hbm] * (2 * RING),
        scratch_shapes=[
            pltpu.VMEM((KEYS, 2 * WIDTH), bf16),
            pltpu.VMEM((ROW, 2 * QW), bf16),
            pltpu.VMEM((KEYS, 2 * WIDTH), f32),
            pltpu.VMEM((ROW, QW), bf16),
            pltpu.VMEM((2 * ROW, 2 * WIDTH), bf16),
            pltpu.VMEM((len(LATE), TOK, 2 * WIDTH), bf16),
            pltpu.SemaphoreType.DMA((2 * RING,)),
            pltpu.SemaphoreType.DMA((RING,)),
            pltpu.SemaphoreType.DMA((len(LATE),)),
            pltpu.SemaphoreType.DMA((3 * RING + len(LATE),)),
        ],
        compiler_params=pltpu.CompilerParams(vmem_limit_bytes=VMEM_LIMIT),
        cost_estimate=pl.CostEstimate(flops=1, bytes_accessed=1, transcendentals=0),
        name="attention",
    )(place, starts, *far_first(kv), halo, *far_first(qg), *prior)
    return results[:RING], results[RING:]


def join_first_kernel(place_ref, *rest):
    own_refs = in_order(rest[:RING])
    dq_out, own, sems, sems_out = rest[RING:]
    z = place_ref[0]
    inward, outward = Copies(sems), Copies(sems_out)
    for s in range(RING):
        inward.start(own_refs[s].at[:, :QW], own.at[s])
    for s in range(RING):
        head = lax.rem(z + RING - s, RING) * CHUNKS
        inward.started[s].wait()
        outward.start(own.at[s], columns(dq_out, head * QW, QW))
    outward.wait()


def join_first(place, own):
    return pl.pallas_call(
        join_first_kernel,
        out_shape=jax.ShapeDtypeStruct((TOK, RING * CHUNKS * QW), jnp.bfloat16),
        in_specs=[in_smem] + [in_hbm] * RING,
        out_specs=in_hbm,
        scratch_shapes=[
            pltpu.VMEM((RING, TOK, QW), jnp.bfloat16),
            pltpu.SemaphoreType.DMA((RING,)),
            pltpu.SemaphoreType.DMA((RING,)),
        ],
        compiler_params=pltpu.CompilerParams(vmem_limit_bytes=VMEM_LIMIT),
        name="join_first",
    )(place, *far_first(own))


def join_kernel(place_ref, begun_ref, *rest):
    n = RING * CHUNKS
    own_refs, rest = in_order(rest[:RING]) + in_order(rest[RING:n]), rest[n:]
    early_refs, late_refs = rest[: 2 * len(EARLY)], rest[2 * len(EARLY) : 2 * len(EARLY) + len(LATE)]
    dq_out, dk_out, dv_out, own, dq, back, total, sems, sems_dq, sems_back, sems_out = rest[
        2 * len(EARLY) + len(LATE) :
    ]
    z = place_ref[0]
    copies = [Copies(x) for x in (sems, sems_dq, sems_back, sems_out)]
    inward, inward_dq, terms, outward = copies
    pieces = [(c, s) for c in range(CHUNKS) for s in range(RING)]
    for s in range(RING):
        inward_dq.start(own_refs[RING + s].at[:, :QW], dq.at[s])
    for i, (c, s) in enumerate(pieces):
        inward.start(own_refs[i].at[:, QW:], own.at[i])
        if s in EARLY:
            term = early_refs[c * len(EARLY) + EARLY.index(s)]
        else:
            term = late_refs[LATE.index(s)].at[:, 2 * c * WIDTH : 2 * (c + 1) * WIDTH]
        terms.start(term, back.at[i])
    for s in range(RING):
        head = lax.rem(z + RING - s, RING) * CHUNKS + 1
        inward_dq.started[s].wait()
        outward.start(dq.at[s], columns(dq_out, head * QW, QW))
    for i, (c, s) in enumerate(pieces):
        head = lax.rem(z + RING - s, RING) * CHUNKS + c
        inward.started[i].wait()
        terms.started[i].wait()
        sums = own[i].astype(jnp.float32) + back[i].astype(jnp.float32)
        total[i] = sums.astype(total.dtype)
        outward.start(total.at[i, :, :WIDTH], columns(dk_out, head * WIDTH, WIDTH))
        outward.start(total.at[i, :, WIDTH:], columns(dv_out, head * WIDTH, WIDTH))
    outward.wait()


def join(place, begun, own, early, late):
    heads = RING * CHUNKS
    bf16 = jnp.bfloat16
    return pl.pallas_call(
        join_kernel,
        out_shape=[
            jax.ShapeDtypeStruct((TOK, heads * QW), bf16),
            jax.ShapeDtypeStruct((TOK, heads * WIDTH), bf16),
            jax.ShapeDtypeStruct((TOK, heads * WIDTH), bf16),
        ],
        in_specs=[in_smem] + [in_hbm] * (1 + heads + 2 * len(EARLY) + len(LATE)),
        out_specs=[in_hbm] * 3,
        input_output_aliases={1: 0},
        scratch_shapes=[
            pltpu.VMEM((heads, TOK, 2 * WIDTH), bf16),
            pltpu.VMEM((RING, TOK, QW), bf16),
            pltpu.VMEM((heads, TOK, 2 * WIDTH), bf16),
            pltpu.VMEM((heads, TOK, 2 * WIDTH), bf16),
            pltpu.SemaphoreType.DMA((heads,)),
            pltpu.SemaphoreType.DMA((RING,)),
            pltpu.SemaphoreType.DMA((heads,)),
            pltpu.SemaphoreType.DMA((RING + 2 * heads,)),
        ],
        compiler_params=pltpu.CompilerParams(vmem_limit_bytes=VMEM_LIMIT),
        name="join",
    )(place, begun, *far_first(own[:RING]), *far_first(own[RING:]), *early, *late)


def body(queries, keys, values, grad_out, weights, doc_ids):
    count = lax.axis_size(AXES)
    index = lax.axis_index(AXES)
    place = jnp.stack([lax.rem(index, RING), index // RING]).astype(jnp.int32)

    def send(pieces):
        sent = {s: shift_ring(pieces[s], s, count) for s in (2, 1, 3)}
        return [pieces[0]] + [sent[s] for s in range(1, RING)]

    kv = pack_keys(place, keys, values, doc_ids[None, :])
    kv = send(kv)
    qg = pack_queries(place, weights[None, :], queries, grad_out)
    two_hops = shift_ring(qg[0][2], 2, count)
    gathered, (now, next_) = lax.optimization_barrier((gather_halo(kv), qg))
    halo = [shift_row(gathered[0], 1, 0, count)]
    now = [now[0], shift_ring(now[1], 1, count), two_hops, shift_ring(now[3], 3, count)]
    halo.append(shift_row(gathered[1], 1, 0, count))
    now, next_ = lax.optimization_barrier((now, next_))
    qg = [now, send(next_)]
    starts = document_starts(place, kv, halo[0])

    first_own, first_back = attention(0, place, starts, kv, halo[0], qg[0], ())
    owns = send(first_own)
    early = [shift_row(first_back[s], -1, s, count) for s in EARLY]
    prior = [first_back[s] for s in LATE]
    own, back = attention(1, place, starts, kv, halo[1], qg[1], prior)
    own, back, owns, early = lax.optimization_barrier((own, back, owns, early))
    begun = join_first(place, owns)
    late = [shift_row(back[s], -1, s, count) for s in LATE]
    owns += send(own)
    *rest, late = lax.optimization_barrier((*[back[s] for s in EARLY], late))
    early += [shift_row(piece, -1, s, count) for piece, s in zip(rest, EARLY)]
    return tuple(join(place, begun, owns, early, late))


def solution(mesh):
    rows = P(("dp", "inner", "outer"), None)
    flat = P(("dp", "inner", "outer"))
    return jax.shard_map(
        body,
        mesh=mesh,
        in_specs=(rows, rows, rows, rows, flat, flat),
        out_specs=(rows, rows, rows),
        check_vma=False,
    )
```

```python
import functools
import math

import jax
import jax.numpy as jnp
from jax import lax
from jax.experimental import pallas as pl
from jax.experimental.pallas import tpu as pltpu
from jax.sharding import PartitionSpec as P

WIDTH = 128
GROUP = 3
RING = 4
TOK = 256
ROW = RING * TOK
CHUNKS = 2
QT = 256
KT = 128
QW = GROUP * WIDTH
TILES = ROW // QT
KEYS = 2 * ROW
WINDOWS = (2, 3, 4, 5, 7, 10)
IDS = 16
EARLY, LATE = (0, 2), (1, 3)
FAR_FIRST = (2, 1, 3, 0)
AXES = ("inner", "outer")
NEG = -1e30
LOG2E = 1.4426950408889634
VMEM_LIMIT = 48 * 1024 * 1024
PACK_LIMIT = 60 * 1024 * 1024

in_hbm = pl.BlockSpec(memory_space=pltpu.HBM)
in_vmem = pl.BlockSpec(memory_space=pltpu.VMEM)


def my_place():
    index = lax.axis_index(AXES)
    return lax.rem(index, RING), index // RING


def far_first(pieces):
    return [pieces[s] for s in FAR_FIRST]


def in_order(refs):
    return [refs[FAR_FIRST.index(s)] for s in range(RING)]


def shift_ring(x, by, count):
    return lax.ppermute(x, AXES, [(i, i // RING * RING + (i + by) % RING) for i in range(count)])


def shift_row(x, by, ring_by, count):
    pairs = [(i, (i // RING + by) * RING + (i + ring_by) % RING) for i in range(count)]
    return lax.ppermute(x, AXES, [(i, j) for i, j in pairs if 0 <= j < count])


class Copies:
    def __init__(self, sems):
        self.sems, self.started = sems, []

    def prepare(self, source, target):
        copy = pltpu.make_async_copy(source, target, self.sems.at[len(self.started)])
        self.started.append(copy)
        return copy

    def start(self, source, target):
        self.prepare(source, target).start()

    def wait(self):
        for copy in self.started:
            copy.wait()


def columns(ref, first, width):
    return ref.at[:, pl.ds(pl.multiple_of(first, WIDTH), width)]


def pack_keys_kernel(k_ref, v_ref, ids_ref, *rest):
    kv_refs, (kv, sems_in, sems_out) = rest[:RING], rest[RING:]
    z, _ = my_place()
    order = (2, 1, 3, 0)
    inward, outward = Copies(sems_in), Copies(sems_out)
    for s in order:
        target = lax.rem(z + s, RING)
        for c in range(CHUNKS):
            for i, ref in enumerate((k_ref, v_ref)):
                source = columns(ref, (target * CHUNKS + c) * WIDTH, WIDTH)
                rows = pl.ds(IDS + c * TOK, TOK)
                inward.start(source, kv.at[s, rows, i * WIDTH : (i + 1) * WIDTH])
    ids = ids_ref[...].astype(jnp.float32).astype(jnp.bfloat16)
    ids = jnp.concatenate([ids, jnp.zeros((IDS - 1, TOK), jnp.bfloat16)], axis=0)
    for s in range(RING):
        kv[s, 0:IDS, :] = ids
    for i, s in enumerate(order):
        for copy in inward.started[2 * CHUNKS * i : 2 * CHUNKS * (i + 1)]:
            copy.wait()
        outward.start(kv.at[s], kv_refs[s])
    outward.wait()


def pack_keys(keys, values, ids):
    bf16 = jnp.bfloat16
    shape = (IDS + CHUNKS * TOK, 2 * WIDTH)
    return pl.pallas_call(
        pack_keys_kernel,
        out_shape=[jax.ShapeDtypeStruct(shape, bf16)] * RING,
        in_specs=[in_hbm, in_hbm, in_vmem],
        out_specs=[in_hbm] * RING,
        scratch_shapes=[
            pltpu.VMEM((RING,) + shape, bf16),
            pltpu.SemaphoreType.DMA((RING * 2 * CHUNKS,)),
            pltpu.SemaphoreType.DMA((RING,)),
        ],
        compiler_params=pltpu.CompilerParams(vmem_limit_bytes=PACK_LIMIT),
        name="pack_keys",
    )(keys, values, ids)


def pack_queries_kernel(w_ref, q_ref, g_ref, *rest):
    n = RING * CHUNKS
    qg_refs, (qg, sems_in, sems_out) = rest[:n], rest[n:]
    z, _ = my_place()
    order = [c * RING + s for c in range(CHUNKS) for s in (2, 1, 3, 0)]
    inward, outward = Copies(sems_in), Copies(sems_out)
    for n in order:
        first = (lax.rem(z + n % RING, RING) * CHUNKS + n // RING) * QW
        inward.start(columns(q_ref, first, QW), qg.at[n, :, :QW])
        inward.start(columns(g_ref, first, QW), qg.at[n, :, QW:])
    w = jnp.broadcast_to(w_ref[...], (8, TOK)).T[:, 0:1]
    for i, n in enumerate(order):
        inward.started[2 * i].wait()
        inward.started[2 * i + 1].wait()
        qg[n, :, QW:] = (w * qg[n, :, QW:].astype(jnp.float32)).astype(jnp.bfloat16)
        outward.start(qg.at[n], qg_refs[n])
    outward.wait()


def pack_queries(weights, queries, grad_out):
    bf16 = jnp.bfloat16
    n = RING * CHUNKS
    pieces = pl.pallas_call(
        pack_queries_kernel,
        out_shape=[jax.ShapeDtypeStruct((TOK, 2 * QW), bf16)] * n,
        in_specs=[in_vmem, in_hbm, in_hbm],
        out_specs=[in_hbm] * n,
        scratch_shapes=[
            pltpu.VMEM((n, TOK, 2 * QW), bf16),
            pltpu.SemaphoreType.DMA((2 * n,)),
            pltpu.SemaphoreType.DMA((n,)),
        ],
        compiler_params=pltpu.CompilerParams(vmem_limit_bytes=PACK_LIMIT),
        name="pack_queries",
    )(weights, queries, grad_out)
    return [pieces[c * RING : (c + 1) * RING] for c in range(CHUNKS)]


def gather_halo_kernel(*refs):
    kv_refs = in_order(refs[:RING])
    first_ref, second_ref, kv, sems_in, sems_out = refs[RING:]
    inward, outward = Copies(sems_in), Copies(sems_out)
    for s in range(RING):
        inward.start(kv_refs[s], kv.at[s])
    top = IDS + TOK
    for s in range(RING):
        inward.started[s].wait()
        outward.start(kv.at[s, 0:top, :], first_ref.at[s * top : (s + 1) * top, :])
        outward.start(kv.at[s, top:, :], second_ref.at[s * TOK : (s + 1) * TOK, :])
    outward.wait()


def gather_halo(kv):
    bf16 = jnp.bfloat16
    return pl.pallas_call(
        gather_halo_kernel,
        out_shape=[
            jax.ShapeDtypeStruct((RING * (IDS + TOK), 2 * WIDTH), bf16),
            jax.ShapeDtypeStruct((ROW, 2 * WIDTH), bf16),
        ],
        in_specs=[in_hbm] * RING,
        out_specs=[in_hbm] * 2,
        scratch_shapes=[
            pltpu.VMEM((RING, IDS + CHUNKS * TOK, 2 * WIDTH), bf16),
            pltpu.SemaphoreType.DMA((RING,)),
            pltpu.SemaphoreType.DMA((2 * RING,)),
        ],
        compiler_params=pltpu.CompilerParams(vmem_limit_bytes=VMEM_LIMIT),
        name="gather_halo",
    )(*far_first(kv))


def starts_kernel(*rest):
    kv_refs = in_order(rest[:RING])
    halo_ref, starts_ref, ids, sems = rest[RING:]
    copies = Copies(sems)
    for i, ref in enumerate(kv_refs):
        copies.start(ref.at[0:IDS, :], ids.at[i * IDS : (i + 1) * IDS, :])
    for s in range(RING):
        first, i = s * (IDS + TOK), RING + s
        copies.start(halo_ref.at[first : first + IDS, :], ids.at[i * IDS : (i + 1) * IDS, :])
    copies.wait()
    z, row = my_place()
    rows = ids[...].astype(jnp.float32)
    by_key = rows.T
    past = jnp.where(row > 0, by_key[:, RING * IDS :], -1.0)
    before = [by_key[:, s * IDS : s * IDS + 1] for s in range(RING)]
    before += [past[:, s * IDS : s * IDS + 1] for s in range(RING)]
    for s in range(RING):
        own = rows[s * IDS : s * IDS + 1, :]
        found = jnp.zeros((TOK, TOK), jnp.int32)
        for column in before:
            found += jnp.where(column < own, 1, 0)
        source = lax.rem(z + RING - s, RING)
        at = pl.multiple_of(source * TOK, TOK)
        starts_ref[:, pl.ds(at, TOK)] = jnp.sum(found, axis=0, keepdims=True)


def document_starts(kv, halo):
    return pl.pallas_call(
        starts_kernel,
        out_shape=jax.ShapeDtypeStruct((1, ROW), jnp.int32),
        in_specs=[in_hbm] * (RING + 1),
        out_specs=in_vmem,
        scratch_shapes=[
            pltpu.VMEM((2 * RING * IDS, TOK), jnp.bfloat16),
            pltpu.SemaphoreType.DMA((2 * RING,)),
        ],
        compiler_params=pltpu.CompilerParams(vmem_limit_bytes=VMEM_LIMIT),
        name="document_starts",
    )(*far_first(kv), halo)


def attention_kernel(chunk, start_ref, *rest):
    kv_refs, halo_ref = in_order(rest[:RING]), rest[RING]
    qg_refs, rest = in_order(rest[RING + 1 : 2 * RING + 1]), rest[2 * RING + 1 :]
    prior_refs, rest = rest[: len(LATE) * chunk], rest[len(LATE) * chunk :]
    own_refs, back_refs = rest[:RING], rest[RING : 2 * RING]
    kv, qg, dkv, dq, dkv16, prior, sems_kv, sems_qg, sems_prior, sems_out = rest[2 * RING :]
    z, _ = my_place()
    scale = 1.0 / math.sqrt(WIDTH)

    inward_kv, inward_qg, inward_prior = Copies(sems_kv), Copies(sems_qg), Copies(sems_prior)
    sources = [lax.rem(z + RING - s, RING) for s in range(RING)]
    skip = 0 if chunk else IDS
    for s in range(RING):
        halo_rows = pl.ds(pl.multiple_of(sources[s] * TOK, WIDTH), TOK)
        own_rows = pl.ds(pl.multiple_of(ROW + sources[s] * TOK, WIDTH), TOK)
        inward_kv.start(kv_refs[s].at[pl.ds(IDS + chunk * TOK, TOK), :], kv.at[own_rows, :])
        first = s * (skip + TOK) + skip
        inward_kv.start(halo_ref.at[first : first + TOK, :], kv.at[halo_rows, :])
    for s in range(RING):
        rows = pl.ds(pl.multiple_of(sources[s] * TOK, TOK), TOK)
        inward_qg.start(qg_refs[s], qg.at[rows, :])
    for i, ref in enumerate(prior_refs):
        inward_prior.start(ref, prior.at[i])
    dkv[...] = jnp.zeros(dkv.shape, dkv.dtype)
    inward_kv.wait()

    outward = Copies(sems_out)
    dq_copies = []
    for s in range(RING):
        rows = pl.ds(pl.multiple_of(lax.rem(z + s, RING) * TOK, TOK), TOK)
        dq_copies.append(outward.prepare(dq.at[rows, :], own_refs[s].at[:, :QW]))

    def tile(i, carry):
        first = pl.multiple_of(lax.rem(z + i, RING) * QT, QT)
        for s in range(RING):
            pl.when(i == s)(inward_qg.started[(RING - s) % RING].wait)
        starts = start_ref[:, pl.ds(first, QT)]
        end = ROW + first + QT
        count = (end - jnp.min(starts) + KT - 1) // KT

        def work(windows):
            span = windows * KT
            base = pl.multiple_of(end - span, WIDTH)
            keys = pl.ds(base, span)
            rows = qg[pl.ds(first, QT), :]
            heads = [rows[:, h * WIDTH : (h + 1) * WIDTH] for h in range(2 * GROUP)]
            qs = jnp.concatenate(heads[:GROUP], axis=0)
            gs = jnp.concatenate(heads[GROUP:], axis=0)
            q_t, g_t = qs.T, gs.T
            k, v = kv[keys, :WIDTH], kv[keys, WIDTH:]
            k_t, v_t = k.T, v.T
            s = jnp.dot(k, q_t, preferred_element_type=jnp.float32)
            key_at = lax.broadcasted_iota(jnp.int32, (span, QT), 0) + base
            query_at = ROW + first + lax.broadcasted_iota(jnp.int32, (span, QT), 1)
            seen = (key_at >= starts) & (key_at <= query_at)
            s = jnp.where(jnp.concatenate([seen] * GROUP, axis=1), s, NEG)
            e = jnp.exp2((s - jnp.max(s, axis=0, keepdims=True)) * (scale * LOG2E))
            p = e * (1.0 / jnp.sum(e, axis=0, keepdims=True))
            p16 = p.astype(jnp.bfloat16)
            out = jnp.dot(v_t, p16, preferred_element_type=jnp.float32)
            out = out.astype(jnp.bfloat16).astype(jnp.float32)
            delta = jnp.sum(g_t.astype(jnp.float32) * out, axis=0, keepdims=True)
            dp = jnp.dot(v, g_t, preferred_element_type=jnp.float32)
            ds = (p * (dp - delta) * scale).astype(jnp.bfloat16)
            dkv[keys, :WIDTH] += jnp.dot(ds, qs, preferred_element_type=jnp.float32)
            dkv[keys, WIDTH:] += jnp.dot(p16, gs, preferred_element_type=jnp.float32)
            dq_t = jnp.dot(k_t, ds, preferred_element_type=jnp.float32)
            for h in range(GROUP):
                dq[pl.ds(first, QT), h * WIDTH : (h + 1) * WIDTH] = (
                    dq_t[:, h * QT : (h + 1) * QT].T.astype(jnp.bfloat16)
                )

        for fewer, windows in zip((0,) + WINDOWS, WINDOWS):
            pl.when((count > fewer) & (count <= windows))(functools.partial(work, windows))
        for s in range(RING):
            pl.when(i == s)(dq_copies[s].start)
        return carry

    lax.fori_loop(0, TILES, tile, 0)
    for s in range(RING):
        owner = lax.rem(z + s, RING)
        for part in range(2):
            rows = pl.ds(pl.multiple_of(part * ROW + owner * TOK, TOK), TOK)
            dkv16[rows, :] = dkv[rows, :].astype(jnp.bfloat16)
            if part:
                target = own_refs[s].at[:, QW:]
            elif chunk and s in LATE:
                target = back_refs[s].at[:, 2 * WIDTH :]
            else:
                target = back_refs[s]
            outward.start(dkv16.at[rows, :], target)
    inward_prior.wait()
    for i, s in enumerate(LATE[: len(prior_refs)]):
        outward.start(prior.at[i], back_refs[s].at[:, : 2 * WIDTH])
    outward.wait()


def attention(chunk, starts, kv, halo, qg, prior):
    bf16, f32 = jnp.bfloat16, jnp.float32
    wide = [2 if chunk and s in LATE else 1 for s in range(RING)]
    results = pl.pallas_call(
        functools.partial(attention_kernel, chunk),
        out_shape=[jax.ShapeDtypeStruct((TOK, QW + 2 * WIDTH), bf16)] * RING
        + [jax.ShapeDtypeStruct((TOK, 2 * WIDTH * n), bf16) for n in wide],
        in_specs=[in_vmem] + [in_hbm] * (2 * RING + 1 + len(prior)),
        out_specs=[in_hbm] * (2 * RING),
        scratch_shapes=[
            pltpu.VMEM((KEYS, 2 * WIDTH), bf16),
            pltpu.VMEM((ROW, 2 * QW), bf16),
            pltpu.VMEM((KEYS, 2 * WIDTH), f32),
            pltpu.VMEM((ROW, QW), bf16),
            pltpu.VMEM((2 * ROW, 2 * WIDTH), bf16),
            pltpu.VMEM((len(LATE), TOK, 2 * WIDTH), bf16),
            pltpu.SemaphoreType.DMA((2 * RING,)),
            pltpu.SemaphoreType.DMA((RING,)),
            pltpu.SemaphoreType.DMA((len(LATE),)),
            pltpu.SemaphoreType.DMA((3 * RING + len(LATE),)),
        ],
        compiler_params=pltpu.CompilerParams(vmem_limit_bytes=VMEM_LIMIT),
        cost_estimate=pl.CostEstimate(flops=1, bytes_accessed=1, transcendentals=0),
        name="attention",
    )(starts, *far_first(kv), halo, *far_first(qg), *prior)
    return results[:RING], results[RING:]


def join_first_kernel(*rest):
    own_refs = in_order(rest[:RING])
    dq_out, own, sems, sems_out = rest[RING:]
    z, _ = my_place()
    inward, outward = Copies(sems), Copies(sems_out)
    for s in range(RING):
        inward.start(own_refs[s].at[:, :QW], own.at[s])
    for s in range(RING):
        head = lax.rem(z + RING - s, RING) * CHUNKS
        inward.started[s].wait()
        outward.start(own.at[s], columns(dq_out, head * QW, QW))
    outward.wait()


def join_first(own):
    return pl.pallas_call(
        join_first_kernel,
        out_shape=jax.ShapeDtypeStruct((TOK, RING * CHUNKS * QW), jnp.bfloat16),
        in_specs=[in_hbm] * RING,
        out_specs=in_hbm,
        scratch_shapes=[
            pltpu.VMEM((RING, TOK, QW), jnp.bfloat16),
            pltpu.SemaphoreType.DMA((RING,)),
            pltpu.SemaphoreType.DMA((RING,)),
        ],
        compiler_params=pltpu.CompilerParams(vmem_limit_bytes=VMEM_LIMIT),
        name="join_first",
    )(*far_first(own))


def join_kernel(begun_ref, *rest):
    n = RING * CHUNKS
    own_refs, rest = in_order(rest[:RING]) + in_order(rest[RING:n]), rest[n:]
    early_refs, late_refs = rest[: 2 * len(EARLY)], rest[2 * len(EARLY) : 2 * len(EARLY) + len(LATE)]
    dq_out, dk_out, dv_out, own, dq, back, total, sems, sems_dq, sems_back, sems_out = rest[
        2 * len(EARLY) + len(LATE) :
    ]
    z, _ = my_place()
    copies = [Copies(x) for x in (sems, sems_dq, sems_back, sems_out)]
    inward, inward_dq, terms, outward = copies
    pieces = [(c, s) for c in range(CHUNKS) for s in range(RING)]
    for s in range(RING):
        inward_dq.start(own_refs[RING + s].at[:, :QW], dq.at[s])
    for i, (c, s) in enumerate(pieces):
        inward.start(own_refs[i].at[:, QW:], own.at[i])
        if s in EARLY:
            term = early_refs[c * len(EARLY) + EARLY.index(s)]
        else:
            term = late_refs[LATE.index(s)].at[:, 2 * c * WIDTH : 2 * (c + 1) * WIDTH]
        terms.start(term, back.at[i])
    for s in range(RING):
        head = lax.rem(z + RING - s, RING) * CHUNKS + 1
        inward_dq.started[s].wait()
        outward.start(dq.at[s], columns(dq_out, head * QW, QW))
    for i, (c, s) in enumerate(pieces):
        head = lax.rem(z + RING - s, RING) * CHUNKS + c
        inward.started[i].wait()
        terms.started[i].wait()
        sums = own[i].astype(jnp.float32) + back[i].astype(jnp.float32)
        total[i] = sums.astype(total.dtype)
        outward.start(total.at[i, :, :WIDTH], columns(dk_out, head * WIDTH, WIDTH))
        outward.start(total.at[i, :, WIDTH:], columns(dv_out, head * WIDTH, WIDTH))
    outward.wait()


def join(begun, own, early, late):
    heads = RING * CHUNKS
    bf16 = jnp.bfloat16
    return pl.pallas_call(
        join_kernel,
        out_shape=[
            jax.ShapeDtypeStruct((TOK, heads * QW), bf16),
            jax.ShapeDtypeStruct((TOK, heads * WIDTH), bf16),
            jax.ShapeDtypeStruct((TOK, heads * WIDTH), bf16),
        ],
        in_specs=[in_hbm] * (1 + heads + 2 * len(EARLY) + len(LATE)),
        out_specs=[in_hbm] * 3,
        input_output_aliases={0: 0},
        scratch_shapes=[
            pltpu.VMEM((heads, TOK, 2 * WIDTH), bf16),
            pltpu.VMEM((RING, TOK, QW), bf16),
            pltpu.VMEM((heads, TOK, 2 * WIDTH), bf16),
            pltpu.VMEM((heads, TOK, 2 * WIDTH), bf16),
            pltpu.SemaphoreType.DMA((heads,)),
            pltpu.SemaphoreType.DMA((RING,)),
            pltpu.SemaphoreType.DMA((heads,)),
            pltpu.SemaphoreType.DMA((RING + 2 * heads,)),
        ],
        compiler_params=pltpu.CompilerParams(vmem_limit_bytes=VMEM_LIMIT),
        name="join",
    )(begun, *far_first(own[:RING]), *far_first(own[RING:]), *early, *late)


def body(queries, keys, values, grad_out, weights, doc_ids):
    count = lax.axis_size(AXES)

    def send(pieces):
        sent = {s: shift_ring(pieces[s], s, count) for s in (2, 1, 3)}
        return [pieces[0]] + [sent[s] for s in range(1, RING)]

    kv = pack_keys(keys, values, doc_ids[None, :])
    kv = send(kv)
    qg = pack_queries(weights[None, :], queries, grad_out)
    two_hops = shift_ring(qg[0][2], 2, count)
    gathered, (now, next_) = lax.optimization_barrier((gather_halo(kv), qg))
    halo = [shift_row(gathered[0], 1, 0, count)]
    now = [now[0], shift_ring(now[1], 1, count), two_hops, shift_ring(now[3], 3, count)]
    halo.append(shift_row(gathered[1], 1, 0, count))
    now, next_ = lax.optimization_barrier((now, next_))
    qg = [now, send(next_)]
    starts = document_starts(kv, halo[0])

    first_own, first_back = attention(0, starts, kv, halo[0], qg[0], ())
    owns = send(first_own)
    early = [shift_row(first_back[s], -1, s, count) for s in EARLY]
    prior = [first_back[s] for s in LATE]
    own, back = attention(1, starts, kv, halo[1], qg[1], prior)
    own, back, owns, early = lax.optimization_barrier((own, back, owns, early))
    begun = join_first(owns)
    owns += send(own)
    late = [shift_row(back[s], -1, s, count) for s in LATE]
    *rest, owns[RING + 2] = lax.optimization_barrier((*[back[s] for s in EARLY], owns[RING + 2]))
    early += [shift_row(piece, -1, s, count) for piece, s in zip(rest, EARLY)]
    return tuple(join(begun, owns, early, late))


def solution(mesh):
    rows = P(("dp", "inner", "outer"), None)
    flat = P(("dp", "inner", "outer"))
    return jax.shard_map(
        body,
        mesh=mesh,
        in_specs=(rows, rows, rows, rows, flat, flat),
        out_specs=(rows, rows, rows),
        check_vma=False,
    )
```

```python
import functools
import math

import jax
import jax.numpy as jnp
from jax import lax
from jax.experimental import pallas as pl
from jax.experimental.pallas import tpu as pltpu
from jax.sharding import PartitionSpec as P

WIDTH = 128
GROUP = 3
RING = 4
TOK = 256
ROW = RING * TOK
CHUNKS = 2
QT = 256
KT = 128
QW = GROUP * WIDTH
TILES = ROW // QT
KEYS = 2 * ROW
WINDOWS = (2, 3, 4, 5, 7, 10)
IDS = 16
EARLY, LATE = (), (0, 1, 2, 3)
FAR_FIRST = (2, 1, 3, 0)
AXES = ("inner", "outer")
NEG = -1e30
LOG2E = 1.4426950408889634
VMEM_LIMIT = 48 * 1024 * 1024
PACK_LIMIT = 60 * 1024 * 1024

in_hbm = pl.BlockSpec(memory_space=pltpu.HBM)
in_vmem = pl.BlockSpec(memory_space=pltpu.VMEM)


def my_place():
    index = lax.axis_index(AXES)
    return lax.rem(index, RING), index // RING


def far_first(pieces):
    return [pieces[s] for s in FAR_FIRST]


def in_order(refs):
    return [refs[FAR_FIRST.index(s)] for s in range(RING)]


def shift_ring(x, by, count):
    return lax.ppermute(x, AXES, [(i, i // RING * RING + (i + by) % RING) for i in range(count)])


def shift_row(x, by, ring_by, count):
    pairs = [(i, (i // RING + by) * RING + (i + ring_by) % RING) for i in range(count)]
    return lax.ppermute(x, AXES, [(i, j) for i, j in pairs if 0 <= j < count])


class Copies:
    def __init__(self, sems):
        self.sems, self.started = sems, []

    def prepare(self, source, target):
        copy = pltpu.make_async_copy(source, target, self.sems.at[len(self.started)])
        self.started.append(copy)
        return copy

    def start(self, source, target):
        self.prepare(source, target).start()

    def wait(self):
        for copy in self.started:
            copy.wait()


def columns(ref, first, width):
    return ref.at[:, pl.ds(pl.multiple_of(first, WIDTH), width)]


def pack_keys_kernel(k_ref, v_ref, ids_ref, *rest):
    kv_refs, (kv, sems_in, sems_out) = rest[:RING], rest[RING:]
    z, _ = my_place()
    order = (2, 1, 3, 0)
    inward, outward = Copies(sems_in), Copies(sems_out)
    for s in order:
        target = lax.rem(z + s, RING)
        for c in range(CHUNKS):
            for i, ref in enumerate((k_ref, v_ref)):
                source = columns(ref, (target * CHUNKS + c) * WIDTH, WIDTH)
                rows = pl.ds(IDS + c * TOK, TOK)
                inward.start(source, kv.at[s, rows, i * WIDTH : (i + 1) * WIDTH])
    ids = ids_ref[...].astype(jnp.float32).astype(jnp.bfloat16)
    ids = jnp.concatenate([ids, jnp.zeros((IDS - 1, TOK), jnp.bfloat16)], axis=0)
    for s in range(RING):
        kv[s, 0:IDS, :] = ids
    for i, s in enumerate(order):
        for copy in inward.started[2 * CHUNKS * i : 2 * CHUNKS * (i + 1)]:
            copy.wait()
        outward.start(kv.at[s], kv_refs[s])
    outward.wait()


def pack_keys(keys, values, ids):
    bf16 = jnp.bfloat16
    shape = (IDS + CHUNKS * TOK, 2 * WIDTH)
    return pl.pallas_call(
        pack_keys_kernel,
        out_shape=[jax.ShapeDtypeStruct(shape, bf16)] * RING,
        in_specs=[in_hbm, in_hbm, in_vmem],
        out_specs=[in_hbm] * RING,
        scratch_shapes=[
            pltpu.VMEM((RING,) + shape, bf16),
            pltpu.SemaphoreType.DMA((RING * 2 * CHUNKS,)),
            pltpu.SemaphoreType.DMA((RING,)),
        ],
        compiler_params=pltpu.CompilerParams(vmem_limit_bytes=PACK_LIMIT),
        name="pack_keys",
    )(keys, values, ids)


def pack_queries_kernel(w_ref, q_ref, g_ref, *rest):
    n = RING * CHUNKS
    qg_refs, (qg, sems_in, sems_out) = rest[:n], rest[n:]
    z, _ = my_place()
    order = [c * RING + s for c in range(CHUNKS) for s in (2, 1, 3, 0)]
    inward, outward = Copies(sems_in), Copies(sems_out)
    for n in order:
        first = (lax.rem(z + n % RING, RING) * CHUNKS + n // RING) * QW
        inward.start(columns(q_ref, first, QW), qg.at[n, :, :QW])
        inward.start(columns(g_ref, first, QW), qg.at[n, :, QW:])
    w = jnp.broadcast_to(w_ref[...], (8, TOK)).T[:, 0:1]
    for i, n in enumerate(order):
        inward.started[2 * i].wait()
        inward.started[2 * i + 1].wait()
        qg[n, :, QW:] = (w * qg[n, :, QW:].astype(jnp.float32)).astype(jnp.bfloat16)
        outward.start(qg.at[n], qg_refs[n])
    outward.wait()


def pack_queries(weights, queries, grad_out):
    bf16 = jnp.bfloat16
    n = RING * CHUNKS
    pieces = pl.pallas_call(
        pack_queries_kernel,
        out_shape=[jax.ShapeDtypeStruct((TOK, 2 * QW), bf16)] * n,
        in_specs=[in_vmem, in_hbm, in_hbm],
        out_specs=[in_hbm] * n,
        scratch_shapes=[
            pltpu.VMEM((n, TOK, 2 * QW), bf16),
            pltpu.SemaphoreType.DMA((2 * n,)),
            pltpu.SemaphoreType.DMA((n,)),
        ],
        compiler_params=pltpu.CompilerParams(vmem_limit_bytes=PACK_LIMIT),
        name="pack_queries",
    )(weights, queries, grad_out)
    return [pieces[c * RING : (c + 1) * RING] for c in range(CHUNKS)]


def gather_halo_kernel(*refs):
    kv_refs = in_order(refs[:RING])
    first_ref, second_ref, kv, sems_in, sems_out = refs[RING:]
    inward, outward = Copies(sems_in), Copies(sems_out)
    for s in range(RING):
        inward.start(kv_refs[s], kv.at[s])
    top = IDS + TOK
    for s in range(RING):
        inward.started[s].wait()
        outward.start(kv.at[s, 0:top, :], first_ref.at[s * top : (s + 1) * top, :])
        outward.start(kv.at[s, top:, :], second_ref.at[s * TOK : (s + 1) * TOK, :])
    outward.wait()


def gather_halo(kv):
    bf16 = jnp.bfloat16
    return pl.pallas_call(
        gather_halo_kernel,
        out_shape=[
            jax.ShapeDtypeStruct((RING * (IDS + TOK), 2 * WIDTH), bf16),
            jax.ShapeDtypeStruct((ROW, 2 * WIDTH), bf16),
        ],
        in_specs=[in_hbm] * RING,
        out_specs=[in_hbm] * 2,
        scratch_shapes=[
            pltpu.VMEM((RING, IDS + CHUNKS * TOK, 2 * WIDTH), bf16),
            pltpu.SemaphoreType.DMA((RING,)),
            pltpu.SemaphoreType.DMA((2 * RING,)),
        ],
        compiler_params=pltpu.CompilerParams(vmem_limit_bytes=VMEM_LIMIT),
        name="gather_halo",
    )(*far_first(kv))


def starts_kernel(*rest):
    kv_refs = in_order(rest[:RING])
    halo_ref, starts_ref, ids, sems = rest[RING:]
    copies = Copies(sems)
    for i, ref in enumerate(kv_refs):
        copies.start(ref.at[0:IDS, :], ids.at[i * IDS : (i + 1) * IDS, :])
    for s in range(RING):
        first, i = s * (IDS + TOK), RING + s
        copies.start(halo_ref.at[first : first + IDS, :], ids.at[i * IDS : (i + 1) * IDS, :])
    copies.wait()
    z, row = my_place()
    rows = ids[...].astype(jnp.float32)
    by_key = rows.T
    past = jnp.where(row > 0, by_key[:, RING * IDS :], -1.0)
    before = [by_key[:, s * IDS : s * IDS + 1] for s in range(RING)]
    before += [past[:, s * IDS : s * IDS + 1] for s in range(RING)]
    for s in range(RING):
        own = rows[s * IDS : s * IDS + 1, :]
        found = jnp.zeros((TOK, TOK), jnp.int32)
        for column in before:
            found += jnp.where(column < own, 1, 0)
        source = lax.rem(z + RING - s, RING)
        at = pl.multiple_of(source * TOK, TOK)
        starts_ref[:, pl.ds(at, TOK)] = jnp.sum(found, axis=0, keepdims=True)


def document_starts(kv, halo):
    return pl.pallas_call(
        starts_kernel,
        out_shape=jax.ShapeDtypeStruct((1, ROW), jnp.int32),
        in_specs=[in_hbm] * (RING + 1),
        out_specs=in_vmem,
        scratch_shapes=[
            pltpu.VMEM((2 * RING * IDS, TOK), jnp.bfloat16),
            pltpu.SemaphoreType.DMA((2 * RING,)),
        ],
        compiler_params=pltpu.CompilerParams(vmem_limit_bytes=VMEM_LIMIT),
        name="document_starts",
    )(*far_first(kv), halo)


def attention_kernel(chunk, start_ref, *rest):
    kv_refs, halo_ref = in_order(rest[:RING]), rest[RING]
    qg_refs, rest = in_order(rest[RING + 1 : 2 * RING + 1]), rest[2 * RING + 1 :]
    prior_refs, rest = rest[: len(LATE) * chunk], rest[len(LATE) * chunk :]
    own_refs, back_refs = rest[:RING], rest[RING : 2 * RING]
    kv, qg, dkv, dq, dkv16, prior, sems_kv, sems_qg, sems_prior, sems_out = rest[2 * RING :]
    z, _ = my_place()
    scale = 1.0 / math.sqrt(WIDTH)

    inward_kv, inward_qg, inward_prior = Copies(sems_kv), Copies(sems_qg), Copies(sems_prior)
    sources = [lax.rem(z + RING - s, RING) for s in range(RING)]
    skip = 0 if chunk else IDS
    for s in range(RING):
        halo_rows = pl.ds(pl.multiple_of(sources[s] * TOK, WIDTH), TOK)
        own_rows = pl.ds(pl.multiple_of(ROW + sources[s] * TOK, WIDTH), TOK)
        inward_kv.start(kv_refs[s].at[pl.ds(IDS + chunk * TOK, TOK), :], kv.at[own_rows, :])
        first = s * (skip + TOK) + skip
        inward_kv.start(halo_ref.at[first : first + TOK, :], kv.at[halo_rows, :])
    for s in range(RING):
        rows = pl.ds(pl.multiple_of(sources[s] * TOK, TOK), TOK)
        inward_qg.start(qg_refs[s], qg.at[rows, :])
    for i, ref in enumerate(prior_refs):
        inward_prior.start(ref, prior.at[i])
    dkv[...] = jnp.zeros(dkv.shape, dkv.dtype)
    inward_kv.wait()

    outward = Copies(sems_out)
    dq_copies = []
    for s in range(RING):
        rows = pl.ds(pl.multiple_of(lax.rem(z + s, RING) * TOK, TOK), TOK)
        dq_copies.append(outward.prepare(dq.at[rows, :], own_refs[s].at[:, :QW]))

    def tile(i, carry):
        first = pl.multiple_of(lax.rem(z + i, RING) * QT, QT)
        for s in range(RING):
            pl.when(i == s)(inward_qg.started[(RING - s) % RING].wait)
        starts = start_ref[:, pl.ds(first, QT)]
        end = ROW + first + QT
        count = (end - jnp.min(starts) + KT - 1) // KT

        def work(windows):
            span = windows * KT
            base = pl.multiple_of(end - span, WIDTH)
            keys = pl.ds(base, span)
            rows = qg[pl.ds(first, QT), :]
            heads = [rows[:, h * WIDTH : (h + 1) * WIDTH] for h in range(2 * GROUP)]
            qs = jnp.concatenate(heads[:GROUP], axis=0)
            gs = jnp.concatenate(heads[GROUP:], axis=0)
            q_t, g_t = qs.T, gs.T
            k, v = kv[keys, :WIDTH], kv[keys, WIDTH:]
            k_t, v_t = k.T, v.T
            s = jnp.dot(k, q_t, preferred_element_type=jnp.float32)
            key_at = lax.broadcasted_iota(jnp.int32, (span, QT), 0) + base
            query_at = ROW + first + lax.broadcasted_iota(jnp.int32, (span, QT), 1)
            seen = (key_at >= starts) & (key_at <= query_at)
            s = jnp.where(jnp.concatenate([seen] * GROUP, axis=1), s, NEG)
            e = jnp.exp2((s - jnp.max(s, axis=0, keepdims=True)) * (scale * LOG2E))
            p = e * (1.0 / jnp.sum(e, axis=0, keepdims=True))
            p16 = p.astype(jnp.bfloat16)
            out = jnp.dot(v_t, p16, preferred_element_type=jnp.float32)
            out = out.astype(jnp.bfloat16).astype(jnp.float32)
            delta = jnp.sum(g_t.astype(jnp.float32) * out, axis=0, keepdims=True)
            dp = jnp.dot(v, g_t, preferred_element_type=jnp.float32)
            ds = (p * (dp - delta) * scale).astype(jnp.bfloat16)
            dkv[keys, :WIDTH] += jnp.dot(ds, qs, preferred_element_type=jnp.float32)
            dkv[keys, WIDTH:] += jnp.dot(p16, gs, preferred_element_type=jnp.float32)
            dq_t = jnp.dot(k_t, ds, preferred_element_type=jnp.float32)
            for h in range(GROUP):
                dq[pl.ds(first, QT), h * WIDTH : (h + 1) * WIDTH] = (
                    dq_t[:, h * QT : (h + 1) * QT].T.astype(jnp.bfloat16)
                )

        for fewer, windows in zip((0,) + WINDOWS, WINDOWS):
            pl.when((count > fewer) & (count <= windows))(functools.partial(work, windows))
        for s in range(RING):
            pl.when(i == s)(dq_copies[s].start)
        return carry

    lax.fori_loop(0, TILES, tile, 0)
    for s in range(RING):
        owner = lax.rem(z + s, RING)
        for part in range(2):
            rows = pl.ds(pl.multiple_of(part * ROW + owner * TOK, TOK), TOK)
            dkv16[rows, :] = dkv[rows, :].astype(jnp.bfloat16)
            if part:
                target = own_refs[s].at[:, QW:]
            elif chunk and s in LATE:
                target = back_refs[s].at[:, 2 * WIDTH :]
            else:
                target = back_refs[s]
            outward.start(dkv16.at[rows, :], target)
    inward_prior.wait()
    for i, s in enumerate(LATE[: len(prior_refs)]):
        outward.start(prior.at[i], back_refs[s].at[:, : 2 * WIDTH])
    outward.wait()


def attention(chunk, starts, kv, halo, qg, prior):
    bf16, f32 = jnp.bfloat16, jnp.float32
    wide = [2 if chunk and s in LATE else 1 for s in range(RING)]
    results = pl.pallas_call(
        functools.partial(attention_kernel, chunk),
        out_shape=[jax.ShapeDtypeStruct((TOK, QW + 2 * WIDTH), bf16)] * RING
        + [jax.ShapeDtypeStruct((TOK, 2 * WIDTH * n), bf16) for n in wide],
        in_specs=[in_vmem] + [in_hbm] * (2 * RING + 1 + len(prior)),
        out_specs=[in_hbm] * (2 * RING),
        scratch_shapes=[
            pltpu.VMEM((KEYS, 2 * WIDTH), bf16),
            pltpu.VMEM((ROW, 2 * QW), bf16),
            pltpu.VMEM((KEYS, 2 * WIDTH), f32),
            pltpu.VMEM((ROW, QW), bf16),
            pltpu.VMEM((2 * ROW, 2 * WIDTH), bf16),
            pltpu.VMEM((len(LATE), TOK, 2 * WIDTH), bf16),
            pltpu.SemaphoreType.DMA((2 * RING,)),
            pltpu.SemaphoreType.DMA((RING,)),
            pltpu.SemaphoreType.DMA((len(LATE),)),
            pltpu.SemaphoreType.DMA((3 * RING + len(LATE),)),
        ],
        compiler_params=pltpu.CompilerParams(vmem_limit_bytes=VMEM_LIMIT),
        cost_estimate=pl.CostEstimate(flops=1, bytes_accessed=1, transcendentals=0),
        name="attention",
    )(starts, *far_first(kv), halo, *far_first(qg), *prior)
    return results[:RING], results[RING:]


def join_first_kernel(*rest):
    own_refs = in_order(rest[:RING])
    dq_out, own, sems, sems_out = rest[RING:]
    z, _ = my_place()
    inward, outward = Copies(sems), Copies(sems_out)
    for s in range(RING):
        inward.start(own_refs[s].at[:, :QW], own.at[s])
    for s in range(RING):
        head = lax.rem(z + RING - s, RING) * CHUNKS
        inward.started[s].wait()
        outward.start(own.at[s], columns(dq_out, head * QW, QW))
    outward.wait()


def join_first(own):
    return pl.pallas_call(
        join_first_kernel,
        out_shape=jax.ShapeDtypeStruct((TOK, RING * CHUNKS * QW), jnp.bfloat16),
        in_specs=[in_hbm] * RING,
        out_specs=in_hbm,
        scratch_shapes=[
            pltpu.VMEM((RING, TOK, QW), jnp.bfloat16),
            pltpu.SemaphoreType.DMA((RING,)),
            pltpu.SemaphoreType.DMA((RING,)),
        ],
        compiler_params=pltpu.CompilerParams(vmem_limit_bytes=VMEM_LIMIT),
        name="join_first",
    )(*far_first(own))


def join_kernel(begun_ref, *rest):
    n = RING * CHUNKS
    own_refs, rest = in_order(rest[:RING]) + in_order(rest[RING:n]), rest[n:]
    early_refs, late_refs = rest[: 2 * len(EARLY)], rest[2 * len(EARLY) : 2 * len(EARLY) + len(LATE)]
    dq_out, dk_out, dv_out, own, dq, back, total, sems, sems_dq, sems_back, sems_out = rest[
        2 * len(EARLY) + len(LATE) :
    ]
    z, _ = my_place()
    copies = [Copies(x) for x in (sems, sems_dq, sems_back, sems_out)]
    inward, inward_dq, terms, outward = copies
    pieces = [(c, s) for c in range(CHUNKS) for s in range(RING)]
    for s in range(RING):
        inward_dq.start(own_refs[RING + s].at[:, :QW], dq.at[s])
    for i, (c, s) in enumerate(pieces):
        inward.start(own_refs[i].at[:, QW:], own.at[i])
        if s in EARLY:
            term = early_refs[c * len(EARLY) + EARLY.index(s)]
        else:
            term = late_refs[LATE.index(s)].at[:, 2 * c * WIDTH : 2 * (c + 1) * WIDTH]
        terms.start(term, back.at[i])
    for s in range(RING):
        head = lax.rem(z + RING - s, RING) * CHUNKS + 1
        inward_dq.started[s].wait()
        outward.start(dq.at[s], columns(dq_out, head * QW, QW))
    for i, (c, s) in enumerate(pieces):
        head = lax.rem(z + RING - s, RING) * CHUNKS + c
        inward.started[i].wait()
        terms.started[i].wait()
        sums = own[i].astype(jnp.float32) + back[i].astype(jnp.float32)
        total[i] = sums.astype(total.dtype)
        outward.start(total.at[i, :, :WIDTH], columns(dk_out, head * WIDTH, WIDTH))
        outward.start(total.at[i, :, WIDTH:], columns(dv_out, head * WIDTH, WIDTH))
    outward.wait()


def join(begun, own, early, late):
    heads = RING * CHUNKS
    bf16 = jnp.bfloat16
    return pl.pallas_call(
        join_kernel,
        out_shape=[
            jax.ShapeDtypeStruct((TOK, heads * QW), bf16),
            jax.ShapeDtypeStruct((TOK, heads * WIDTH), bf16),
            jax.ShapeDtypeStruct((TOK, heads * WIDTH), bf16),
        ],
        in_specs=[in_hbm] * (1 + heads + 2 * len(EARLY) + len(LATE)),
        out_specs=[in_hbm] * 3,
        input_output_aliases={0: 0},
        scratch_shapes=[
            pltpu.VMEM((heads, TOK, 2 * WIDTH), bf16),
            pltpu.VMEM((RING, TOK, QW), bf16),
            pltpu.VMEM((heads, TOK, 2 * WIDTH), bf16),
            pltpu.VMEM((heads, TOK, 2 * WIDTH), bf16),
            pltpu.SemaphoreType.DMA((heads,)),
            pltpu.SemaphoreType.DMA((RING,)),
            pltpu.SemaphoreType.DMA((heads,)),
            pltpu.SemaphoreType.DMA((RING + 2 * heads,)),
        ],
        compiler_params=pltpu.CompilerParams(vmem_limit_bytes=VMEM_LIMIT),
        name="join",
    )(begun, *far_first(own[:RING]), *far_first(own[RING:]), *early, *late)


def body(queries, keys, values, grad_out, weights, doc_ids):
    count = lax.axis_size(AXES)

    def send(pieces):
        sent = {s: shift_ring(pieces[s], s, count) for s in (2, 1, 3)}
        return [pieces[0]] + [sent[s] for s in range(1, RING)]

    kv = pack_keys(keys, values, doc_ids[None, :])
    kv = send(kv)
    qg = pack_queries(weights[None, :], queries, grad_out)
    two_hops = shift_ring(qg[0][2], 2, count)
    gathered, (now, next_) = lax.optimization_barrier((gather_halo(kv), qg))
    halo = [shift_row(gathered[0], 1, 0, count)]
    now = [now[0], shift_ring(now[1], 1, count), two_hops, shift_ring(now[3], 3, count)]
    halo.append(shift_row(gathered[1], 1, 0, count))
    now, next_ = lax.optimization_barrier((now, next_))
    qg = [now, send(next_)]
    starts = document_starts(kv, halo[0])

    first_own, first_back = attention(0, starts, kv, halo[0], qg[0], ())
    owns = send(first_own)
    early = [shift_row(first_back[s], -1, s, count) for s in EARLY]
    prior = [first_back[s] for s in LATE]
    own, back = attention(1, starts, kv, halo[1], qg[1], prior)
    own, back, owns, early = lax.optimization_barrier((own, back, owns, early))
    begun = join_first(owns)
    owns += send(own)
    first, last = (1, 3), (0, 2)
    late = {s: shift_row(back[s], -1, s, count) for s in first}
    *rest, owns[RING + 2] = lax.optimization_barrier((*[back[s] for s in last], owns[RING + 2]))
    late.update({s: shift_row(piece, -1, s, count) for piece, s in zip(rest, last)})
    late = [late[s] for s in LATE]
    return tuple(join(begun, owns, early, late))


def solution(mesh):
    rows = P(("dp", "inner", "outer"), None)
    flat = P(("dp", "inner", "outer"))
    return jax.shard_map(
        body,
        mesh=mesh,
        in_specs=(rows, rows, rows, rows, flat, flat),
        out_specs=(rows, rows, rows),
        check_vma=False,
    )
```

```python
import functools
import math

import jax
import jax.numpy as jnp
from jax import lax
from jax.experimental import pallas as pl
from jax.experimental.pallas import tpu as pltpu
from jax.sharding import PartitionSpec as P

WIDTH = 128
GROUP = 3
RING = 4
TOK = 256
ROW = RING * TOK
CHUNKS = 2
QT = 256
KT = 128
QW = GROUP * WIDTH
TILES = ROW // QT
KEYS = 2 * ROW
WINDOWS = (2, 3, 4, 5, 7, 10)
IDS = 16
EARLY, LATE = (), (0, 1, 2, 3)
FAR_FIRST = (2, 1, 3, 0)
AXES = ("inner", "outer")
NEG = -1e30
LOG2E = 1.4426950408889634
VMEM_LIMIT = 48 * 1024 * 1024
PACK_LIMIT = 60 * 1024 * 1024

in_hbm = pl.BlockSpec(memory_space=pltpu.HBM)
in_vmem = pl.BlockSpec(memory_space=pltpu.VMEM)


def my_place():
    index = lax.axis_index(AXES)
    return lax.rem(index, RING), index // RING


def far_first(pieces):
    return [pieces[s] for s in FAR_FIRST]


def in_order(refs):
    return [refs[FAR_FIRST.index(s)] for s in range(RING)]


def shift_ring(x, by, count):
    return lax.ppermute(x, AXES, [(i, i // RING * RING + (i + by) % RING) for i in range(count)])


def shift_row(x, by, ring_by, count):
    pairs = [(i, (i // RING + by) * RING + (i + ring_by) % RING) for i in range(count)]
    return lax.ppermute(x, AXES, [(i, j) for i, j in pairs if 0 <= j < count])


class Copies:
    def __init__(self, sems):
        self.sems, self.started = sems, []

    def prepare(self, source, target):
        copy = pltpu.make_async_copy(source, target, self.sems.at[len(self.started)])
        self.started.append(copy)
        return copy

    def start(self, source, target):
        self.prepare(source, target).start()

    def wait(self):
        for copy in self.started:
            copy.wait()


def columns(ref, first, width):
    return ref.at[:, pl.ds(pl.multiple_of(first, WIDTH), width)]


def pack_keys_kernel(k_ref, v_ref, ids_ref, *rest):
    kv_refs, (kv, sems_in, sems_out) = rest[:RING], rest[RING:]
    z, _ = my_place()
    order = (2, 1, 3, 0)
    inward, outward = Copies(sems_in), Copies(sems_out)
    for s in order:
        target = lax.rem(z + s, RING)
        for c in range(CHUNKS):
            for i, ref in enumerate((k_ref, v_ref)):
                source = columns(ref, (target * CHUNKS + c) * WIDTH, WIDTH)
                rows = pl.ds(IDS + c * TOK, TOK)
                inward.start(source, kv.at[s, rows, i * WIDTH : (i + 1) * WIDTH])
    ids = ids_ref[...].astype(jnp.float32).astype(jnp.bfloat16)
    ids = jnp.concatenate([ids, jnp.zeros((IDS - 1, TOK), jnp.bfloat16)], axis=0)
    for s in range(RING):
        kv[s, 0:IDS, :] = ids
    for i, s in enumerate(order):
        for copy in inward.started[2 * CHUNKS * i : 2 * CHUNKS * (i + 1)]:
            copy.wait()
        outward.start(kv.at[s], kv_refs[s])
    outward.wait()


def pack_keys(keys, values, ids):
    bf16 = jnp.bfloat16
    shape = (IDS + CHUNKS * TOK, 2 * WIDTH)
    return pl.pallas_call(
        pack_keys_kernel,
        out_shape=[jax.ShapeDtypeStruct(shape, bf16)] * RING,
        in_specs=[in_hbm, in_hbm, in_vmem],
        out_specs=[in_hbm] * RING,
        scratch_shapes=[
            pltpu.VMEM((RING,) + shape, bf16),
            pltpu.SemaphoreType.DMA((RING * 2 * CHUNKS,)),
            pltpu.SemaphoreType.DMA((RING,)),
        ],
        compiler_params=pltpu.CompilerParams(vmem_limit_bytes=PACK_LIMIT),
        name="pack_keys",
    )(keys, values, ids)


def pack_queries_kernel(w_ref, q_ref, g_ref, *rest):
    n = RING * CHUNKS
    qg_refs, (qg, sems_in, sems_out) = rest[:n], rest[n:]
    z, _ = my_place()
    order = [c * RING + s for c in range(CHUNKS) for s in (2, 1, 3, 0)]
    inward, outward = Copies(sems_in), Copies(sems_out)
    for n in order:
        first = (lax.rem(z + n % RING, RING) * CHUNKS + n // RING) * QW
        inward.start(columns(q_ref, first, QW), qg.at[n, :, :QW])
        inward.start(columns(g_ref, first, QW), qg.at[n, :, QW:])
    w = jnp.broadcast_to(w_ref[...], (8, TOK)).T[:, 0:1]
    for i, n in enumerate(order):
        inward.started[2 * i].wait()
        inward.started[2 * i + 1].wait()
        qg[n, :, QW:] = (w * qg[n, :, QW:].astype(jnp.float32)).astype(jnp.bfloat16)
        outward.start(qg.at[n], qg_refs[n])
    outward.wait()


def pack_queries(weights, queries, grad_out):
    bf16 = jnp.bfloat16
    n = RING * CHUNKS
    pieces = pl.pallas_call(
        pack_queries_kernel,
        out_shape=[jax.ShapeDtypeStruct((TOK, 2 * QW), bf16)] * n,
        in_specs=[in_vmem, in_hbm, in_hbm],
        out_specs=[in_hbm] * n,
        scratch_shapes=[
            pltpu.VMEM((n, TOK, 2 * QW), bf16),
            pltpu.SemaphoreType.DMA((2 * n,)),
            pltpu.SemaphoreType.DMA((n,)),
        ],
        compiler_params=pltpu.CompilerParams(vmem_limit_bytes=PACK_LIMIT),
        name="pack_queries",
    )(weights, queries, grad_out)
    return [pieces[c * RING : (c + 1) * RING] for c in range(CHUNKS)]


def gather_halo_kernel(*refs):
    kv_refs = in_order(refs[:RING])
    first_ref, second_ref, kv, sems_in, sems_out = refs[RING:]
    inward, outward = Copies(sems_in), Copies(sems_out)
    for s in range(RING):
        inward.start(kv_refs[s], kv.at[s])
    top = IDS + TOK
    for s in range(RING):
        inward.started[s].wait()
        outward.start(kv.at[s, 0:top, :], first_ref.at[s * top : (s + 1) * top, :])
        outward.start(kv.at[s, top:, :], second_ref.at[s * TOK : (s + 1) * TOK, :])
    outward.wait()


def gather_halo(kv):
    bf16 = jnp.bfloat16
    return pl.pallas_call(
        gather_halo_kernel,
        out_shape=[
            jax.ShapeDtypeStruct((RING * (IDS + TOK), 2 * WIDTH), bf16),
            jax.ShapeDtypeStruct((ROW, 2 * WIDTH), bf16),
        ],
        in_specs=[in_hbm] * RING,
        out_specs=[in_hbm] * 2,
        scratch_shapes=[
            pltpu.VMEM((RING, IDS + CHUNKS * TOK, 2 * WIDTH), bf16),
            pltpu.SemaphoreType.DMA((RING,)),
            pltpu.SemaphoreType.DMA((2 * RING,)),
        ],
        compiler_params=pltpu.CompilerParams(vmem_limit_bytes=VMEM_LIMIT),
        name="gather_halo",
    )(*far_first(kv))


def starts_kernel(*rest):
    kv_refs = in_order(rest[:RING])
    halo_ref, starts_ref, ids, sems = rest[RING:]
    copies = Copies(sems)
    for i, ref in enumerate(kv_refs):
        copies.start(ref.at[0:IDS, :], ids.at[i * IDS : (i + 1) * IDS, :])
    for s in range(RING):
        first, i = s * (IDS + TOK), RING + s
        copies.start(halo_ref.at[first : first + IDS, :], ids.at[i * IDS : (i + 1) * IDS, :])
    copies.wait()
    z, row = my_place()
    rows = ids[...].astype(jnp.float32)
    by_key = rows.T
    past = jnp.where(row > 0, by_key[:, RING * IDS :], -1.0)
    before = [by_key[:, s * IDS : s * IDS + 1] for s in range(RING)]
    before += [past[:, s * IDS : s * IDS + 1] for s in range(RING)]
    for s in range(RING):
        own = rows[s * IDS : s * IDS + 1, :]
        found = jnp.zeros((TOK, TOK), jnp.int32)
        for column in before:
            found += jnp.where(column < own, 1, 0)
        source = lax.rem(z + RING - s, RING)
        at = pl.multiple_of(source * TOK, TOK)
        starts_ref[:, pl.ds(at, TOK)] = jnp.sum(found, axis=0, keepdims=True)


def document_starts(kv, halo):
    return pl.pallas_call(
        starts_kernel,
        out_shape=jax.ShapeDtypeStruct((1, ROW), jnp.int32),
        in_specs=[in_hbm] * (RING + 1),
        out_specs=in_vmem,
        scratch_shapes=[
            pltpu.VMEM((2 * RING * IDS, TOK), jnp.bfloat16),
            pltpu.SemaphoreType.DMA((2 * RING,)),
        ],
        compiler_params=pltpu.CompilerParams(vmem_limit_bytes=VMEM_LIMIT),
        name="document_starts",
    )(*far_first(kv), halo)


def attention_kernel(chunk, start_ref, *rest):
    kv_refs, halo_ref = in_order(rest[:RING]), rest[RING]
    qg_refs, rest = in_order(rest[RING + 1 : 2 * RING + 1]), rest[2 * RING + 1 :]
    prior_refs, rest = rest[: len(LATE) * chunk], rest[len(LATE) * chunk :]
    own_refs, back_refs = rest[:RING], rest[RING : 2 * RING]
    kv, qg, dkv, dq, dkv16, prior, sems_kv, sems_qg, sems_prior, sems_out = rest[2 * RING :]
    z, _ = my_place()
    scale = 1.0 / math.sqrt(WIDTH)

    inward_kv, inward_qg, inward_prior = Copies(sems_kv), Copies(sems_qg), Copies(sems_prior)
    sources = [lax.rem(z + RING - s, RING) for s in range(RING)]
    skip = 0 if chunk else IDS
    for s in range(RING):
        halo_rows = pl.ds(pl.multiple_of(sources[s] * TOK, WIDTH), TOK)
        own_rows = pl.ds(pl.multiple_of(ROW + sources[s] * TOK, WIDTH), TOK)
        inward_kv.start(kv_refs[s].at[pl.ds(IDS + chunk * TOK, TOK), :], kv.at[own_rows, :])
        first = s * (skip + TOK) + skip
        inward_kv.start(halo_ref.at[first : first + TOK, :], kv.at[halo_rows, :])
    for s in range(RING):
        rows = pl.ds(pl.multiple_of(sources[s] * TOK, TOK), TOK)
        inward_qg.start(qg_refs[s], qg.at[rows, :])
    for i, ref in enumerate(prior_refs):
        inward_prior.start(ref, prior.at[i])
    dkv[...] = jnp.zeros(dkv.shape, dkv.dtype)
    inward_kv.wait()

    outward = Copies(sems_out)
    dq_copies = []
    for s in range(RING):
        rows = pl.ds(pl.multiple_of(lax.rem(z + s, RING) * TOK, TOK), TOK)
        dq_copies.append(outward.prepare(dq.at[rows, :], own_refs[s].at[:, :QW]))

    def tile(i, carry):
        first = pl.multiple_of(lax.rem(z + i, RING) * QT, QT)
        for s in range(RING):
            pl.when(i == s)(inward_qg.started[(RING - s) % RING].wait)
        starts = start_ref[:, pl.ds(first, QT)]
        end = ROW + first + QT
        count = (end - jnp.min(starts) + KT - 1) // KT

        def work(windows):
            span = windows * KT
            base = pl.multiple_of(end - span, WIDTH)
            keys = pl.ds(base, span)
            rows = qg[pl.ds(first, QT), :]
            heads = [rows[:, h * WIDTH : (h + 1) * WIDTH] for h in range(2 * GROUP)]
            qs = jnp.concatenate(heads[:GROUP], axis=0)
            gs = jnp.concatenate(heads[GROUP:], axis=0)
            q_t, g_t = qs.T, gs.T
            k, v = kv[keys, :WIDTH], kv[keys, WIDTH:]
            k_t, v_t = k.T, v.T
            s = jnp.dot(k, q_t, preferred_element_type=jnp.float32)
            key_at = lax.broadcasted_iota(jnp.int32, (span, QT), 0) + base
            query_at = ROW + first + lax.broadcasted_iota(jnp.int32, (span, QT), 1)
            seen = (key_at >= starts) & (key_at <= query_at)
            s = jnp.where(jnp.concatenate([seen] * GROUP, axis=1), s, NEG)
            e = jnp.exp2((s - jnp.max(s, axis=0, keepdims=True)) * (scale * LOG2E))
            p = e * (1.0 / jnp.sum(e, axis=0, keepdims=True))
            p16 = p.astype(jnp.bfloat16)
            out = jnp.dot(v_t, p16, preferred_element_type=jnp.float32)
            out = out.astype(jnp.bfloat16).astype(jnp.float32)
            delta = jnp.sum(g_t.astype(jnp.float32) * out, axis=0, keepdims=True)
            dp = jnp.dot(v, g_t, preferred_element_type=jnp.float32)
            ds = (p * (dp - delta) * scale).astype(jnp.bfloat16)
            dkv[keys, :WIDTH] += jnp.dot(ds, qs, preferred_element_type=jnp.float32)
            dkv[keys, WIDTH:] += jnp.dot(p16, gs, preferred_element_type=jnp.float32)
            dq_t = jnp.dot(k_t, ds, preferred_element_type=jnp.float32)
            for h in range(GROUP):
                dq[pl.ds(first, QT), h * WIDTH : (h + 1) * WIDTH] = (
                    dq_t[:, h * QT : (h + 1) * QT].T.astype(jnp.bfloat16)
                )

        for fewer, windows in zip((0,) + WINDOWS, WINDOWS):
            pl.when((count > fewer) & (count <= windows))(functools.partial(work, windows))
        for s in range(RING):
            pl.when(i == s)(dq_copies[s].start)
        return carry

    lax.fori_loop(0, TILES, tile, 0)
    for s in range(RING):
        owner = lax.rem(z + s, RING)
        for part in range(2):
            rows = pl.ds(pl.multiple_of(part * ROW + owner * TOK, TOK), TOK)
            dkv16[rows, :] = dkv[rows, :].astype(jnp.bfloat16)
            if part:
                target = own_refs[s].at[:, QW:]
            elif chunk and s in LATE:
                target = back_refs[s].at[:, 2 * WIDTH :]
            else:
                target = back_refs[s]
            outward.start(dkv16.at[rows, :], target)
    inward_prior.wait()
    for i, s in enumerate(LATE[: len(prior_refs)]):
        outward.start(prior.at[i], back_refs[s].at[:, : 2 * WIDTH])
    outward.wait()


def attention(chunk, starts, kv, halo, qg, prior):
    bf16, f32 = jnp.bfloat16, jnp.float32
    wide = [2 if chunk and s in LATE else 1 for s in range(RING)]
    results = pl.pallas_call(
        functools.partial(attention_kernel, chunk),
        out_shape=[jax.ShapeDtypeStruct((TOK, QW + 2 * WIDTH), bf16)] * RING
        + [jax.ShapeDtypeStruct((TOK, 2 * WIDTH * n), bf16) for n in wide],
        in_specs=[in_vmem] + [in_hbm] * (2 * RING + 1 + len(prior)),
        out_specs=[in_hbm] * (2 * RING),
        scratch_shapes=[
            pltpu.VMEM((KEYS, 2 * WIDTH), bf16),
            pltpu.VMEM((ROW, 2 * QW), bf16),
            pltpu.VMEM((KEYS, 2 * WIDTH), f32),
            pltpu.VMEM((ROW, QW), bf16),
            pltpu.VMEM((2 * ROW, 2 * WIDTH), bf16),
            pltpu.VMEM((len(LATE), TOK, 2 * WIDTH), bf16),
            pltpu.SemaphoreType.DMA((2 * RING,)),
            pltpu.SemaphoreType.DMA((RING,)),
            pltpu.SemaphoreType.DMA((len(LATE),)),
            pltpu.SemaphoreType.DMA((3 * RING + len(LATE),)),
        ],
        compiler_params=pltpu.CompilerParams(vmem_limit_bytes=VMEM_LIMIT),
        cost_estimate=pl.CostEstimate(flops=1, bytes_accessed=1, transcendentals=0),
        name="attention",
    )(starts, *far_first(kv), halo, *far_first(qg), *prior)
    return results[:RING], results[RING:]


def join_first_kernel(*rest):
    own_refs = in_order(rest[:RING])
    dq_out, own, sems, sems_out = rest[RING:]
    z, _ = my_place()
    inward, outward = Copies(sems), Copies(sems_out)
    for s in range(RING):
        inward.start(own_refs[s].at[:, :QW], own.at[s])
    for s in range(RING):
        head = lax.rem(z + RING - s, RING) * CHUNKS
        inward.started[s].wait()
        outward.start(own.at[s], columns(dq_out, head * QW, QW))
    outward.wait()


def join_first(own):
    return pl.pallas_call(
        join_first_kernel,
        out_shape=jax.ShapeDtypeStruct((TOK, RING * CHUNKS * QW), jnp.bfloat16),
        in_specs=[in_hbm] * RING,
        out_specs=in_hbm,
        scratch_shapes=[
            pltpu.VMEM((RING, TOK, QW), jnp.bfloat16),
            pltpu.SemaphoreType.DMA((RING,)),
            pltpu.SemaphoreType.DMA((RING,)),
        ],
        compiler_params=pltpu.CompilerParams(vmem_limit_bytes=VMEM_LIMIT),
        name="join_first",
    )(*far_first(own))


def join_kernel(begun_ref, *rest):
    n = RING * CHUNKS
    own_refs, rest = in_order(rest[:RING]) + in_order(rest[RING:n]), rest[n:]
    early_refs, late_refs = rest[: 2 * len(EARLY)], rest[2 * len(EARLY) : 2 * len(EARLY) + len(LATE)]
    dq_out, dk_out, dv_out, own, dq, back, total, sems, sems_dq, sems_back, sems_out = rest[
        2 * len(EARLY) + len(LATE) :
    ]
    z, _ = my_place()
    copies = [Copies(x) for x in (sems, sems_dq, sems_back, sems_out)]
    inward, inward_dq, terms, outward = copies
    pieces = [(c, s) for c in range(CHUNKS) for s in range(RING)]
    for s in range(RING):
        inward_dq.start(own_refs[RING + s].at[:, :QW], dq.at[s])
    for i, (c, s) in enumerate(pieces):
        inward.start(own_refs[i].at[:, QW:], own.at[i])
        if s in EARLY:
            term = early_refs[c * len(EARLY) + EARLY.index(s)]
        else:
            term = late_refs[LATE.index(s)].at[:, 2 * c * WIDTH : 2 * (c + 1) * WIDTH]
        terms.start(term, back.at[i])
    for s in range(RING):
        head = lax.rem(z + RING - s, RING) * CHUNKS + 1
        inward_dq.started[s].wait()
        outward.start(dq.at[s], columns(dq_out, head * QW, QW))
    for i, (c, s) in enumerate(pieces):
        head = lax.rem(z + RING - s, RING) * CHUNKS + c
        inward.started[i].wait()
        terms.started[i].wait()
        sums = own[i].astype(jnp.float32) + back[i].astype(jnp.float32)
        total[i] = sums.astype(total.dtype)
        outward.start(total.at[i, :, :WIDTH], columns(dk_out, head * WIDTH, WIDTH))
        outward.start(total.at[i, :, WIDTH:], columns(dv_out, head * WIDTH, WIDTH))
    outward.wait()


def join(begun, own, early, late):
    heads = RING * CHUNKS
    bf16 = jnp.bfloat16
    return pl.pallas_call(
        join_kernel,
        out_shape=[
            jax.ShapeDtypeStruct((TOK, heads * QW), bf16),
            jax.ShapeDtypeStruct((TOK, heads * WIDTH), bf16),
            jax.ShapeDtypeStruct((TOK, heads * WIDTH), bf16),
        ],
        in_specs=[in_hbm] * (1 + heads + 2 * len(EARLY) + len(LATE)),
        out_specs=[in_hbm] * 3,
        input_output_aliases={0: 0},
        scratch_shapes=[
            pltpu.VMEM((heads, TOK, 2 * WIDTH), bf16),
            pltpu.VMEM((RING, TOK, QW), bf16),
            pltpu.VMEM((heads, TOK, 2 * WIDTH), bf16),
            pltpu.VMEM((heads, TOK, 2 * WIDTH), bf16),
            pltpu.SemaphoreType.DMA((heads,)),
            pltpu.SemaphoreType.DMA((RING,)),
            pltpu.SemaphoreType.DMA((heads,)),
            pltpu.SemaphoreType.DMA((RING + 2 * heads,)),
        ],
        compiler_params=pltpu.CompilerParams(vmem_limit_bytes=VMEM_LIMIT),
        name="join",
    )(begun, *far_first(own[:RING]), *far_first(own[RING:]), *early, *late)


def body(queries, keys, values, grad_out, weights, doc_ids):
    count = lax.axis_size(AXES)

    def send(pieces):
        sent = {s: shift_ring(pieces[s], s, count) for s in (2, 1, 3)}
        return [pieces[0]] + [sent[s] for s in range(1, RING)]

    kv = pack_keys(keys, values, doc_ids[None, :])
    kv = send(kv)
    qg = pack_queries(weights[None, :], queries, grad_out)
    two_hops = shift_ring(qg[0][2], 2, count)
    gathered, (now, next_) = lax.optimization_barrier((gather_halo(kv), qg))
    halo = [shift_row(gathered[0], 1, 0, count)]
    now = [now[0], shift_ring(now[1], 1, count), two_hops, shift_ring(now[3], 3, count)]
    halo.append(shift_row(gathered[1], 1, 0, count))
    now, next_ = lax.optimization_barrier((now, next_))
    qg = [now, send(next_)]
    starts = document_starts(kv, halo[0])

    first_own, first_back = attention(0, starts, kv, halo[0], qg[0], ())
    owns = send(first_own)
    early = [shift_row(first_back[s], -1, s, count) for s in EARLY]
    prior = [first_back[s] for s in LATE]
    own, back = attention(1, starts, kv, halo[1], qg[1], prior)
    own, back, owns, early = lax.optimization_barrier((own, back, owns, early))
    begun = join_first(owns)
    late = [shift_row(back[s], -1, s, count) for s in LATE]
    two_hops = shift_ring(own[2], 2, count)
    near, far, two_hops = lax.optimization_barrier((own[1], own[3], two_hops))
    owns += [own[0], shift_ring(near, 1, count), two_hops, shift_ring(far, 3, count)]
    return tuple(join(begun, owns, early, late))


def solution(mesh):
    rows = P(("dp", "inner", "outer"), None)
    flat = P(("dp", "inner", "outer"))
    return jax.shard_map(
        body,
        mesh=mesh,
        in_specs=(rows, rows, rows, rows, flat, flat),
        out_specs=(rows, rows, rows),
        check_vma=False,
    )
```

```python
import functools
import math

import jax
import jax.numpy as jnp
from jax import lax
from jax.experimental import pallas as pl
from jax.experimental.pallas import tpu as pltpu
from jax.sharding import PartitionSpec as P

WIDTH = 128
GROUP = 3
RING = 4
TOK = 256
ROW = RING * TOK
CHUNKS = 2
QT = 256
KT = 128
QW = GROUP * WIDTH
TILES = ROW // QT
KEYS = 2 * ROW
WINDOWS = (2, 3, 4, 5, 7, 10)
IDS = 16
EARLY, LATE = (), (0, 1, 2, 3)
FAR_FIRST = (2, 1, 3, 0)
AXES = ("inner", "outer")
NEG = -1e30
LOG2E = 1.4426950408889634
VMEM_LIMIT = 48 * 1024 * 1024
PACK_LIMIT = 60 * 1024 * 1024

in_hbm = pl.BlockSpec(memory_space=pltpu.HBM)
in_vmem = pl.BlockSpec(memory_space=pltpu.VMEM)


def my_place():
    index = lax.axis_index(AXES)
    return lax.rem(index, RING), index // RING


def far_first(pieces):
    return [pieces[s] for s in FAR_FIRST]


def in_order(refs):
    return [refs[FAR_FIRST.index(s)] for s in range(RING)]


def shift_ring(x, by, count):
    return lax.ppermute(x, AXES, [(i, i // RING * RING + (i + by) % RING) for i in range(count)])


def shift_row(x, by, ring_by, count):
    pairs = [(i, (i // RING + by) * RING + (i + ring_by) % RING) for i in range(count)]
    return lax.ppermute(x, AXES, [(i, j) for i, j in pairs if 0 <= j < count])


class Copies:
    def __init__(self, sems):
        self.sems, self.started = sems, []

    def prepare(self, source, target):
        copy = pltpu.make_async_copy(source, target, self.sems.at[len(self.started)])
        self.started.append(copy)
        return copy

    def start(self, source, target):
        self.prepare(source, target).start()

    def wait(self):
        for copy in self.started:
            copy.wait()


def columns(ref, first, width):
    return ref.at[:, pl.ds(pl.multiple_of(first, WIDTH), width)]


def pack_keys_kernel(k_ref, v_ref, ids_ref, *rest):
    kv_refs, (kv, sems_in, sems_out) = rest[:RING], rest[RING:]
    z, _ = my_place()
    order = (2, 1, 3, 0)
    inward, outward = Copies(sems_in), Copies(sems_out)
    for s in order:
        target = lax.rem(z + s, RING)
        for c in range(CHUNKS):
            for i, ref in enumerate((k_ref, v_ref)):
                source = columns(ref, (target * CHUNKS + c) * WIDTH, WIDTH)
                rows = pl.ds(IDS + c * TOK, TOK)
                inward.start(source, kv.at[s, rows, i * WIDTH : (i + 1) * WIDTH])
    ids = ids_ref[...].astype(jnp.float32).astype(jnp.bfloat16)
    ids = jnp.concatenate([ids, jnp.zeros((IDS - 1, TOK), jnp.bfloat16)], axis=0)
    for s in range(RING):
        kv[s, 0:IDS, :] = ids
    for i, s in enumerate(order):
        for copy in inward.started[2 * CHUNKS * i : 2 * CHUNKS * (i + 1)]:
            copy.wait()
        outward.start(kv.at[s], kv_refs[s])
    outward.wait()


def pack_keys(keys, values, ids):
    bf16 = jnp.bfloat16
    shape = (IDS + CHUNKS * TOK, 2 * WIDTH)
    return pl.pallas_call(
        pack_keys_kernel,
        out_shape=[jax.ShapeDtypeStruct(shape, bf16)] * RING,
        in_specs=[in_hbm, in_hbm, in_vmem],
        out_specs=[in_hbm] * RING,
        scratch_shapes=[
            pltpu.VMEM((RING,) + shape, bf16),
            pltpu.SemaphoreType.DMA((RING * 2 * CHUNKS,)),
            pltpu.SemaphoreType.DMA((RING,)),
        ],
        compiler_params=pltpu.CompilerParams(vmem_limit_bytes=PACK_LIMIT),
        name="pack_keys",
    )(keys, values, ids)


def pack_queries_kernel(w_ref, q_ref, g_ref, *rest):
    n = RING * CHUNKS
    qg_refs, (qg, sems_in, sems_out) = rest[:n], rest[n:]
    z, _ = my_place()
    order = [c * RING + s for c in range(CHUNKS) for s in (2, 1, 3, 0)]
    inward, outward = Copies(sems_in), Copies(sems_out)
    for n in order:
        first = (lax.rem(z + n % RING, RING) * CHUNKS + n // RING) * QW
        inward.start(columns(q_ref, first, QW), qg.at[n, :, :QW])
        inward.start(columns(g_ref, first, QW), qg.at[n, :, QW:])
    w = jnp.broadcast_to(w_ref[...], (8, TOK)).T[:, 0:1]
    for i, n in enumerate(order):
        inward.started[2 * i].wait()
        inward.started[2 * i + 1].wait()
        qg[n, :, QW:] = (w * qg[n, :, QW:].astype(jnp.float32)).astype(jnp.bfloat16)
        outward.start(qg.at[n], qg_refs[n])
    outward.wait()


def pack_queries(weights, queries, grad_out):
    bf16 = jnp.bfloat16
    n = RING * CHUNKS
    pieces = pl.pallas_call(
        pack_queries_kernel,
        out_shape=[jax.ShapeDtypeStruct((TOK, 2 * QW), bf16)] * n,
        in_specs=[in_vmem, in_hbm, in_hbm],
        out_specs=[in_hbm] * n,
        scratch_shapes=[
            pltpu.VMEM((n, TOK, 2 * QW), bf16),
            pltpu.SemaphoreType.DMA((2 * n,)),
            pltpu.SemaphoreType.DMA((n,)),
        ],
        compiler_params=pltpu.CompilerParams(vmem_limit_bytes=PACK_LIMIT),
        name="pack_queries",
    )(weights, queries, grad_out)
    return [pieces[c * RING : (c + 1) * RING] for c in range(CHUNKS)]


def gather_halo_kernel(*refs):
    kv_refs = in_order(refs[:RING])
    first_ref, second_ref, kv, sems_in, sems_out = refs[RING:]
    inward, outward = Copies(sems_in), Copies(sems_out)
    for s in range(RING):
        inward.start(kv_refs[s], kv.at[s])
    top = IDS + TOK
    for s in range(RING):
        inward.started[s].wait()
        outward.start(kv.at[s, 0:top, :], first_ref.at[s * top : (s + 1) * top, :])
        outward.start(kv.at[s, top:, :], second_ref.at[s * TOK : (s + 1) * TOK, :])
    outward.wait()


def gather_halo(kv):
    bf16 = jnp.bfloat16
    return pl.pallas_call(
        gather_halo_kernel,
        out_shape=[
            jax.ShapeDtypeStruct((RING * (IDS + TOK), 2 * WIDTH), bf16),
            jax.ShapeDtypeStruct((ROW, 2 * WIDTH), bf16),
        ],
        in_specs=[in_hbm] * RING,
        out_specs=[in_hbm] * 2,
        scratch_shapes=[
            pltpu.VMEM((RING, IDS + CHUNKS * TOK, 2 * WIDTH), bf16),
            pltpu.SemaphoreType.DMA((RING,)),
            pltpu.SemaphoreType.DMA((2 * RING,)),
        ],
        compiler_params=pltpu.CompilerParams(vmem_limit_bytes=VMEM_LIMIT),
        name="gather_halo",
    )(*far_first(kv))


def starts_kernel(*rest):
    kv_refs = in_order(rest[:RING])
    halo_ref, starts_ref, ids, sems = rest[RING:]
    copies = Copies(sems)
    for i, ref in enumerate(kv_refs):
        copies.start(ref.at[0:IDS, :], ids.at[i * IDS : (i + 1) * IDS, :])
    for s in range(RING):
        first, i = s * (IDS + TOK), RING + s
        copies.start(halo_ref.at[first : first + IDS, :], ids.at[i * IDS : (i + 1) * IDS, :])
    copies.wait()
    z, row = my_place()
    rows = ids[...].astype(jnp.float32)
    by_key = rows.T
    past = jnp.where(row > 0, by_key[:, RING * IDS :], -1.0)
    before = [by_key[:, s * IDS : s * IDS + 1] for s in range(RING)]
    before += [past[:, s * IDS : s * IDS + 1] for s in range(RING)]
    for s in range(RING):
        own = rows[s * IDS : s * IDS + 1, :]
        found = jnp.zeros((TOK, TOK), jnp.int32)
        for column in before:
            found += jnp.where(column < own, 1, 0)
        source = lax.rem(z + RING - s, RING)
        at = pl.multiple_of(source * TOK, TOK)
        starts_ref[:, pl.ds(at, TOK)] = jnp.sum(found, axis=0, keepdims=True)


def document_starts(kv, halo):
    return pl.pallas_call(
        starts_kernel,
        out_shape=jax.ShapeDtypeStruct((1, ROW), jnp.int32),
        in_specs=[in_hbm] * (RING + 1),
        out_specs=in_vmem,
        scratch_shapes=[
            pltpu.VMEM((2 * RING * IDS, TOK), jnp.bfloat16),
            pltpu.SemaphoreType.DMA((2 * RING,)),
        ],
        compiler_params=pltpu.CompilerParams(vmem_limit_bytes=VMEM_LIMIT),
        name="document_starts",
    )(*far_first(kv), halo)


def attention_kernel(chunk, start_ref, *rest):
    kv_refs, halo_ref = in_order(rest[:RING]), rest[RING]
    qg_refs, rest = in_order(rest[RING + 1 : 2 * RING + 1]), rest[2 * RING + 1 :]
    prior_refs, rest = rest[: len(LATE) * chunk], rest[len(LATE) * chunk :]
    own_refs, back_refs = rest[:RING], rest[RING : 2 * RING]
    kv, qg, dkv, dq, dkv16, prior, sems_kv, sems_qg, sems_prior, sems_out = rest[2 * RING :]
    z, _ = my_place()
    scale = 1.0 / math.sqrt(WIDTH)

    inward_kv, inward_qg, inward_prior = Copies(sems_kv), Copies(sems_qg), Copies(sems_prior)
    sources = [lax.rem(z + RING - s, RING) for s in range(RING)]
    skip = 0 if chunk else IDS
    for s in range(RING):
        halo_rows = pl.ds(pl.multiple_of(sources[s] * TOK, WIDTH), TOK)
        own_rows = pl.ds(pl.multiple_of(ROW + sources[s] * TOK, WIDTH), TOK)
        inward_kv.start(kv_refs[s].at[pl.ds(IDS + chunk * TOK, TOK), :], kv.at[own_rows, :])
        first = s * (skip + TOK) + skip
        inward_kv.start(halo_ref.at[first : first + TOK, :], kv.at[halo_rows, :])
    for s in range(RING):
        rows = pl.ds(pl.multiple_of(sources[s] * TOK, TOK), TOK)
        inward_qg.start(qg_refs[s], qg.at[rows, :])
    for i, ref in enumerate(prior_refs):
        inward_prior.start(ref, prior.at[i])
    dkv[...] = jnp.zeros(dkv.shape, dkv.dtype)
    inward_kv.wait()

    outward = Copies(sems_out)
    dq_copies = []
    for s in range(RING):
        rows = pl.ds(pl.multiple_of(lax.rem(z + s, RING) * TOK, TOK), TOK)
        dq_copies.append(outward.prepare(dq.at[rows, :], own_refs[s].at[:, :QW]))

    def tile(i, carry):
        first = pl.multiple_of(lax.rem(z + i, RING) * QT, QT)
        for s in range(RING):
            pl.when(i == s)(inward_qg.started[(RING - s) % RING].wait)
        starts = start_ref[:, pl.ds(first, QT)]
        end = ROW + first + QT
        count = (end - jnp.min(starts) + KT - 1) // KT

        def work(windows):
            span = windows * KT
            base = pl.multiple_of(end - span, WIDTH)
            keys = pl.ds(base, span)
            rows = qg[pl.ds(first, QT), :]
            heads = [rows[:, h * WIDTH : (h + 1) * WIDTH] for h in range(2 * GROUP)]
            qs = jnp.concatenate(heads[:GROUP], axis=0)
            gs = jnp.concatenate(heads[GROUP:], axis=0)
            q_t, g_t = qs.T, gs.T
            k, v = kv[keys, :WIDTH], kv[keys, WIDTH:]
            k_t, v_t = k.T, v.T
            s = jnp.dot(k, q_t, preferred_element_type=jnp.float32)
            key_at = lax.broadcasted_iota(jnp.int32, (span, QT), 0) + base
            query_at = ROW + first + lax.broadcasted_iota(jnp.int32, (span, QT), 1)
            seen = (key_at >= starts) & (key_at <= query_at)
            s = jnp.where(jnp.concatenate([seen] * GROUP, axis=1), s, NEG)
            e = jnp.exp2((s - jnp.max(s, axis=0, keepdims=True)) * (scale * LOG2E))
            p = e * (1.0 / jnp.sum(e, axis=0, keepdims=True))
            p16 = p.astype(jnp.bfloat16)
            out = jnp.dot(v_t, p16, preferred_element_type=jnp.float32)
            out = out.astype(jnp.bfloat16).astype(jnp.float32)
            delta = jnp.sum(g_t.astype(jnp.float32) * out, axis=0, keepdims=True)
            dp = jnp.dot(v, g_t, preferred_element_type=jnp.float32)
            ds = (p * (dp - delta) * scale).astype(jnp.bfloat16)
            dkv[keys, :WIDTH] += jnp.dot(ds, qs, preferred_element_type=jnp.float32)
            dkv[keys, WIDTH:] += jnp.dot(p16, gs, preferred_element_type=jnp.float32)
            dq_t = jnp.dot(k_t, ds, preferred_element_type=jnp.float32)
            for h in range(GROUP):
                dq[pl.ds(first, QT), h * WIDTH : (h + 1) * WIDTH] = (
                    dq_t[:, h * QT : (h + 1) * QT].T.astype(jnp.bfloat16)
                )

        for fewer, windows in zip((0,) + WINDOWS, WINDOWS):
            pl.when((count > fewer) & (count <= windows))(functools.partial(work, windows))
        for s in range(RING):
            pl.when(i == s)(dq_copies[s].start)
        return carry

    lax.fori_loop(0, TILES, tile, 0)
    for s in range(RING):
        owner = lax.rem(z + s, RING)
        for part in range(2):
            rows = pl.ds(pl.multiple_of(part * ROW + owner * TOK, TOK), TOK)
            dkv16[rows, :] = dkv[rows, :].astype(jnp.bfloat16)
            if part:
                target = own_refs[s].at[:, QW:]
            elif chunk and s in LATE:
                target = back_refs[s].at[:, 2 * WIDTH :]
            else:
                target = back_refs[s]
            outward.start(dkv16.at[rows, :], target)
    inward_prior.wait()
    for i, s in enumerate(LATE[: len(prior_refs)]):
        outward.start(prior.at[i], back_refs[s].at[:, : 2 * WIDTH])
    outward.wait()


def attention(chunk, starts, kv, halo, qg, prior):
    bf16, f32 = jnp.bfloat16, jnp.float32
    wide = [2 if chunk and s in LATE else 1 for s in range(RING)]
    results = pl.pallas_call(
        functools.partial(attention_kernel, chunk),
        out_shape=[jax.ShapeDtypeStruct((TOK, QW + 2 * WIDTH), bf16)] * RING
        + [jax.ShapeDtypeStruct((TOK, 2 * WIDTH * n), bf16) for n in wide],
        in_specs=[in_vmem] + [in_hbm] * (2 * RING + 1 + len(prior)),
        out_specs=[in_hbm] * (2 * RING),
        scratch_shapes=[
            pltpu.VMEM((KEYS, 2 * WIDTH), bf16),
            pltpu.VMEM((ROW, 2 * QW), bf16),
            pltpu.VMEM((KEYS, 2 * WIDTH), f32),
            pltpu.VMEM((ROW, QW), bf16),
            pltpu.VMEM((2 * ROW, 2 * WIDTH), bf16),
            pltpu.VMEM((len(LATE), TOK, 2 * WIDTH), bf16),
            pltpu.SemaphoreType.DMA((2 * RING,)),
            pltpu.SemaphoreType.DMA((RING,)),
            pltpu.SemaphoreType.DMA((len(LATE),)),
            pltpu.SemaphoreType.DMA((3 * RING + len(LATE),)),
        ],
        compiler_params=pltpu.CompilerParams(vmem_limit_bytes=VMEM_LIMIT),
        cost_estimate=pl.CostEstimate(flops=1, bytes_accessed=1, transcendentals=0),
        name="attention",
    )(starts, *far_first(kv), halo, *far_first(qg), *prior)
    return results[:RING], results[RING:]


def join_first_kernel(*rest):
    own_refs = in_order(rest[:RING])
    dq_out, own, sems, sems_out = rest[RING:]
    z, _ = my_place()
    inward, outward = Copies(sems), Copies(sems_out)
    for s in range(RING):
        inward.start(own_refs[s].at[:, :QW], own.at[s])
    for s in range(RING):
        head = lax.rem(z + RING - s, RING) * CHUNKS
        inward.started[s].wait()
        outward.start(own.at[s], columns(dq_out, head * QW, QW))
    outward.wait()


def join_first(own):
    return pl.pallas_call(
        join_first_kernel,
        out_shape=jax.ShapeDtypeStruct((TOK, RING * CHUNKS * QW), jnp.bfloat16),
        in_specs=[in_hbm] * RING,
        out_specs=in_hbm,
        scratch_shapes=[
            pltpu.VMEM((RING, TOK, QW), jnp.bfloat16),
            pltpu.SemaphoreType.DMA((RING,)),
            pltpu.SemaphoreType.DMA((RING,)),
        ],
        compiler_params=pltpu.CompilerParams(vmem_limit_bytes=VMEM_LIMIT),
        name="join_first",
    )(*far_first(own))


def join_kernel(begun_ref, *rest):
    n = RING * CHUNKS
    own_refs, rest = in_order(rest[:RING]) + in_order(rest[RING:n]), rest[n:]
    early_refs, late_refs = rest[: 2 * len(EARLY)], rest[2 * len(EARLY) : 2 * len(EARLY) + len(LATE)]
    dq_out, dk_out, dv_out, own, dq, back, total, sems, sems_dq, sems_back, sems_out = rest[
        2 * len(EARLY) + len(LATE) :
    ]
    z, _ = my_place()
    copies = [Copies(x) for x in (sems, sems_dq, sems_back, sems_out)]
    inward, inward_dq, terms, outward = copies
    pieces = [(c, s) for c in range(CHUNKS) for s in range(RING)]
    for s in range(RING):
        inward_dq.start(own_refs[RING + s].at[:, :QW], dq.at[s])
    for i, (c, s) in enumerate(pieces):
        inward.start(own_refs[i].at[:, QW:], own.at[i])
        if s in EARLY:
            term = early_refs[c * len(EARLY) + EARLY.index(s)]
        else:
            term = late_refs[LATE.index(s)].at[:, 2 * c * WIDTH : 2 * (c + 1) * WIDTH]
        terms.start(term, back.at[i])
    for s in range(RING):
        head = lax.rem(z + RING - s, RING) * CHUNKS + 1
        inward_dq.started[s].wait()
        outward.start(dq.at[s], columns(dq_out, head * QW, QW))
    for i, (c, s) in enumerate(pieces):
        head = lax.rem(z + RING - s, RING) * CHUNKS + c
        inward.started[i].wait()
        terms.started[i].wait()
        sums = own[i].astype(jnp.float32) + back[i].astype(jnp.float32)
        total[i] = sums.astype(total.dtype)
        outward.start(total.at[i, :, :WIDTH], columns(dk_out, head * WIDTH, WIDTH))
        outward.start(total.at[i, :, WIDTH:], columns(dv_out, head * WIDTH, WIDTH))
    outward.wait()


def join(begun, own, early, late):
    heads = RING * CHUNKS
    bf16 = jnp.bfloat16
    return pl.pallas_call(
        join_kernel,
        out_shape=[
            jax.ShapeDtypeStruct((TOK, heads * QW), bf16),
            jax.ShapeDtypeStruct((TOK, heads * WIDTH), bf16),
            jax.ShapeDtypeStruct((TOK, heads * WIDTH), bf16),
        ],
        in_specs=[in_hbm] * (1 + heads + 2 * len(EARLY) + len(LATE)),
        out_specs=[in_hbm] * 3,
        input_output_aliases={0: 0},
        scratch_shapes=[
            pltpu.VMEM((heads, TOK, 2 * WIDTH), bf16),
            pltpu.VMEM((RING, TOK, QW), bf16),
            pltpu.VMEM((heads, TOK, 2 * WIDTH), bf16),
            pltpu.VMEM((heads, TOK, 2 * WIDTH), bf16),
            pltpu.SemaphoreType.DMA((heads,)),
            pltpu.SemaphoreType.DMA((RING,)),
            pltpu.SemaphoreType.DMA((heads,)),
            pltpu.SemaphoreType.DMA((RING + 2 * heads,)),
        ],
        compiler_params=pltpu.CompilerParams(vmem_limit_bytes=VMEM_LIMIT),
        name="join",
    )(begun, *far_first(own[:RING]), *far_first(own[RING:]), *early, *late)


def body(queries, keys, values, grad_out, weights, doc_ids):
    count = lax.axis_size(AXES)

    def send(pieces):
        sent = {s: shift_ring(pieces[s], s, count) for s in (2, 1, 3)}
        return [pieces[0]] + [sent[s] for s in range(1, RING)]

    kv = pack_keys(keys, values, doc_ids[None, :])
    kv = send(kv)
    qg = pack_queries(weights[None, :], queries, grad_out)
    two_hops = shift_ring(qg[0][2], 2, count)
    gathered, (now, next_) = lax.optimization_barrier((gather_halo(kv), qg))
    halo = [shift_row(gathered[0], 1, 0, count)]
    now = [now[0], shift_ring(now[1], 1, count), two_hops, shift_ring(now[3], 3, count)]
    halo.append(shift_row(gathered[1], 1, 0, count))
    now, next_ = lax.optimization_barrier((now, next_))
    qg = [now, send(next_)]
    starts = document_starts(kv, halo[0])

    first_own, first_back = attention(0, starts, kv, halo[0], qg[0], ())
    owns = send(first_own)
    early = [shift_row(first_back[s], -1, s, count) for s in EARLY]
    prior = [first_back[s] for s in LATE]
    own, back = attention(1, starts, kv, halo[1], qg[1], prior)
    own, back, owns, early = lax.optimization_barrier((own, back, owns, early))
    begun = join_first(owns)
    owns += send(own)
    first, last = (2, 3), (1, 0)
    late = {s: shift_row(back[s], -1, s, count) for s in first}
    *rest, owns[RING + 2] = lax.optimization_barrier((*[back[s] for s in last], owns[RING + 2]))
    late.update({s: shift_row(piece, -1, s, count) for piece, s in zip(rest, last)})
    late = [late[s] for s in LATE]
    return tuple(join(begun, owns, early, late))


def solution(mesh):
    rows = P(("dp", "inner", "outer"), None)
    flat = P(("dp", "inner", "outer"))
    return jax.shard_map(
        body,
        mesh=mesh,
        in_specs=(rows, rows, rows, rows, flat, flat),
        out_specs=(rows, rows, rows),
        check_vma=False,
    )
```

```python
import functools
import math

import jax
import jax.numpy as jnp
from jax import lax
from jax.experimental import pallas as pl
from jax.experimental.pallas import tpu as pltpu
from jax.sharding import PartitionSpec as P

WIDTH = 128
GROUP = 3
RING = 4
TOK = 256
ROW = RING * TOK
CHUNKS = 2
QT = 256
KT = 128
QW = GROUP * WIDTH
TILES = ROW // QT
KEYS = 2 * ROW
WINDOWS = (2, 3, 4, 5, 7, 10)
IDS = 16
EARLY, LATE = (), (0, 1, 2, 3)
FAR_FIRST = (2, 1, 3, 0)
AXES = ("inner", "outer")
NEG = -1e30
LOG2E = 1.4426950408889634
VMEM_LIMIT = 48 * 1024 * 1024
PACK_LIMIT = 60 * 1024 * 1024

in_hbm = pl.BlockSpec(memory_space=pltpu.HBM)
in_vmem = pl.BlockSpec(memory_space=pltpu.VMEM)


def my_place():
    index = lax.axis_index(AXES)
    return lax.rem(index, RING), index // RING


def far_first(pieces):
    return [pieces[s] for s in FAR_FIRST]


def in_order(refs):
    return [refs[FAR_FIRST.index(s)] for s in range(RING)]


def shift_ring(x, by, count):
    return lax.ppermute(x, AXES, [(i, i // RING * RING + (i + by) % RING) for i in range(count)])


def shift_row(x, by, ring_by, count):
    pairs = [(i, (i // RING + by) * RING + (i + ring_by) % RING) for i in range(count)]
    return lax.ppermute(x, AXES, [(i, j) for i, j in pairs if 0 <= j < count])


class Copies:
    def __init__(self, sems):
        self.sems, self.started = sems, []

    def prepare(self, source, target):
        copy = pltpu.make_async_copy(source, target, self.sems.at[len(self.started)])
        self.started.append(copy)
        return copy

    def start(self, source, target):
        self.prepare(source, target).start()

    def wait(self):
        for copy in self.started:
            copy.wait()


def columns(ref, first, width):
    return ref.at[:, pl.ds(pl.multiple_of(first, WIDTH), width)]


def pack_keys_kernel(k_ref, v_ref, ids_ref, *rest):
    kv_refs, (kv, sems_in, sems_out) = rest[:RING], rest[RING:]
    z, _ = my_place()
    order = (2, 1, 3, 0)
    inward, outward = Copies(sems_in), Copies(sems_out)
    for s in order:
        target = lax.rem(z + s, RING)
        for c in range(CHUNKS):
            for i, ref in enumerate((k_ref, v_ref)):
                source = columns(ref, (target * CHUNKS + c) * WIDTH, WIDTH)
                rows = pl.ds(IDS + c * TOK, TOK)
                inward.start(source, kv.at[s, rows, i * WIDTH : (i + 1) * WIDTH])
    ids = ids_ref[...].astype(jnp.float32).astype(jnp.bfloat16)
    ids = jnp.concatenate([ids, jnp.zeros((IDS - 1, TOK), jnp.bfloat16)], axis=0)
    for s in range(RING):
        kv[s, 0:IDS, :] = ids
    for i, s in enumerate(order):
        for copy in inward.started[2 * CHUNKS * i : 2 * CHUNKS * (i + 1)]:
            copy.wait()
        outward.start(kv.at[s], kv_refs[s])
    outward.wait()


def pack_keys(keys, values, ids):
    bf16 = jnp.bfloat16
    shape = (IDS + CHUNKS * TOK, 2 * WIDTH)
    return pl.pallas_call(
        pack_keys_kernel,
        out_shape=[jax.ShapeDtypeStruct(shape, bf16)] * RING,
        in_specs=[in_hbm, in_hbm, in_vmem],
        out_specs=[in_hbm] * RING,
        scratch_shapes=[
            pltpu.VMEM((RING,) + shape, bf16),
            pltpu.SemaphoreType.DMA((RING * 2 * CHUNKS,)),
            pltpu.SemaphoreType.DMA((RING,)),
        ],
        compiler_params=pltpu.CompilerParams(vmem_limit_bytes=PACK_LIMIT),
        name="pack_keys",
    )(keys, values, ids)


def pack_queries_kernel(w_ref, q_ref, g_ref, *rest):
    n = RING * CHUNKS
    qg_refs, (qg, sems_in, sems_out) = rest[:n], rest[n:]
    z, _ = my_place()
    order = [c * RING + s for c in range(CHUNKS) for s in (2, 1, 3, 0)]
    inward, outward = Copies(sems_in), Copies(sems_out)
    for n in order:
        first = (lax.rem(z + n % RING, RING) * CHUNKS + n // RING) * QW
        inward.start(columns(q_ref, first, QW), qg.at[n, :, :QW])
        inward.start(columns(g_ref, first, QW), qg.at[n, :, QW:])
    w = jnp.broadcast_to(w_ref[...], (8, TOK)).T[:, 0:1]
    for i, n in enumerate(order):
        inward.started[2 * i].wait()
        inward.started[2 * i + 1].wait()
        qg[n, :, QW:] = (w * qg[n, :, QW:].astype(jnp.float32)).astype(jnp.bfloat16)
        outward.start(qg.at[n], qg_refs[n])
    outward.wait()


def pack_queries(weights, queries, grad_out):
    bf16 = jnp.bfloat16
    n = RING * CHUNKS
    pieces = pl.pallas_call(
        pack_queries_kernel,
        out_shape=[jax.ShapeDtypeStruct((TOK, 2 * QW), bf16)] * n,
        in_specs=[in_vmem, in_hbm, in_hbm],
        out_specs=[in_hbm] * n,
        scratch_shapes=[
            pltpu.VMEM((n, TOK, 2 * QW), bf16),
            pltpu.SemaphoreType.DMA((2 * n,)),
            pltpu.SemaphoreType.DMA((n,)),
        ],
        compiler_params=pltpu.CompilerParams(vmem_limit_bytes=PACK_LIMIT),
        name="pack_queries",
    )(weights, queries, grad_out)
    return [pieces[c * RING : (c + 1) * RING] for c in range(CHUNKS)]


def gather_halo_kernel(*refs):
    kv_refs = in_order(refs[:RING])
    first_ref, second_ref, kv, sems_in, sems_out = refs[RING:]
    inward, outward = Copies(sems_in), Copies(sems_out)
    for s in range(RING):
        inward.start(kv_refs[s], kv.at[s])
    top = IDS + TOK
    for s in range(RING):
        inward.started[s].wait()
        outward.start(kv.at[s, 0:top, :], first_ref.at[s * top : (s + 1) * top, :])
        outward.start(kv.at[s, top:, :], second_ref.at[s * TOK : (s + 1) * TOK, :])
    outward.wait()


def gather_halo(kv):
    bf16 = jnp.bfloat16
    return pl.pallas_call(
        gather_halo_kernel,
        out_shape=[
            jax.ShapeDtypeStruct((RING * (IDS + TOK), 2 * WIDTH), bf16),
            jax.ShapeDtypeStruct((ROW, 2 * WIDTH), bf16),
        ],
        in_specs=[in_hbm] * RING,
        out_specs=[in_hbm] * 2,
        scratch_shapes=[
            pltpu.VMEM((RING, IDS + CHUNKS * TOK, 2 * WIDTH), bf16),
            pltpu.SemaphoreType.DMA((RING,)),
            pltpu.SemaphoreType.DMA((2 * RING,)),
        ],
        compiler_params=pltpu.CompilerParams(vmem_limit_bytes=VMEM_LIMIT),
        name="gather_halo",
    )(*far_first(kv))


def fill_starts(starts_ref, ids):
    z, row = my_place()
    rows = ids[...].astype(jnp.float32)
    by_key = rows.T
    past = jnp.where(row > 0, by_key[:, RING * IDS :], -1.0)
    before = [by_key[:, s * IDS : s * IDS + 1] for s in range(RING)]
    before += [past[:, s * IDS : s * IDS + 1] for s in range(RING)]
    for s in range(RING):
        own = rows[s * IDS : s * IDS + 1, :]
        found = jnp.zeros((TOK, TOK), jnp.int32)
        for column in before:
            found += jnp.where(column < own, 1, 0)
        source = lax.rem(z + RING - s, RING)
        at = pl.multiple_of(source * TOK, TOK)
        starts_ref[:, pl.ds(at, TOK)] = jnp.sum(found, axis=0, keepdims=True)


def attention_kernel(chunk, *rest):
    if chunk:
        start_ref, rest = rest[0], rest[1:]
    kv_refs, halo_ref = in_order(rest[:RING]), rest[RING]
    qg_refs, rest = in_order(rest[RING + 1 : 2 * RING + 1]), rest[2 * RING + 1 :]
    prior_refs, rest = rest[: len(LATE) * chunk], rest[len(LATE) * chunk :]
    own_refs, back_refs = rest[:RING], rest[RING : 2 * RING]
    rest = rest[2 * RING :]
    if not chunk:
        start_ref, *rest, ids, sems_ids = rest
    kv, qg, dkv, dq, dkv16, prior, sems_kv, sems_qg, sems_prior, sems_out = rest
    z, _ = my_place()
    scale = 1.0 / math.sqrt(WIDTH)

    inward_kv, inward_qg, inward_prior = Copies(sems_kv), Copies(sems_qg), Copies(sems_prior)
    sources = [lax.rem(z + RING - s, RING) for s in range(RING)]
    skip = 0 if chunk else IDS
    if not chunk:
        inward_ids = Copies(sems_ids)
        for s in range(RING):
            inward_ids.start(kv_refs[s].at[0:IDS, :], ids.at[s * IDS : (s + 1) * IDS, :])
        for s in range(RING):
            first, at = s * (IDS + TOK), (RING + s) * IDS
            inward_ids.start(halo_ref.at[first : first + IDS, :], ids.at[at : at + IDS, :])
    for s in range(RING):
        halo_rows = pl.ds(pl.multiple_of(sources[s] * TOK, WIDTH), TOK)
        own_rows = pl.ds(pl.multiple_of(ROW + sources[s] * TOK, WIDTH), TOK)
        inward_kv.start(kv_refs[s].at[pl.ds(IDS + chunk * TOK, TOK), :], kv.at[own_rows, :])
        first = s * (skip + TOK) + skip
        inward_kv.start(halo_ref.at[first : first + TOK, :], kv.at[halo_rows, :])
    for s in range(RING):
        rows = pl.ds(pl.multiple_of(sources[s] * TOK, TOK), TOK)
        inward_qg.start(qg_refs[s], qg.at[rows, :])
    for i, ref in enumerate(prior_refs):
        inward_prior.start(ref, prior.at[i])
    dkv[...] = jnp.zeros(dkv.shape, dkv.dtype)
    if not chunk:
        inward_ids.wait()
        fill_starts(start_ref, ids)
    inward_kv.wait()

    outward = Copies(sems_out)
    dq_copies = []
    for s in range(RING):
        rows = pl.ds(pl.multiple_of(lax.rem(z + s, RING) * TOK, TOK), TOK)
        dq_copies.append(outward.prepare(dq.at[rows, :], own_refs[s].at[:, :QW]))

    def tile(i, carry):
        first = pl.multiple_of(lax.rem(z + i, RING) * QT, QT)
        for s in range(RING):
            pl.when(i == s)(inward_qg.started[(RING - s) % RING].wait)
        starts = start_ref[:, pl.ds(first, QT)]
        end = ROW + first + QT
        count = (end - jnp.min(starts) + KT - 1) // KT

        def work(windows):
            span = windows * KT
            base = pl.multiple_of(end - span, WIDTH)
            keys = pl.ds(base, span)
            rows = qg[pl.ds(first, QT), :]
            heads = [rows[:, h * WIDTH : (h + 1) * WIDTH] for h in range(2 * GROUP)]
            qs = jnp.concatenate(heads[:GROUP], axis=0)
            gs = jnp.concatenate(heads[GROUP:], axis=0)
            q_t, g_t = qs.T, gs.T
            k, v = kv[keys, :WIDTH], kv[keys, WIDTH:]
            k_t, v_t = k.T, v.T
            s = jnp.dot(k, q_t, preferred_element_type=jnp.float32)
            key_at = lax.broadcasted_iota(jnp.int32, (span, QT), 0) + base
            query_at = ROW + first + lax.broadcasted_iota(jnp.int32, (span, QT), 1)
            seen = (key_at >= starts) & (key_at <= query_at)
            s = jnp.where(jnp.concatenate([seen] * GROUP, axis=1), s, NEG)
            e = jnp.exp2((s - jnp.max(s, axis=0, keepdims=True)) * (scale * LOG2E))
            p = e * (1.0 / jnp.sum(e, axis=0, keepdims=True))
            p16 = p.astype(jnp.bfloat16)
            out = jnp.dot(v_t, p16, preferred_element_type=jnp.float32)
            out = out.astype(jnp.bfloat16).astype(jnp.float32)
            delta = jnp.sum(g_t.astype(jnp.float32) * out, axis=0, keepdims=True)
            dp = jnp.dot(v, g_t, preferred_element_type=jnp.float32)
            ds = (p * (dp - delta) * scale).astype(jnp.bfloat16)
            dkv[keys, :WIDTH] += jnp.dot(ds, qs, preferred_element_type=jnp.float32)
            dkv[keys, WIDTH:] += jnp.dot(p16, gs, preferred_element_type=jnp.float32)
            dq_t = jnp.dot(k_t, ds, preferred_element_type=jnp.float32)
            for h in range(GROUP):
                dq[pl.ds(first, QT), h * WIDTH : (h + 1) * WIDTH] = (
                    dq_t[:, h * QT : (h + 1) * QT].T.astype(jnp.bfloat16)
                )

        for fewer, windows in zip((0,) + WINDOWS, WINDOWS):
            pl.when((count > fewer) & (count <= windows))(functools.partial(work, windows))
        for s in range(RING):
            pl.when(i == s)(dq_copies[s].start)
        return carry

    lax.fori_loop(0, TILES, tile, 0)
    for s in range(RING):
        owner = lax.rem(z + s, RING)
        for part in range(2):
            rows = pl.ds(pl.multiple_of(part * ROW + owner * TOK, TOK), TOK)
            dkv16[rows, :] = dkv[rows, :].astype(jnp.bfloat16)
            if part:
                target = own_refs[s].at[:, QW:]
            elif chunk and s in LATE:
                target = back_refs[s].at[:, 2 * WIDTH :]
            else:
                target = back_refs[s]
            outward.start(dkv16.at[rows, :], target)
    inward_prior.wait()
    for i, s in enumerate(LATE[: len(prior_refs)]):
        outward.start(prior.at[i], back_refs[s].at[:, : 2 * WIDTH])
    outward.wait()


def attention(chunk, starts, kv, halo, qg, prior):
    bf16, f32 = jnp.bfloat16, jnp.float32
    wide = [2 if chunk and s in LATE else 1 for s in range(RING)]
    given = [] if starts is None else [starts]
    found = [jax.ShapeDtypeStruct((1, ROW), jnp.int32)] if starts is None else []
    ids_scratch = [
        pltpu.VMEM((2 * RING * IDS, TOK), bf16),
        pltpu.SemaphoreType.DMA((2 * RING,)),
    ]
    results = pl.pallas_call(
        functools.partial(attention_kernel, chunk),
        out_shape=[jax.ShapeDtypeStruct((TOK, QW + 2 * WIDTH), bf16)] * RING
        + [jax.ShapeDtypeStruct((TOK, 2 * WIDTH * n), bf16) for n in wide]
        + found,
        in_specs=[in_vmem] * len(given) + [in_hbm] * (2 * RING + 1 + len(prior)),
        out_specs=[in_hbm] * (2 * RING) + [in_vmem] * len(found),
        scratch_shapes=[
            pltpu.VMEM((KEYS, 2 * WIDTH), bf16),
            pltpu.VMEM((ROW, 2 * QW), bf16),
            pltpu.VMEM((KEYS, 2 * WIDTH), f32),
            pltpu.VMEM((ROW, QW), bf16),
            pltpu.VMEM((2 * ROW, 2 * WIDTH), bf16),
            pltpu.VMEM((len(LATE), TOK, 2 * WIDTH), bf16),
            pltpu.SemaphoreType.DMA((2 * RING,)),
            pltpu.SemaphoreType.DMA((RING,)),
            pltpu.SemaphoreType.DMA((len(LATE),)),
            pltpu.SemaphoreType.DMA((3 * RING + len(LATE),)),
        ]
        + (ids_scratch if found else []),
        compiler_params=pltpu.CompilerParams(vmem_limit_bytes=VMEM_LIMIT),
        cost_estimate=pl.CostEstimate(flops=1, bytes_accessed=1, transcendentals=0),
        name="attention",
    )(*given, *far_first(kv), halo, *far_first(qg), *prior)
    if found:
        starts = results[2 * RING]
    return results[:RING], results[RING : 2 * RING], starts


def join_first_kernel(*rest):
    own_refs = in_order(rest[:RING])
    dq_out, own, sems, sems_out = rest[RING:]
    z, _ = my_place()
    inward, outward = Copies(sems), Copies(sems_out)
    for s in range(RING):
        inward.start(own_refs[s].at[:, :QW], own.at[s])
    for s in range(RING):
        head = lax.rem(z + RING - s, RING) * CHUNKS
        inward.started[s].wait()
        outward.start(own.at[s], columns(dq_out, head * QW, QW))
    outward.wait()


def join_first(own):
    return pl.pallas_call(
        join_first_kernel,
        out_shape=jax.ShapeDtypeStruct((TOK, RING * CHUNKS * QW), jnp.bfloat16),
        in_specs=[in_hbm] * RING,
        out_specs=in_hbm,
        scratch_shapes=[
            pltpu.VMEM((RING, TOK, QW), jnp.bfloat16),
            pltpu.SemaphoreType.DMA((RING,)),
            pltpu.SemaphoreType.DMA((RING,)),
        ],
        compiler_params=pltpu.CompilerParams(vmem_limit_bytes=VMEM_LIMIT),
        name="join_first",
    )(*far_first(own))


def join_kernel(begun_ref, *rest):
    n = RING * CHUNKS
    own_refs, rest = in_order(rest[:RING]) + in_order(rest[RING:n]), rest[n:]
    early_refs, late_refs = rest[: 2 * len(EARLY)], rest[2 * len(EARLY) : 2 * len(EARLY) + len(LATE)]
    dq_out, dk_out, dv_out, own, dq, back, total, sems, sems_dq, sems_back, sems_out = rest[
        2 * len(EARLY) + len(LATE) :
    ]
    z, _ = my_place()
    copies = [Copies(x) for x in (sems, sems_dq, sems_back, sems_out)]
    inward, inward_dq, terms, outward = copies
    pieces = [(c, s) for c in range(CHUNKS) for s in range(RING)]
    for s in range(RING):
        inward_dq.start(own_refs[RING + s].at[:, :QW], dq.at[s])
    for i, (c, s) in enumerate(pieces):
        inward.start(own_refs[i].at[:, QW:], own.at[i])
        if s in EARLY:
            term = early_refs[c * len(EARLY) + EARLY.index(s)]
        else:
            term = late_refs[LATE.index(s)].at[:, 2 * c * WIDTH : 2 * (c + 1) * WIDTH]
        terms.start(term, back.at[i])
    for s in range(RING):
        head = lax.rem(z + RING - s, RING) * CHUNKS + 1
        inward_dq.started[s].wait()
        outward.start(dq.at[s], columns(dq_out, head * QW, QW))
    for i, (c, s) in enumerate(pieces):
        head = lax.rem(z + RING - s, RING) * CHUNKS + c
        inward.started[i].wait()
        terms.started[i].wait()
        sums = own[i].astype(jnp.float32) + back[i].astype(jnp.float32)
        total[i] = sums.astype(total.dtype)
        outward.start(total.at[i, :, :WIDTH], columns(dk_out, head * WIDTH, WIDTH))
        outward.start(total.at[i, :, WIDTH:], columns(dv_out, head * WIDTH, WIDTH))
    outward.wait()


def join(begun, own, early, late):
    heads = RING * CHUNKS
    bf16 = jnp.bfloat16
    return pl.pallas_call(
        join_kernel,
        out_shape=[
            jax.ShapeDtypeStruct((TOK, heads * QW), bf16),
            jax.ShapeDtypeStruct((TOK, heads * WIDTH), bf16),
            jax.ShapeDtypeStruct((TOK, heads * WIDTH), bf16),
        ],
        in_specs=[in_hbm] * (1 + heads + 2 * len(EARLY) + len(LATE)),
        out_specs=[in_hbm] * 3,
        input_output_aliases={0: 0},
        scratch_shapes=[
            pltpu.VMEM((heads, TOK, 2 * WIDTH), bf16),
            pltpu.VMEM((RING, TOK, QW), bf16),
            pltpu.VMEM((heads, TOK, 2 * WIDTH), bf16),
            pltpu.VMEM((heads, TOK, 2 * WIDTH), bf16),
            pltpu.SemaphoreType.DMA((heads,)),
            pltpu.SemaphoreType.DMA((RING,)),
            pltpu.SemaphoreType.DMA((heads,)),
            pltpu.SemaphoreType.DMA((RING + 2 * heads,)),
        ],
        compiler_params=pltpu.CompilerParams(vmem_limit_bytes=VMEM_LIMIT),
        name="join",
    )(begun, *far_first(own[:RING]), *far_first(own[RING:]), *early, *late)


def body(queries, keys, values, grad_out, weights, doc_ids):
    count = lax.axis_size(AXES)

    def send(pieces):
        sent = {s: shift_ring(pieces[s], s, count) for s in (2, 1, 3)}
        return [pieces[0]] + [sent[s] for s in range(1, RING)]

    kv = pack_keys(keys, values, doc_ids[None, :])
    kv = send(kv)
    qg = pack_queries(weights[None, :], queries, grad_out)
    two_hops = shift_ring(qg[0][2], 2, count)
    gathered, (now, next_) = lax.optimization_barrier((gather_halo(kv), qg))
    halo = [shift_row(gathered[0], 1, 0, count)]
    now = [now[0], shift_ring(now[1], 1, count), two_hops, shift_ring(now[3], 3, count)]
    halo.append(shift_row(gathered[1], 1, 0, count))
    now, next_ = lax.optimization_barrier((now, next_))
    qg = [now, send(next_)]

    first_own, first_back, starts = attention(0, None, kv, halo[0], qg[0], ())
    owns = send(first_own)
    early = [shift_row(first_back[s], -1, s, count) for s in EARLY]
    prior = [first_back[s] for s in LATE]
    own, back, _ = attention(1, starts, kv, halo[1], qg[1], prior)
    own, back, owns, early = lax.optimization_barrier((own, back, owns, early))
    begun = join_first(owns)
    owns += send(own)
    first, last = (1, 3), (0, 2)
    late = {s: shift_row(back[s], -1, s, count) for s in first}
    *rest, owns[RING + 2] = lax.optimization_barrier((*[back[s] for s in last], owns[RING + 2]))
    late.update({s: shift_row(piece, -1, s, count) for piece, s in zip(rest, last)})
    late = [late[s] for s in LATE]
    return tuple(join(begun, owns, early, late))


def solution(mesh):
    rows = P(("dp", "inner", "outer"), None)
    flat = P(("dp", "inner", "outer"))
    return jax.shard_map(
        body,
        mesh=mesh,
        in_specs=(rows, rows, rows, rows, flat, flat),
        out_specs=(rows, rows, rows),
        check_vma=False,
    )
```

```python
import functools
import math

import jax
import jax.numpy as jnp
from jax import lax
from jax.experimental import pallas as pl
from jax.experimental.pallas import tpu as pltpu
from jax.sharding import PartitionSpec as P

WIDTH = 128
GROUP = 3
RING = 4
TOK = 256
ROW = RING * TOK
CHUNKS = 2
QT = 256
KT = 128
QW = GROUP * WIDTH
TILES = ROW // QT
KEYS = 2 * ROW
WINDOWS = (3, 5, 7, 9, 10)
IDS = 16
EARLY, LATE = (), (0, 1, 2, 3)
FAR_FIRST = (2, 1, 3, 0)
AXES = ("inner", "outer")
NEG = -1e30
LOG2E = 1.4426950408889634
VMEM_LIMIT = 48 * 1024 * 1024
PACK_LIMIT = 60 * 1024 * 1024

in_hbm = pl.BlockSpec(memory_space=pltpu.HBM)
in_vmem = pl.BlockSpec(memory_space=pltpu.VMEM)


def my_place():
    index = lax.axis_index(AXES)
    return lax.rem(index, RING), index // RING


def far_first(pieces):
    return [pieces[s] for s in FAR_FIRST]


def in_order(refs):
    return [refs[FAR_FIRST.index(s)] for s in range(RING)]


def shift_ring(x, by, count):
    return lax.ppermute(x, AXES, [(i, i // RING * RING + (i + by) % RING) for i in range(count)])


def shift_row(x, by, ring_by, count):
    pairs = [(i, (i // RING + by) * RING + (i + ring_by) % RING) for i in range(count)]
    return lax.ppermute(x, AXES, [(i, j) for i, j in pairs if 0 <= j < count])


class Copies:
    def __init__(self, sems):
        self.sems, self.started = sems, []

    def prepare(self, source, target):
        copy = pltpu.make_async_copy(source, target, self.sems.at[len(self.started)])
        self.started.append(copy)
        return copy

    def start(self, source, target):
        self.prepare(source, target).start()

    def wait(self):
        for copy in self.started:
            copy.wait()


def columns(ref, first, width):
    return ref.at[:, pl.ds(pl.multiple_of(first, WIDTH), width)]


def pack_keys_kernel(k_ref, v_ref, ids_ref, *rest):
    kv_refs, (kv, sems_in, sems_out) = rest[:RING], rest[RING:]
    z, _ = my_place()
    order = (2, 1, 3, 0)
    inward, outward = Copies(sems_in), Copies(sems_out)
    for s in order:
        target = lax.rem(z + s, RING)
        for c in range(CHUNKS):
            for i, ref in enumerate((k_ref, v_ref)):
                source = columns(ref, (target * CHUNKS + c) * WIDTH, WIDTH)
                rows = pl.ds(IDS + c * TOK, TOK)
                inward.start(source, kv.at[s, rows, i * WIDTH : (i + 1) * WIDTH])
    ids = ids_ref[...].astype(jnp.float32).astype(jnp.bfloat16)
    ids = jnp.concatenate([ids, jnp.zeros((IDS - 1, TOK), jnp.bfloat16)], axis=0)
    for s in range(RING):
        kv[s, 0:IDS, :] = ids
    for i, s in enumerate(order):
        for copy in inward.started[2 * CHUNKS * i : 2 * CHUNKS * (i + 1)]:
            copy.wait()
        outward.start(kv.at[s], kv_refs[s])
    outward.wait()


def pack_keys(keys, values, ids):
    bf16 = jnp.bfloat16
    shape = (IDS + CHUNKS * TOK, 2 * WIDTH)
    return pl.pallas_call(
        pack_keys_kernel,
        out_shape=[jax.ShapeDtypeStruct(shape, bf16)] * RING,
        in_specs=[in_hbm, in_hbm, in_vmem],
        out_specs=[in_hbm] * RING,
        scratch_shapes=[
            pltpu.VMEM((RING,) + shape, bf16),
            pltpu.SemaphoreType.DMA((RING * 2 * CHUNKS,)),
            pltpu.SemaphoreType.DMA((RING,)),
        ],
        compiler_params=pltpu.CompilerParams(vmem_limit_bytes=PACK_LIMIT),
        name="pack_keys",
    )(keys, values, ids)


def pack_queries_kernel(w_ref, q_ref, g_ref, *rest):
    n = RING * CHUNKS
    qg_refs, (qg, sems_in, sems_out) = rest[:n], rest[n:]
    z, _ = my_place()
    order = [c * RING + s for c in range(CHUNKS) for s in (2, 1, 3, 0)]
    inward, outward = Copies(sems_in), Copies(sems_out)
    for n in order:
        first = (lax.rem(z + n % RING, RING) * CHUNKS + n // RING) * QW
        inward.start(columns(q_ref, first, QW), qg.at[n, :, :QW])
        inward.start(columns(g_ref, first, QW), qg.at[n, :, QW:])
    w = jnp.broadcast_to(w_ref[...], (8, TOK)).T[:, 0:1]
    for i, n in enumerate(order):
        inward.started[2 * i].wait()
        inward.started[2 * i + 1].wait()
        qg[n, :, QW:] = (w * qg[n, :, QW:].astype(jnp.float32)).astype(jnp.bfloat16)
        outward.start(qg.at[n], qg_refs[n])
    outward.wait()


def pack_queries(weights, queries, grad_out):
    bf16 = jnp.bfloat16
    n = RING * CHUNKS
    pieces = pl.pallas_call(
        pack_queries_kernel,
        out_shape=[jax.ShapeDtypeStruct((TOK, 2 * QW), bf16)] * n,
        in_specs=[in_vmem, in_hbm, in_hbm],
        out_specs=[in_hbm] * n,
        scratch_shapes=[
            pltpu.VMEM((n, TOK, 2 * QW), bf16),
            pltpu.SemaphoreType.DMA((2 * n,)),
            pltpu.SemaphoreType.DMA((n,)),
        ],
        compiler_params=pltpu.CompilerParams(vmem_limit_bytes=PACK_LIMIT),
        name="pack_queries",
    )(weights, queries, grad_out)
    return [pieces[c * RING : (c + 1) * RING] for c in range(CHUNKS)]


def gather_halo_kernel(*refs):
    kv_refs = in_order(refs[:RING])
    first_ref, second_ref, kv, sems_in, sems_out = refs[RING:]
    inward, outward = Copies(sems_in), Copies(sems_out)
    for s in range(RING):
        inward.start(kv_refs[s], kv.at[s])
    top = IDS + TOK
    for s in range(RING):
        inward.started[s].wait()
        outward.start(kv.at[s, 0:top, :], first_ref.at[s * top : (s + 1) * top, :])
        outward.start(kv.at[s, top:, :], second_ref.at[s * TOK : (s + 1) * TOK, :])
    outward.wait()


def gather_halo(kv):
    bf16 = jnp.bfloat16
    return pl.pallas_call(
        gather_halo_kernel,
        out_shape=[
            jax.ShapeDtypeStruct((RING * (IDS + TOK), 2 * WIDTH), bf16),
            jax.ShapeDtypeStruct((ROW, 2 * WIDTH), bf16),
        ],
        in_specs=[in_hbm] * RING,
        out_specs=[in_hbm] * 2,
        scratch_shapes=[
            pltpu.VMEM((RING, IDS + CHUNKS * TOK, 2 * WIDTH), bf16),
            pltpu.SemaphoreType.DMA((RING,)),
            pltpu.SemaphoreType.DMA((2 * RING,)),
        ],
        compiler_params=pltpu.CompilerParams(vmem_limit_bytes=VMEM_LIMIT),
        name="gather_halo",
    )(*far_first(kv))


def starts_kernel(*rest):
    kv_refs = in_order(rest[:RING])
    halo_ref, starts_ref, ids, sems = rest[RING:]
    copies = Copies(sems)
    for i, ref in enumerate(kv_refs):
        copies.start(ref.at[0:IDS, :], ids.at[i * IDS : (i + 1) * IDS, :])
    for s in range(RING):
        first, i = s * (IDS + TOK), RING + s
        copies.start(halo_ref.at[first : first + IDS, :], ids.at[i * IDS : (i + 1) * IDS, :])
    copies.wait()
    z, row = my_place()
    rows = ids[...].astype(jnp.float32)
    by_key = rows.T
    past = jnp.where(row > 0, by_key[:, RING * IDS :], -1.0)
    before = [by_key[:, s * IDS : s * IDS + 1] for s in range(RING)]
    before += [past[:, s * IDS : s * IDS + 1] for s in range(RING)]
    for s in range(RING):
        own = rows[s * IDS : s * IDS + 1, :]
        found = jnp.zeros((TOK, TOK), jnp.int32)
        for column in before:
            found += jnp.where(column < own, 1, 0)
        source = lax.rem(z + RING - s, RING)
        at = pl.multiple_of(source * TOK, TOK)
        starts_ref[:, pl.ds(at, TOK)] = jnp.sum(found, axis=0, keepdims=True)


def document_starts(kv, halo):
    return pl.pallas_call(
        starts_kernel,
        out_shape=jax.ShapeDtypeStruct((1, ROW), jnp.int32),
        in_specs=[in_hbm] * (RING + 1),
        out_specs=in_vmem,
        scratch_shapes=[
            pltpu.VMEM((2 * RING * IDS, TOK), jnp.bfloat16),
            pltpu.SemaphoreType.DMA((2 * RING,)),
        ],
        compiler_params=pltpu.CompilerParams(vmem_limit_bytes=VMEM_LIMIT),
        name="document_starts",
    )(*far_first(kv), halo)


def attention_kernel(chunk, start_ref, *rest):
    kv_refs, halo_ref = in_order(rest[:RING]), rest[RING]
    qg_refs, rest = in_order(rest[RING + 1 : 2 * RING + 1]), rest[2 * RING + 1 :]
    prior_refs, rest = rest[: len(LATE) * chunk], rest[len(LATE) * chunk :]
    own_refs, back_refs = rest[:RING], rest[RING : 2 * RING]
    kv, qg, dkv, dq, dkv16, prior, sems_kv, sems_qg, sems_prior, sems_out = rest[2 * RING :]
    z, _ = my_place()
    scale = 1.0 / math.sqrt(WIDTH)

    inward_kv, inward_qg, inward_prior = Copies(sems_kv), Copies(sems_qg), Copies(sems_prior)
    sources = [lax.rem(z + RING - s, RING) for s in range(RING)]
    skip = 0 if chunk else IDS
    for s in range(RING):
        halo_rows = pl.ds(pl.multiple_of(sources[s] * TOK, WIDTH), TOK)
        own_rows = pl.ds(pl.multiple_of(ROW + sources[s] * TOK, WIDTH), TOK)
        inward_kv.start(kv_refs[s].at[pl.ds(IDS + chunk * TOK, TOK), :], kv.at[own_rows, :])
        first = s * (skip + TOK) + skip
        inward_kv.start(halo_ref.at[first : first + TOK, :], kv.at[halo_rows, :])
    for s in range(RING):
        rows = pl.ds(pl.multiple_of(sources[s] * TOK, TOK), TOK)
        inward_qg.start(qg_refs[s], qg.at[rows, :])
    for i, ref in enumerate(prior_refs):
        inward_prior.start(ref, prior.at[i])
    dkv[...] = jnp.zeros(dkv.shape, dkv.dtype)
    inward_kv.wait()

    outward = Copies(sems_out)
    dq_copies = []
    for s in range(RING):
        rows = pl.ds(pl.multiple_of(lax.rem(z + s, RING) * TOK, TOK), TOK)
        dq_copies.append(outward.prepare(dq.at[rows, :], own_refs[s].at[:, :QW]))

    def tile(i, carry):
        first = pl.multiple_of(lax.rem(z + i, RING) * QT, QT)
        for s in range(RING):
            pl.when(i == s)(inward_qg.started[(RING - s) % RING].wait)
        starts = start_ref[:, pl.ds(first, QT)]
        end = ROW + first + QT
        count = (end - jnp.min(starts) + KT - 1) // KT

        def work(windows):
            span = windows * KT
            base = pl.multiple_of(end - span, WIDTH)
            keys = pl.ds(base, span)
            rows = qg[pl.ds(first, QT), :]
            heads = [rows[:, h * WIDTH : (h + 1) * WIDTH] for h in range(2 * GROUP)]
            qs = jnp.concatenate(heads[:GROUP], axis=0)
            gs = jnp.concatenate(heads[GROUP:], axis=0)
            q_t, g_t = qs.T, gs.T
            k, v = kv[keys, :WIDTH], kv[keys, WIDTH:]
            k_t, v_t = k.T, v.T
            s = jnp.dot(k, q_t, preferred_element_type=jnp.float32)
            key_at = lax.broadcasted_iota(jnp.int32, (span, QT), 0) + base
            query_at = ROW + first + lax.broadcasted_iota(jnp.int32, (span, QT), 1)
            seen = (key_at >= starts) & (key_at <= query_at)
            s = jnp.where(jnp.concatenate([seen] * GROUP, axis=1), s, NEG)
            e = jnp.exp2((s - jnp.max(s, axis=0, keepdims=True)) * (scale * LOG2E))
            p = e * (1.0 / jnp.sum(e, axis=0, keepdims=True))
            p16 = p.astype(jnp.bfloat16)
            out = jnp.dot(v_t, p16, preferred_element_type=jnp.float32)
            out = out.astype(jnp.bfloat16).astype(jnp.float32)
            delta = jnp.sum(g_t.astype(jnp.float32) * out, axis=0, keepdims=True)
            dp = jnp.dot(v, g_t, preferred_element_type=jnp.float32)
            ds = (p * (dp - delta) * scale).astype(jnp.bfloat16)
            dkv[keys, :WIDTH] += jnp.dot(ds, qs, preferred_element_type=jnp.float32)
            dkv[keys, WIDTH:] += jnp.dot(p16, gs, preferred_element_type=jnp.float32)
            dq_t = jnp.dot(k_t, ds, preferred_element_type=jnp.float32)
            for h in range(GROUP):
                dq[pl.ds(first, QT), h * WIDTH : (h + 1) * WIDTH] = (
                    dq_t[:, h * QT : (h + 1) * QT].T.astype(jnp.bfloat16)
                )

        for fewer, windows in zip((0,) + WINDOWS, WINDOWS):
            pl.when((count > fewer) & (count <= windows))(functools.partial(work, windows))
        for s in range(RING):
            pl.when(i == s)(dq_copies[s].start)
        return carry

    lax.fori_loop(0, TILES, tile, 0)
    for s in range(RING):
        owner = lax.rem(z + s, RING)
        for part in range(2):
            rows = pl.ds(pl.multiple_of(part * ROW + owner * TOK, TOK), TOK)
            dkv16[rows, :] = dkv[rows, :].astype(jnp.bfloat16)
            if part:
                target = own_refs[s].at[:, QW:]
            elif chunk and s in LATE:
                target = back_refs[s].at[:, 2 * WIDTH :]
            else:
                target = back_refs[s]
            outward.start(dkv16.at[rows, :], target)
    inward_prior.wait()
    for i, s in enumerate(LATE[: len(prior_refs)]):
        outward.start(prior.at[i], back_refs[s].at[:, : 2 * WIDTH])
    outward.wait()


def attention(chunk, starts, kv, halo, qg, prior):
    bf16, f32 = jnp.bfloat16, jnp.float32
    wide = [2 if chunk and s in LATE else 1 for s in range(RING)]
    results = pl.pallas_call(
        functools.partial(attention_kernel, chunk),
        out_shape=[jax.ShapeDtypeStruct((TOK, QW + 2 * WIDTH), bf16)] * RING
        + [jax.ShapeDtypeStruct((TOK, 2 * WIDTH * n), bf16) for n in wide],
        in_specs=[in_vmem] + [in_hbm] * (2 * RING + 1 + len(prior)),
        out_specs=[in_hbm] * (2 * RING),
        scratch_shapes=[
            pltpu.VMEM((KEYS, 2 * WIDTH), bf16),
            pltpu.VMEM((ROW, 2 * QW), bf16),
            pltpu.VMEM((KEYS, 2 * WIDTH), f32),
            pltpu.VMEM((ROW, QW), bf16),
            pltpu.VMEM((2 * ROW, 2 * WIDTH), bf16),
            pltpu.VMEM((len(LATE), TOK, 2 * WIDTH), bf16),
            pltpu.SemaphoreType.DMA((2 * RING,)),
            pltpu.SemaphoreType.DMA((RING,)),
            pltpu.SemaphoreType.DMA((len(LATE),)),
            pltpu.SemaphoreType.DMA((3 * RING + len(LATE),)),
        ],
        compiler_params=pltpu.CompilerParams(vmem_limit_bytes=VMEM_LIMIT),
        cost_estimate=pl.CostEstimate(flops=1, bytes_accessed=1, transcendentals=0),
        name="attention",
    )(starts, *far_first(kv), halo, *far_first(qg), *prior)
    return results[:RING], results[RING:]


def join_first_kernel(*rest):
    own_refs = in_order(rest[:RING])
    dq_out, own, sems, sems_out = rest[RING:]
    z, _ = my_place()
    inward, outward = Copies(sems), Copies(sems_out)
    for s in range(RING):
        inward.start(own_refs[s].at[:, :QW], own.at[s])
    for s in range(RING):
        head = lax.rem(z + RING - s, RING) * CHUNKS
        inward.started[s].wait()
        outward.start(own.at[s], columns(dq_out, head * QW, QW))
    outward.wait()


def join_first(own):
    return pl.pallas_call(
        join_first_kernel,
        out_shape=jax.ShapeDtypeStruct((TOK, RING * CHUNKS * QW), jnp.bfloat16),
        in_specs=[in_hbm] * RING,
        out_specs=in_hbm,
        scratch_shapes=[
            pltpu.VMEM((RING, TOK, QW), jnp.bfloat16),
            pltpu.SemaphoreType.DMA((RING,)),
            pltpu.SemaphoreType.DMA((RING,)),
        ],
        compiler_params=pltpu.CompilerParams(vmem_limit_bytes=VMEM_LIMIT),
        name="join_first",
    )(*far_first(own))


def join_kernel(begun_ref, *rest):
    n = RING * CHUNKS
    own_refs, rest = in_order(rest[:RING]) + in_order(rest[RING:n]), rest[n:]
    early_refs, late_refs = rest[: 2 * len(EARLY)], rest[2 * len(EARLY) : 2 * len(EARLY) + len(LATE)]
    dq_out, dk_out, dv_out, own, dq, back, total, sems, sems_dq, sems_back, sems_out = rest[
        2 * len(EARLY) + len(LATE) :
    ]
    z, _ = my_place()
    copies = [Copies(x) for x in (sems, sems_dq, sems_back, sems_out)]
    inward, inward_dq, terms, outward = copies
    pieces = [(c, s) for c in range(CHUNKS) for s in range(RING)]
    for s in range(RING):
        inward_dq.start(own_refs[RING + s].at[:, :QW], dq.at[s])
    for i, (c, s) in enumerate(pieces):
        inward.start(own_refs[i].at[:, QW:], own.at[i])
        if s in EARLY:
            term = early_refs[c * len(EARLY) + EARLY.index(s)]
        else:
            term = late_refs[LATE.index(s)].at[:, 2 * c * WIDTH : 2 * (c + 1) * WIDTH]
        terms.start(term, back.at[i])
    for s in range(RING):
        head = lax.rem(z + RING - s, RING) * CHUNKS + 1
        inward_dq.started[s].wait()
        outward.start(dq.at[s], columns(dq_out, head * QW, QW))
    for i, (c, s) in enumerate(pieces):
        head = lax.rem(z + RING - s, RING) * CHUNKS + c
        inward.started[i].wait()
        terms.started[i].wait()
        sums = own[i].astype(jnp.float32) + back[i].astype(jnp.float32)
        total[i] = sums.astype(total.dtype)
        outward.start(total.at[i, :, :WIDTH], columns(dk_out, head * WIDTH, WIDTH))
        outward.start(total.at[i, :, WIDTH:], columns(dv_out, head * WIDTH, WIDTH))
    outward.wait()


def join(begun, own, early, late):
    heads = RING * CHUNKS
    bf16 = jnp.bfloat16
    return pl.pallas_call(
        join_kernel,
        out_shape=[
            jax.ShapeDtypeStruct((TOK, heads * QW), bf16),
            jax.ShapeDtypeStruct((TOK, heads * WIDTH), bf16),
            jax.ShapeDtypeStruct((TOK, heads * WIDTH), bf16),
        ],
        in_specs=[in_hbm] * (1 + heads + 2 * len(EARLY) + len(LATE)),
        out_specs=[in_hbm] * 3,
        input_output_aliases={0: 0},
        scratch_shapes=[
            pltpu.VMEM((heads, TOK, 2 * WIDTH), bf16),
            pltpu.VMEM((RING, TOK, QW), bf16),
            pltpu.VMEM((heads, TOK, 2 * WIDTH), bf16),
            pltpu.VMEM((heads, TOK, 2 * WIDTH), bf16),
            pltpu.SemaphoreType.DMA((heads,)),
            pltpu.SemaphoreType.DMA((RING,)),
            pltpu.SemaphoreType.DMA((heads,)),
            pltpu.SemaphoreType.DMA((RING + 2 * heads,)),
        ],
        compiler_params=pltpu.CompilerParams(vmem_limit_bytes=VMEM_LIMIT),
        name="join",
    )(begun, *far_first(own[:RING]), *far_first(own[RING:]), *early, *late)


def body(queries, keys, values, grad_out, weights, doc_ids):
    count = lax.axis_size(AXES)

    def send(pieces):
        sent = {s: shift_ring(pieces[s], s, count) for s in (2, 1, 3)}
        return [pieces[0]] + [sent[s] for s in range(1, RING)]

    kv = pack_keys(keys, values, doc_ids[None, :])
    kv = send(kv)
    qg = pack_queries(weights[None, :], queries, grad_out)
    two_hops = shift_ring(qg[0][2], 2, count)
    gathered, (now, next_) = lax.optimization_barrier((gather_halo(kv), qg))
    halo = [shift_row(gathered[0], 1, 0, count)]
    now = [now[0], shift_ring(now[1], 1, count), two_hops, shift_ring(now[3], 3, count)]
    halo.append(shift_row(gathered[1], 1, 0, count))
    now, next_ = lax.optimization_barrier((now, next_))
    qg = [now, send(next_)]
    starts = document_starts(kv, halo[0])

    first_own, first_back = attention(0, starts, kv, halo[0], qg[0], ())
    owns = send(first_own)
    early = [shift_row(first_back[s], -1, s, count) for s in EARLY]
    prior = [first_back[s] for s in LATE]
    own, back = attention(1, starts, kv, halo[1], qg[1], prior)
    own, back, owns, early = lax.optimization_barrier((own, back, owns, early))
    begun = join_first(owns)
    owns += send(own)
    first, last = (1, 3), (0, 2)
    late = {s: shift_row(back[s], -1, s, count) for s in first}
    *rest, owns[RING + 2] = lax.optimization_barrier((*[back[s] for s in last], owns[RING + 2]))
    late.update({s: shift_row(piece, -1, s, count) for piece, s in zip(rest, last)})
    late = [late[s] for s in LATE]
    return tuple(join(begun, owns, early, late))


def solution(mesh):
    rows = P(("dp", "inner", "outer"), None)
    flat = P(("dp", "inner", "outer"))
    return jax.shard_map(
        body,
        mesh=mesh,
        in_specs=(rows, rows, rows, rows, flat, flat),
        out_specs=(rows, rows, rows),
        check_vma=False,
    )
```
